32 devices in a mesh: dp: 8 (over y, x, core), seq: 4 (over z).
Axes of the slice: x: 2, y: 2, z: 4, core: 2. Of those that a mesh axis runs over, the one named last changes fastest.
Arguments:
- tokens: bfloat16 [16, 512, 768], P('dp', 'seq'), may hold values from -6 to 6
- cotangent: bfloat16 [16, 512, 768], P('dp', 'seq'), may hold values from -6 to 6
- lengths: int32 [16], P('dp'), may hold values from 128 to 512, as said below
- repeats: int32 [16], P('dp'), may hold values from 1 to 4
- w_qkv: bfloat16 [2, 768, 2304], replicated, may hold values from -0.21875 to 0.21875
- w_out: bfloat16 [2, 768, 768], replicated, may hold values from -1.25 to 1.25
- w_up: bfloat16 [2, 768, 3072], replicated, may hold values from -0.21875 to 0.21875
- w_down: bfloat16 [2, 3072, 768], replicated, may hold values from -0.109375 to 0.109375
- bias_qv: bfloat16 [2, 2, 768], replicated, may hold values from -4 to 4
- bias_proj: bfloat16 [2, 2, 768], replicated, may hold values from -4 to 4
- bias_up: bfloat16 [2, 3072], replicated, may hold values from -4 to 4
- gains: bfloat16 [2, 2, 768], replicated, may hold values from 0.5 to 1.5
- shifts: bfloat16 [2, 2, 768], replicated, may hold values from -4 to 4
Outputs:
- hidden_out: float32 [16, 512, 768], P('dp', 'seq')
- grad_tokens: float32 [16, 512, 768], P('dp', 'seq')
- grad_qkv: float32 [2, 768, 2304], P(None, 'dp', 'seq')
- grad_out: float32 [2, 768, 768], P(None, 'dp', 'seq')
- grad_up: float32 [2, 768, 3072], P(None, 'dp', 'seq')
- grad_down: float32 [2, 3072, 768], P(None, 'dp', 'seq')
- grad_bias_qv: float32 [2, 2, 768], replicated
- grad_bias_proj: float32 [2, 2, 768], replicated
- grad_bias_up: float32 [2, 3072], replicated
- grad_gains: float32 [2, 2, 768], replicated
- grad_shifts: float32 [2, 2, 768], replicated
The draws below stay inside these ranges and needn't reach their ends.
Inputs may be any that keep to these rules, and one draw needn't show every extreme that they name: `lengths`: among the 2 sequences of each index of dp, one drawn from the seed has length 512.
All inputs are finite; a program needn't handle non-finite values.
Results may differ from the reference program's by a relative error of at most 0.02.
Values may be sent and summed in bfloat16 or wider, within the bound.
No kernel may reach another device: no remote copies, remote signals or barrier semaphores. Data moves between devices by JAX's collectives and lax.ppermute only.
A program may use at most 256 MiB of HBM per device.

```python
import jax
import jax.numpy as jnp
from jax import lax

D = 768
FF = 3072
HEADS = 12
HEAD = 64
L = 512
LAYERS = 2
SEQS = 2
BATCH = 16


def draw_lengths(key, part):
    key = jax.random.fold_in(key, 11)
    first_key, second_key = jax.random.split(key)
    base = jax.random.randint(first_key, (BATCH // SEQS, SEQS), L // 4, L + 1)
    picked = jax.random.randint(second_key, (BATCH // SEQS, 1), 0, SEQS)
    longest = jnp.arange(SEQS)[None, :] == picked
    return jnp.where(longest, L, base).reshape(BATCH).astype(jnp.int32)


def touch_ends(array, stream_key, least, top_value):
    spot = [jax.random.randint(jax.random.fold_in(stream_key, axis), (), 0, length) for axis, length in enumerate(array.shape)]
    widest = array.shape.index(max(array.shape))
    next_to = spot[:widest] + [(spot[widest] + 1) % array.shape[widest]] + spot[widest + 1:]
    return array.at[tuple(spot)].set(least).at[tuple(next_to)].set(top_value)


def levels(rng, extent, cuts, smallest, top_value):
    def one(dim, shards_of):
        heights = jax.random.uniform(jax.random.fold_in(jax.random.fold_in(rng, 6), dim), (shards_of,), jnp.float32, smallest / len(cuts), top_value / len(cuts))
        return jnp.repeat(jnp.exp(heights), extent[dim] // shards_of).reshape((-1,) + (1,) * (len(extent) - dim - 1))

    gain = one(*cuts[0])
    for cut in cuts[1:]:
        gain = gain * one(*cut)
    return gain


def gaussian(own_key, dims, width, reach, shards=(), dtype=jnp.bfloat16):
    gain = levels(own_key, dims, shards, -0.22, 0.18) if shards else 1.0
    array = jax.random.normal(own_key, dims, jnp.float32) * width * gain
    return jnp.minimum(jnp.maximum(array, -reach), reach).astype(dtype)


def setup_inputs(seed: int = 0) -> dict:
    streams_of = jax.random.split(jax.random.key(seed), 14)
    return {
        "tokens": gaussian(streams_of[0], (BATCH, L, D), 1.0, 6.0, ((0, 8), (1, 4))),
        "cotangent": gaussian(streams_of[1], (BATCH, L, D), 1.0, 6.0, ((0, 8), (1, 4))),
        "lengths": draw_lengths(jax.random.fold_in(streams_of[13], 71), 0),
        "repeats": touch_ends(jax.random.randint(streams_of[3], (BATCH,), 1, 5), jax.random.fold_in(streams_of[3], 1), 1, 4).astype(jnp.int32),
        "w_qkv": gaussian(streams_of[4], (LAYERS, D, 3 * D), D ** -0.5, 0.21875),
        "w_out": gaussian(streams_of[5], (LAYERS, D, D), (D // 32) ** -0.5, 1.25),
        "w_up": gaussian(streams_of[6], (LAYERS, D, FF), D ** -0.5, 0.21875),
        "w_down": gaussian(streams_of[7], (LAYERS, FF, D), FF ** -0.5, 0.109375),
        "bias_qv": gaussian(streams_of[8], (LAYERS, 2, D), 0.3, 4.0),
        "bias_proj": gaussian(streams_of[9], (LAYERS, 2, D), 0.3, 4.0),
        "bias_up": gaussian(streams_of[10], (LAYERS, FF), 0.3, 4.0),
        "gains": jnp.clip(1.0 + 0.1 * jax.random.normal(streams_of[11], (LAYERS, 2, D), jnp.float32), 0.5, 1.5).astype(jnp.bfloat16),
        "shifts": gaussian(streams_of[12], (LAYERS, 2, D), 0.3, 4.0),
    }


@jax.custom_vjp
def low(v):
    return lax.optimization_barrier(v.astype(jnp.bfloat16)).astype(jnp.float32)

@jax.custom_vjp
def low_back(v):
    return v

def low_keep(v):
    return (low(v), None)

def low_pass(kept, grad):
    return (grad,)

def back_keep(v):
    return (v, None)

def back_low(kept, grad):
    return (low(grad),)
low.defvjp(low_keep, low_pass)
low_back.defvjp(back_keep, back_low)
highest = lax.Precision.HIGHEST
norm_eps = 1e-05
masked_score = -1000000000.0

def layer_norm(summed, gain_row, shift_row):
    average = lax.optimization_barrier(jnp.mean(summed, -1, keepdims=True))
    centered = summed - average
    variance = lax.optimization_barrier(jnp.mean(centered * centered, -1, keepdims=True))
    return centered * lax.rsqrt(variance + norm_eps) * gain_row + shift_row

def encoder_block(stream, key_valid, w_qkv, w_out, w_up, w_down, bias_qv, bias_proj, bias_up, gains, shifts):
    seq_count = stream.shape[0]
    score_scale = 1.0 / HEAD ** 0.5
    packed = jnp.einsum('nld,de->nle', low(stream), w_qkv, precision=highest)
    bias_all = jnp.concatenate([bias_qv[0], jnp.zeros_like(bias_qv[0]), bias_qv[1]])
    packed = low(low_back(packed + bias_all)).reshape(seq_count, L, 3, HEADS, HEAD)
    queries = packed[:, :, 0]
    key_rows = packed[:, :, 1]
    value_rows = packed[:, :, 2]
    scores = low_back(jnp.einsum('nqhe,nkhe->nhqk', queries, key_rows, precision=highest) * score_scale)
    scores = jnp.where(key_valid[:, None, None, :], scores, masked_score)
    attn_probs = jax.nn.softmax(scores, axis=-1)
    attended = jnp.einsum('nhqk,nkhe->nqhe', low(attn_probs), value_rows, precision=highest)
    attended = low(low_back(attended)).reshape(seq_count, L, D)
    branch = low_back(jnp.einsum('nld,de->nle', attended, w_out, precision=highest) + bias_proj[0])
    normed = layer_norm(stream + branch, gains[0], shifts[0])
    before = low_back(jnp.einsum('nld,df->nlf', low(normed), w_up, precision=highest) + bias_up)
    active = low(jax.nn.gelu(before, approximate=False))
    mixed_out = low_back(jnp.einsum('nlf,fd->nld', active, w_down, precision=highest) + bias_proj[1])
    return layer_norm(normed + mixed_out, gains[1], shifts[1])

def add_pair(summed, fresh_grad):
    return summed + fresh_grad

def reference(tokens, cotangent, lengths, repeats, w_qkv, w_out, w_up, w_down, bias_qv, bias_proj, bias_up, gains, shifts):
    params = tuple((member.astype(jnp.float32) for member in (w_qkv, w_out, w_up, w_down, bias_qv, bias_proj, bias_up, gains, shifts)))
    groups = BATCH // SEQS
    positions = jnp.arange(L)
    stream_all = tokens.astype(jnp.float32).reshape(groups, SEQS, L, D)
    upstream_all = cotangent.astype(jnp.float32).reshape(groups, SEQS, L, D)
    len_all = lengths.reshape(groups, SEQS)
    rep_all = repeats.reshape(groups, SEQS)

    def one_group(totals, inputs):
        stream, upstream, group_len, group_rep = inputs
        key_valid = positions[None, :] < group_len[:, None]

        def forward(stream_in, weights):
            hidden = stream_in
            for layer_index in range(LAYERS):
                hidden = encoder_block(hidden, key_valid, *[member[layer_index] for member in weights])
            return hidden
        output, pullback = jax.vjp(forward, stream, params)
        row_scale = group_rep.astype(jnp.float32)[:, None, None] * key_valid.astype(jnp.float32)[:, :, None]
        grad_stream, grad_params = pullback(upstream * row_scale)
        return (jax.tree.map(add_pair, totals, grad_params), (output, grad_stream))
    zeros_init = jax.tree.map(jnp.zeros_like, params)
    totals, results = lax.scan(one_group, zeros_init, (stream_all, upstream_all, len_all, rep_all))
    outputs, grad_streams = results
    return (outputs.reshape(BATCH, L, D), grad_streams.reshape(BATCH, L, D), totals[0], totals[1], totals[2], totals[3], totals[4], totals[5], totals[6], totals[7], totals[8])
```

```python
import jax
import jax.numpy as jnp
from jax import lax
from jax.sharding import PartitionSpec as P

D = 768
FF = 3072
HEADS = 12
HEAD = 64
LAYERS = 2
EPS = 1e-05
MASKED = -1000000000.0
SCALE = 1.0 / HEAD**0.5
F32 = jnp.float32
BF16 = jnp.bfloat16


class Place:
    def __init__(self):
        self.dp_width = lax.axis_size("dp")
        self.seq_width = lax.axis_size("seq")
        self.dp = lax.axis_index("dp")
        self.z = lax.axis_index("seq")
        self.core = self.dp % 2
        self.dp_bits = self.dp_width.bit_length() - 2
        self.seq_bits = self.seq_width.bit_length() - 1

    def swap_dp(self, value, bit):
        pairs = [(i, i ^ (1 << bit)) for i in range(self.dp_width)]
        return lax.ppermute(value, "dp", pairs)

    def swap_core(self, value):
        return self.swap_dp(value, 0)

    def swap_seq(self, value, bit):
        pairs = [(i, i ^ (1 << bit)) for i in range(self.seq_width)]
        return lax.ppermute(value, "seq", pairs)

    def spread_pairs(self, flip, back):
        pairs = []
        for dp in range(self.dp_width):
            chip, core = dp // 2, dp % 2
            for z in range(self.seq_width):
                s = (z % 2) ^ flip
                src = dp * self.seq_width + z
                dst = (2 * chip + z // 2) * self.seq_width + 2 * core + s
                pairs.append((dst, src) if back else (src, dst))
        return pairs

    def to_chip(self, value):
        low = self.z % 2
        first = lax.dynamic_index_in_dim(value, low, 0, keepdims=False)
        second = lax.dynamic_index_in_dim(value, 1 - low, 0, keepdims=False)
        got0 = lax.ppermute(first, ("dp", "seq"), self.spread_pairs(0, False))
        got1 = lax.ppermute(second, ("dp", "seq"), self.spread_pairs(1, False))
        even = low == 0
        return jnp.concatenate([jnp.where(even, got0, got1), jnp.where(even, got1, got0)], 0)

    def from_chip(self, value):
        low = self.z % 2
        blocks = value.reshape(2, value.shape[0] // 2, value.shape[1])
        first = lax.dynamic_index_in_dim(blocks, low, 0, keepdims=False)
        second = lax.dynamic_index_in_dim(blocks, 1 - low, 0, keepdims=False)
        got0 = lax.ppermute(first, ("dp", "seq"), self.spread_pairs(0, True))
        got1 = lax.ppermute(second, ("dp", "seq"), self.spread_pairs(1, True))
        even = low == 0
        return jnp.stack([jnp.where(even, got0, got1), jnp.where(even, got1, got0)], 0)

    def all_sum(self, value):
        value = value + self.swap_core(value)
        for bit in range(1, self.dp_bits + 1):
            value = value + self.swap_dp(value, bit)
        for bit in range(self.seq_bits):
            value = value + self.swap_seq(value, bit)
        return value

    def halve(self, blocks, axis, mine, swap):
        keep = lax.dynamic_index_in_dim(blocks, mine, axis, keepdims=False)
        send = lax.dynamic_index_in_dim(blocks, 1 - mine, axis, keepdims=False)
        got = swap(send)
        return (keep.astype(F32) + got.astype(F32)).astype(BF16)

    def scatter_sum(self, grad, low_first):
        chips = self.dp_width // 2
        rows = grad.shape[0] // chips
        cols = grad.shape[1]
        blocks = grad.reshape((2,) * self.dp_bits + (rows, cols))
        order = list(range(self.dp_bits))
        if low_first:
            order = order[::-1]
        left = list(range(self.dp_bits))
        for member in order:
            axis = left.index(member)
            bit = self.dp_bits - member
            mine = (self.dp >> bit) % 2
            blocks = self.halve(blocks, axis, mine, lambda v, bit=bit: self.swap_dp(v, bit))
            left.remove(member)
        blocks = blocks.reshape(rows, self.seq_width, cols // self.seq_width).transpose(1, 0, 2)
        blocks = blocks.reshape((2,) * self.seq_bits + (rows, cols // self.seq_width))
        for bit in range(self.seq_bits):
            axis = self.seq_bits - 1 - bit
            mine = (self.z >> bit) % 2
            blocks = self.halve(blocks, axis, mine, lambda v, bit=bit: self.swap_seq(v, bit))
        return blocks.astype(F32)

    def core_half(self, lhs, which):
        width = lhs.shape[1] // self.dp_width
        grouped = lhs.reshape(lhs.shape[0], self.dp_width // 2, 2, width)
        return lax.dynamic_index_in_dim(grouped, which, 2, keepdims=False).reshape(lhs.shape[0], -1)

    def weight_grad(self, lhs, rhs):
        own = self.core_half(lhs, self.core)
        other = self.swap_core(self.core_half(lhs, 1 - self.core))
        rhs_other = self.swap_core(rhs)
        return (inner_rows(own, rhs) + inner_rows(other, rhs_other)).astype(BF16)


def inner_rows(left, right):
    return lax.dot_general(left, right, (((0,), (0,)), ((), ())), preferred_element_type=F32)


def times_back(left, right):
    return lax.dot_general(left, right, (((1,), (1,)), ((), ())), preferred_element_type=F32)


def times(left, right):
    return jnp.dot(left, right, preferred_element_type=F32)


def norm_parts(summed):
    average = jnp.mean(summed, -1, keepdims=True)
    centered = summed - average
    variance = jnp.mean(centered * centered, -1, keepdims=True)
    inverse = lax.rsqrt(variance + EPS)
    return centered * inverse, inverse


def norm_back(grad, hat, inverse, gain_row):
    scaled = grad * gain_row
    mean_one = jnp.mean(scaled, -1, keepdims=True)
    mean_hat = jnp.mean(scaled * hat, -1, keepdims=True)
    out = (scaled - mean_one - hat * mean_hat) * inverse
    return out, jnp.sum(grad * hat, 0), jnp.sum(grad, 0)


def heads(value):
    return value.reshape(value.shape[0], HEADS, HEAD)


def forward_layer(place, stream, key_valid, layer, weights):
    w_qkv, w_out, w_up, w_down, bias_qv, bias_proj, bias_up, gains, shifts = weights
    low = stream.astype(BF16)
    bias_pair = bias_qv[layer].astype(F32)
    w = w_qkv[layer]
    keys = times(low, w[:, D : 2 * D]).astype(BF16)
    values = (times(low, w[:, 2 * D :]) + bias_pair[1]).astype(BF16)
    own = jnp.concatenate([keys, values], 1)
    other = place.swap_core(own)
    queries = (times(low, w[:, :D]) + bias_pair[0]).astype(BF16)
    both = jnp.concatenate([own, other], 0)
    keys, values = both[:, :D], both[:, D:]
    scores = jnp.einsum("qhe,khe->hqk", heads(queries), heads(keys), preferred_element_type=F32) * SCALE
    scores = jnp.where(key_valid[None, None, :], scores, MASKED)
    top = jnp.max(scores, -1, keepdims=True)
    total = top + jnp.log(jnp.sum(jnp.exp(scores - top), -1, keepdims=True))
    probs = jnp.exp(scores - total).astype(BF16)
    attended = jnp.einsum("hqk,khe->qhe", probs, heads(values), preferred_element_type=F32)
    attended = attended.astype(BF16).reshape(-1, D)
    proj = bias_proj[layer].astype(F32)
    gain = gains[layer].astype(F32)
    shift = shifts[layer].astype(F32)
    hat1, inv1 = norm_parts(stream + (times(attended, w_out[layer]) + proj[0]))
    normed = hat1 * gain[0] + shift[0]
    normed_low = normed.astype(BF16)
    before = times(normed_low, w_up[layer]) + bias_up[layer].astype(F32)
    cdf = 0.5 * (1.0 + lax.erf(before * (0.5**0.5)))
    active = (before * cdf).astype(BF16)
    slope = cdf + before * (jnp.exp(-0.5 * before * before) * 0.3989422804014327)
    hat2, inv2 = norm_parts(normed + (times(active, w_down[layer]) + proj[1]))
    out = hat2 * gain[1] + shift[1]
    return out, (low, queries, keys, values, total, attended, hat1, inv1, normed_low, slope, active, hat2, inv2)


def backward_layer(place, grad, kept, key_valid, layer, weights):
    w_qkv, w_out, w_up, w_down, bias_qv, bias_proj, bias_up, gains, shifts = weights
    low, queries, keys, values, total, attended, hat1, inv1, normed_low, slope, active, hat2, inv2 = kept
    gain = gains[layer].astype(F32)
    grad_two, gain_two, shift_two = norm_back(grad, hat2, inv2, gain[1])
    mixed = grad_two.astype(BF16)
    bias_down_grad = jnp.sum(mixed.astype(F32), 0)
    grad_down = place.scatter_sum(place.weight_grad(active, mixed), True)
    grad_before = (times_back(mixed, w_down[layer]) * slope).astype(BF16)
    bias_up_grad = jnp.sum(grad_before.astype(F32), 0)
    grad_up = place.scatter_sum(place.weight_grad(normed_low, grad_before), False)
    grad_normed = grad_two + times_back(grad_before, w_up[layer])
    grad_one, gain_one, shift_one = norm_back(grad_normed, hat1, inv1, gain[0])
    branch = grad_one.astype(BF16)
    bias_out_grad = jnp.sum(branch.astype(F32), 0)
    grad_out = place.scatter_sum(place.weight_grad(attended, branch), True)
    grad_att = times_back(branch, w_out[layer]).astype(BF16)
    scores = jnp.einsum("qhe,khe->hqk", heads(queries), heads(keys), preferred_element_type=F32) * SCALE
    scores = jnp.where(key_valid[None, None, :], scores, MASKED)
    probs = jnp.exp(scores - total)
    grad_probs = jnp.einsum("qhe,khe->hqk", heads(grad_att), heads(values), preferred_element_type=F32)
    delta = jnp.sum(probs * grad_probs, -1, keepdims=True)
    grad_scores = (probs * (grad_probs - delta)).astype(BF16)
    probs_low = probs.astype(BF16)
    grad_q = jnp.einsum("hqk,khe->qhe", grad_scores, heads(keys), preferred_element_type=F32) * SCALE
    grad_k = jnp.einsum("hqk,qhe->khe", grad_scores, heads(queries), preferred_element_type=F32) * SCALE
    grad_v = jnp.einsum("hqk,qhe->khe", probs_low, heads(grad_att), preferred_element_type=F32)
    rows = queries.shape[0]
    grad_kv = jnp.concatenate([grad_k.reshape(-1, D), grad_v.reshape(-1, D)], 1)
    received = place.swap_core(grad_kv[rows:].astype(BF16))
    grad_kv = grad_kv[:rows] + received.astype(F32)
    packed = jnp.concatenate([grad_q.reshape(-1, D), grad_kv], 1).astype(BF16)
    bias_sums = jnp.sum(packed.astype(F32), 0)
    grad_qkv = place.scatter_sum(place.weight_grad(low, packed), False)
    grad_input = grad_one + times_back(packed, w_qkv[layer])
    small = jnp.concatenate(
        [
            bias_sums[:D],
            bias_sums[2 * D :],
            bias_out_grad,
            bias_down_grad,
            gain_one,
            gain_two,
            shift_one,
            shift_two,
            bias_up_grad,
        ]
    )
    return grad_input, (grad_qkv, grad_out, grad_up, grad_down), small


def local(
    tokens, cotangent, lengths, repeats, w_qkv, w_out, w_up, w_down, bias_qv, bias_proj, bias_up, gains, shifts
):
    weights = (w_qkv, w_out, w_up, w_down, bias_qv, bias_proj, bias_up, gains, shifts)
    place = Place()
    counts = jnp.stack([lengths, repeats])
    other_counts = place.swap_core(counts)
    counts = jnp.where(place.core == place.z // 2, counts, other_counts)
    counts = lax.dynamic_index_in_dim(counts, place.z % 2, 1, keepdims=False)
    length, repeat = counts[0], counts[1]
    tokens_here = place.to_chip(tokens)
    cot_here = place.to_chip(cotangent)
    rows = tokens_here.shape[0]
    own_pos = place.core * rows + jnp.arange(rows)
    other_pos = (1 - place.core) * rows + jnp.arange(rows)
    key_valid = jnp.concatenate([own_pos, other_pos]) < length
    stream = tokens_here.astype(F32)
    kept = []
    for layer in range(LAYERS):
        stream, values = forward_layer(place, stream, key_valid, layer, weights)
        kept.append(values)
    hidden = place.from_chip(stream.astype(BF16)).astype(F32)
    row_scale = jnp.where(own_pos < length, repeat, 0).astype(F32)
    grad = cot_here.astype(F32) * row_scale[:, None]
    big = [None] * LAYERS
    small = [None] * LAYERS
    for layer in reversed(range(LAYERS)):
        grad, big[layer], small[layer] = backward_layer(place, grad, kept[layer], key_valid, layer, weights)
    grad_tokens = place.from_chip(grad.astype(BF16)).astype(F32)
    total = place.all_sum(jnp.stack(small))
    table = total[:, : 8 * D].reshape(LAYERS, 8, D)
    stacked = [jnp.stack([big[layer][k] for layer in range(LAYERS)]) for k in range(4)]
    return (
        hidden,
        grad_tokens,
        *stacked,
        table[:, 0:2],
        table[:, 2:4],
        total[:, 8 * D :],
        table[:, 4:6],
        table[:, 6:8],
    )


def solution(mesh):
    rows = P("dp", "seq", None)
    blocks = P(None, "dp", "seq")
    return jax.shard_map(
        local,
        mesh=mesh,
        in_specs=(rows, rows, P("dp"), P("dp")) + (P(),) * 9,
        out_specs=(rows, rows) + (blocks,) * 4 + (P(),) * 5,
        check_vma=False,
    )
```

```python
import functools

import jax
import jax.numpy as jnp
from jax import lax
from jax.experimental import pallas as pl
from jax.experimental.pallas import tpu as pltpu
from jax.sharding import PartitionSpec as P

D = 768
FF = 3072
HEADS = 12
HEAD = 64
PAIR = 2 * HEAD
LAYERS = 2
EPS = 1e-05
MASKED = -1000000000.0
SCALE = 1.0 / HEAD**0.5
F32 = jnp.float32
BF16 = jnp.bfloat16
FF_STEP = 512
ERFCX_POINT = 0.48
ERFCX = (
    0.270751081,
    0.27211497,
    0.227394229,
    0.241744859,
    -0.115868816,
    0.444806334,
    -0.579913037,
    0.294191549,
    -0.05522118,
)


class Place:
    def __init__(self):
        self.dp_width = lax.axis_size("dp")
        self.seq_width = lax.axis_size("seq")
        self.dp = lax.axis_index("dp")
        self.z = lax.axis_index("seq")
        self.core = self.dp % 2
        self.dp_bits = self.dp_width.bit_length() - 2
        self.seq_bits = self.seq_width.bit_length() - 1

    def swap_dp(self, value, bit):
        pairs = [(i, i ^ (1 << bit)) for i in range(self.dp_width)]
        return lax.ppermute(value, "dp", pairs)

    def swap_core(self, value):
        return self.swap_dp(value, 0)

    def swap_seq(self, value, bit):
        pairs = [(i, i ^ (1 << bit)) for i in range(self.seq_width)]
        return lax.ppermute(value, "seq", pairs)

    def spread_pairs(self, flip, back):
        pairs = []
        for dp in range(self.dp_width):
            chip, core = dp // 2, dp % 2
            for z in range(self.seq_width):
                s = (z % 2) ^ flip
                src = dp * self.seq_width + z
                dst = (2 * chip + z // 2) * self.seq_width + 2 * core + s
                pairs.append((dst, src) if back else (src, dst))
        return pairs

    def to_chip(self, value):
        low = self.z % 2
        first = lax.dynamic_index_in_dim(value, low, 0, keepdims=False)
        second = lax.dynamic_index_in_dim(value, 1 - low, 0, keepdims=False)
        got0 = lax.ppermute(first, ("dp", "seq"), self.spread_pairs(0, False))
        got1 = lax.ppermute(second, ("dp", "seq"), self.spread_pairs(1, False))
        return got0, got1

    def from_chip(self, value):
        low = self.z % 2
        blocks = value.reshape(2, value.shape[0] // 2, value.shape[1])
        first = lax.dynamic_index_in_dim(blocks, low, 0, keepdims=False)
        second = lax.dynamic_index_in_dim(blocks, 1 - low, 0, keepdims=False)
        got0 = lax.ppermute(first, ("dp", "seq"), self.spread_pairs(0, True))
        got1 = lax.ppermute(second, ("dp", "seq"), self.spread_pairs(1, True))
        even = low == 0
        return jnp.stack([jnp.where(even, got0, got1), jnp.where(even, got1, got0)], 0)

    def all_sum(self, value):
        value = value + self.swap_core(value)
        for bit in range(1, self.dp_bits + 1):
            value = value + self.swap_dp(value, bit)
        for bit in range(self.seq_bits):
            value = value + self.swap_seq(value, bit)
        return value

    def halve(self, blocks, axis, mine, swap):
        keep = lax.dynamic_index_in_dim(blocks, mine, axis, keepdims=False)
        send = lax.dynamic_index_in_dim(blocks, 1 - mine, axis, keepdims=False)
        got = swap(send)
        return (keep.astype(F32) + got.astype(F32)).astype(BF16)

    def scatter_sum(self, send, keep, first_bit):
        rows = send.shape[0] // (self.dp_width // 4)
        cols = send.shape[1]
        got = self.swap_dp(send, first_bit)
        blocks = (keep.astype(F32) + got.astype(F32)).astype(BF16)
        left = [bit for bit in range(self.dp_bits, 0, -1) if bit != first_bit]
        blocks = blocks.reshape((2,) * len(left) + (rows, cols))
        for bit in list(left):
            mine = (self.dp >> bit) % 2
            blocks = self.halve(blocks, left.index(bit), mine, lambda v, bit=bit: self.swap_dp(v, bit))
            left.remove(bit)
        blocks = blocks.reshape(rows, self.seq_width, cols // self.seq_width).transpose(1, 0, 2)
        blocks = blocks.reshape((2,) * self.seq_bits + (rows, cols // self.seq_width))
        for bit in range(self.seq_bits):
            axis = self.seq_bits - 1 - bit
            mine = (self.z >> bit) % 2
            blocks = self.halve(blocks, axis, mine, lambda v, bit=bit: self.swap_seq(v, bit))
        return blocks.astype(F32)


def call(body, operands, outputs, scratch, flops, exps=0, vmem=48):
    spaces = {"v": pltpu.VMEM, "a": pl.ANY, "s": pltpu.SMEM}
    moved = sum(a.size * a.dtype.itemsize for a, p in operands if p == "v")
    moved += sum(functools.reduce(lambda x, y: x * y, s) * jnp.dtype(d).itemsize for s, d in outputs)
    return pl.pallas_call(
        body,
        out_shape=[jax.ShapeDtypeStruct(s, d) for s, d in outputs],
        in_specs=[pl.BlockSpec(memory_space=spaces[p]) for _, p in operands],
        out_specs=[pl.BlockSpec(memory_space=pltpu.VMEM) for _ in outputs],
        scratch_shapes=scratch,
        compiler_params=pltpu.CompilerParams(vmem_limit_bytes=vmem << 20),
        cost_estimate=pl.CostEstimate(flops=flops, bytes_accessed=moved, transcendentals=exps),
    )(*[a for a, _ in operands])


def dot(left, right):
    return jnp.dot(left, right, preferred_element_type=F32)


def dot_back(left, right):
    return lax.dot_general(left, right, (((1,), (1,)), ((), ())), preferred_element_type=F32)


def norm_parts(summed):
    average = jnp.mean(summed, -1, keepdims=True)
    centered = summed - average
    variance = jnp.mean(centered * centered, -1, keepdims=True)
    inverse = lax.rsqrt(variance + EPS)
    return centered * inverse, inverse


def norm_back(grad, hat, inverse, gain_row):
    scaled = grad * gain_row
    mean_one = jnp.mean(scaled, -1, keepdims=True)
    mean_hat = jnp.mean(scaled * hat, -1, keepdims=True)
    out = (scaled - mean_one - hat * mean_hat) * inverse
    return out, jnp.sum(grad * hat, 0, keepdims=True), jnp.sum(grad, 0, keepdims=True)


def gelu_parts(before):
    size = jnp.abs(before) * (0.5**0.5)
    spread = jnp.exp(-0.5 * before * before)
    t = 1.0 / (1.0 + ERFCX_POINT * size)
    poly = jnp.full_like(t, ERFCX[-1])
    for factor in ERFCX[-2::-1]:
        poly = poly * t + factor
    tail = 0.5 * (poly * t) * spread
    cdf = jnp.where(before >= 0.0, 1.0 - tail, tail)
    return before * cdf, cdf + before * (spread * 0.3989422804014327)


def load(pairs, sems):
    copies = [pltpu.make_async_copy(src, dst, sems.at[k]) for k, (src, dst) in enumerate(pairs)]
    for copy in copies:
        copy.start()
    return copies


def row(ref, *index):
    return ref[index[:-1] + (pl.ds(index[-1], 1), slice(None))].astype(F32)


def key_masks(scal, rows):
    spot = lax.broadcasted_iota(jnp.int32, (rows, rows), 0)
    own = spot + scal[0] * rows < scal[1]
    other = spot + (1 - scal[0]) * rows < scal[1]
    return own, other


def head_lanes(value, h, axis):
    spot = lax.broadcasted_iota(jnp.int32, value.shape, axis) // HEAD
    return jnp.where(spot == h, value, jnp.zeros_like(value))


def first_kernel(scal, got0, got1, w, bias, low, kv, wkv, sems):
    (copy,) = load([(w.at[0, :, pl.ds(D, 2 * D)], wkv)], sems)
    rows = got0.shape[0]
    even = scal[3] == 0

    @pl.when(even)
    def _():
        low[0:rows] = got0[...]
        low[rows : 2 * rows] = got1[...]

    @pl.when(jnp.logical_not(even))
    def _():
        low[0:rows] = got1[...]
        low[rows : 2 * rows] = got0[...]

    copy.wait()
    kv[:, :D] = dot(low[...], wkv[:, :D]).astype(BF16)
    kv[:, D:] = (dot(low[...], wkv[:, D:]) + row(bias, 0, 1)).astype(BF16)


def query_kernel(layer, low, w, bias, q, wq, sems):
    (copy,) = load([(w.at[layer, :, pl.ds(0, D)], wq)], sems)
    copy.wait()
    full = (dot(low[...], wq[...]) + row(bias, layer, 0)).astype(BF16)
    q[...] = full * jnp.asarray(SCALE, BF16)


def layer_kernel(layer, last, *refs):
    (scal, x, q, kv_own, kv_other, w_out, w_up, w_down, w_qkv) = refs[:9]
    (bias_qv, bias_proj, bias_up, gains, shifts) = refs[9:14]
    refs = refs[14:]
    if last:
        cot0, cot1 = refs[:2]
        refs = refs[2:]
    (att, lse, hat1, inv1, normed_low, active, slope) = refs[:7]
    refs = refs[7:]
    if last:
        out, mixed, grad_two, small = refs[:4]
        refs = refs[4:]
    else:
        hat2, inv2, out, low, kv_next = refs[:5]
        refs = refs[5:]
    (wo, wu, wd, wkv, qt, vt, ot, acc, sems) = refs
    rows = q.shape[0]
    moves = [(w_out.at[layer], wo), (w_up.at[layer], wu), (w_down.at[layer], wd)]
    if not last:
        moves.append((w_qkv.at[layer + 1, :, pl.ds(D, 2 * D)], wkv))
    copies = load(moves, sems)
    qt[...] = q[...].T
    vt[:, 0:rows] = kv_own[:, D:].T
    vt[:, rows : 2 * rows] = kv_other[:, D:].T
    valid_own, valid_other = key_masks(scal, rows)

    def pair(k, carry):
        lanes = pl.ds(pl.multiple_of(k * PAIR, PAIR), PAIR)
        keys_own, keys_other = kv_own[:, lanes], kv_other[:, lanes]
        q_pair = qt[lanes, :]
        for h in range(2):
            q_head = head_lanes(q_pair, h, 0)
            s_own = jnp.where(valid_own, dot(keys_own, q_head), MASKED)
            s_other = jnp.where(valid_other, dot(keys_other, q_head), MASKED)
            top = jnp.maximum(jnp.max(s_own, 0, keepdims=True), jnp.max(s_other, 0, keepdims=True))
            p_own = jnp.exp(s_own - top)
            p_other = jnp.exp(s_other - top)
            total = jnp.sum(p_own, 0, keepdims=True) + jnp.sum(p_other, 0, keepdims=True)
            head = pl.ds(pl.multiple_of(k * PAIR + h * HEAD, HEAD), HEAD)
            o = dot(vt[head, 0:rows], p_own.astype(BF16)) + dot(vt[head, rows : 2 * rows], p_other.astype(BF16))
            ot[head, :] = (o * (1.0 / total)).astype(BF16)
            lse[pl.ds(2 * k + h, 1), :] = top + jnp.log(total)
        return carry

    lax.fori_loop(0, HEADS // 2, pair, 0)
    att[...] = ot[...].T
    copies[0].wait()
    h1, i1 = norm_parts(x[...].astype(F32) + (dot(att[...], wo[...]) + row(bias_proj, layer, 0)))
    hat1[...] = h1
    inv1[...] = jnp.broadcast_to(i1, inv1.shape)
    normed = h1 * row(gains, layer, 0) + row(shifts, layer, 0)
    normed_low[...] = normed.astype(BF16)
    acc[...] = normed + row(bias_proj, layer, 1)
    copies[1].wait()
    copies[2].wait()

    def step(k, carry):
        cols = pl.ds(pl.multiple_of(k * FF_STEP, FF_STEP), FF_STEP)
        before = dot(normed_low[...], wu[:, cols]) + bias_up[pl.ds(layer, 1), cols].astype(F32)
        value, steep = gelu_parts(before)
        value = value.astype(BF16)
        active[:, cols] = value
        slope[:, cols] = steep.astype(BF16)
        acc[...] += dot(value, wd[cols, :])
        return carry

    lax.fori_loop(0, FF // FF_STEP, step, 0)
    h2, i2 = norm_parts(acc[...])
    stream = h2 * row(gains, layer, 1) + row(shifts, layer, 1)
    if not last:
        hat2[...] = h2
        inv2[...] = jnp.broadcast_to(i2, inv2.shape)
        out[...] = stream
        low[...] = stream.astype(BF16)
        copies[3].wait()
        kv_next[:, :D] = dot(low[...], wkv[:, :D]).astype(BF16)
        kv_next[:, D:] = (dot(low[...], wkv[:, D:]) + row(bias_qv, layer + 1, 1)).astype(BF16)
        return
    out[...] = stream.astype(BF16)
    even = scal[3] == 0
    half = rows // 2

    @pl.when(even)
    def _():
        acc[0:half] = cot0[...].astype(F32)
        acc[half:rows] = cot1[...].astype(F32)

    @pl.when(jnp.logical_not(even))
    def _():
        acc[0:half] = cot1[...].astype(F32)
        acc[half:rows] = cot0[...].astype(F32)

    spot = lax.broadcasted_iota(jnp.int32, (rows, 1), 0) + scal[0] * rows
    scale = jnp.where(spot < scal[1], scal[2], 0).astype(F32)
    second_back(layer, acc[...] * scale, h2, i2, gains, mixed, grad_two, small)


def second_back(layer, grad, hat, inverse, gains, mixed, grad_two, small):
    two, gain_two, shift_two = norm_back(grad, hat, inverse, row(gains, layer, 1))
    grad_two[...] = two
    mixed[...] = two.astype(BF16)
    small[0:1] = jnp.sum(mixed[...].astype(F32), 0, keepdims=True)
    small[1:2] = gain_two
    small[2:3] = shift_two


def up_back_kernel(layer, mixed, slope, w_down, grad_before, bias_up_grad, wd, sems):
    steps = FF // FF_STEP
    copies = load([(w_down.at[layer, pl.ds(k * FF_STEP, FF_STEP)], wd.at[k]) for k in range(steps)], sems)
    for k in range(steps):
        copies[k].wait()
        cols = slice(k * FF_STEP, (k + 1) * FF_STEP)
        value = (dot_back(mixed[...], wd[k]) * slope[:, cols].astype(F32)).astype(BF16)
        grad_before[:, cols] = value
        bias_up_grad[:, cols] = jnp.sum(value.astype(F32), 0, keepdims=True)


def attention_back_kernel(layer, *refs):
    (scal, grad_before, grad_two, hat1, inv1, q, kv_own, kv_other, lse, w_up, w_out, gains) = refs[:12]
    (grad_one, branch, grad_q, dkv_own, dkv_other, small) = refs[12:18]
    (wu, wo, datt, qt, dot_t, kt, dqt, sems) = refs[18:]
    rows = q.shape[0]
    copies = load([(w_up.at[layer], wu), (w_out.at[layer], wo)], sems)
    qt[...] = q[...].T
    kt[:, 0:rows] = kv_own[:, :D].T
    kt[:, rows : 2 * rows] = kv_other[:, :D].T
    copies[0].wait()
    grad_normed = grad_two[...] + dot_back(grad_before[...], wu[...])
    one, gain_one, shift_one = norm_back(grad_normed, hat1[...], inv1[:, 0:1], row(gains, layer, 0))
    grad_one[...] = one
    branch[...] = one.astype(BF16)
    small[0:1] = jnp.sum(branch[...].astype(F32), 0, keepdims=True)
    small[1:2] = gain_one
    small[2:3] = shift_one
    copies[1].wait()
    datt[...] = dot_back(branch[...], wo[...]).astype(BF16)
    dot_t[...] = datt[...].T
    valid_own, valid_other = key_masks(scal, rows)

    def pair(k, carry):
        lanes = pl.ds(pl.multiple_of(k * PAIR, PAIR), PAIR)
        v_lanes = pl.ds(pl.multiple_of(D + k * PAIR, PAIR), PAIR)
        keys_own, keys_other = kv_own[:, lanes], kv_other[:, lanes]
        vals_own, vals_other = kv_own[:, v_lanes], kv_other[:, v_lanes]
        sums = None
        for h in range(2):
            qt_head = head_lanes(qt[lanes, :], h, 0)
            dt_head = head_lanes(dot_t[lanes, :], h, 0)
            q_head = head_lanes(q[:, lanes], h, 1)
            d_head = head_lanes(datt[:, lanes], h, 1)
            log_total = lse[pl.ds(2 * k + h, 1), :]
            p_own = jnp.exp(jnp.where(valid_own, dot(keys_own, qt_head), MASKED) - log_total)
            p_other = jnp.exp(jnp.where(valid_other, dot(keys_other, qt_head), MASKED) - log_total)
            dw_own = dot(vals_own, dt_head)
            dw_other = dot(vals_other, dt_head)
            delta = jnp.sum(p_own * dw_own, 0, keepdims=True) + jnp.sum(p_other * dw_other, 0, keepdims=True)
            ds_own = (p_own * (dw_own - delta)).astype(BF16)
            ds_other = (p_other * (dw_other - delta)).astype(BF16)
            head = pl.ds(pl.multiple_of(k * PAIR + h * HEAD, HEAD), HEAD)
            dq = dot(kt[head, 0:rows], ds_own) + dot(kt[head, rows : 2 * rows], ds_other)
            dqt[head, :] = (dq * SCALE).astype(BF16)
            parts = (
                dot(ds_own, q_head),
                dot(ds_other, q_head),
                dot(p_own.astype(BF16), d_head),
                dot(p_other.astype(BF16), d_head),
            )
            sums = parts if sums is None else tuple(a + b for a, b in zip(sums, parts))
        dkv_own[:, lanes] = sums[0]
        dkv_other[:, lanes] = sums[1].astype(BF16)
        dkv_own[:, v_lanes] = sums[2]
        dkv_other[:, v_lanes] = sums[3].astype(BF16)
        return carry

    lax.fori_loop(0, HEADS // 2, pair, 0)
    grad_q[...] = dqt[...].T


def input_back_kernel(layer, *refs):
    (grad_q, dkv_own, dkv_got, grad_one, w_qkv) = refs[:5]
    refs = refs[5:]
    if layer > 0:
        hat2, inv2, gains = refs[:3]
        packed, small_in, mixed, grad_two, small, w, sems = refs[3:]
    else:
        packed, small_in, out, w, sems = refs
    (copy,) = load([(w_qkv.at[layer], w)], sems)
    packed[:, :D] = grad_q[...]
    packed[:, D:] = (dkv_own[...] + dkv_got[...].astype(F32)).astype(BF16)
    small_in[0:1] = jnp.sum(packed[:, :D].astype(F32), 0, keepdims=True)
    small_in[1:2] = jnp.sum(packed[:, 2 * D :].astype(F32), 0, keepdims=True)
    copy.wait()
    grad = grad_one[...] + dot_back(packed[...], w[...])
    if layer > 0:
        second_back(layer - 1, grad, hat2[...], inv2[:, 0:1], gains, mixed, grad_two, small)
    else:
        out[...] = grad.astype(BF16)


def grad_kernel(bit, block, chips, scal, own, other, rhs_own, rhs_other, send, keep, turned, picked):
    rows = own.shape[0]
    turned[:, 0:rows] = own[...].T
    turned[:, rows : 2 * rows] = other[...].T
    core, chip = scal[0], scal[4]
    mine = (chip >> bit) & 1
    half = chips // 2
    for part in range(2):
        want = (1 - mine) if part == 0 else mine
        for i in range(half):
            spot = ((i >> bit) << (bit + 1)) | (i & ((1 << bit) - 1))
            spot = ((spot + (want << bit)) * 2 + core) * block
            at = (part * half + i) * block
            picked[at : at + block, :] = turned[pl.ds(pl.multiple_of(spot, 16), block), :]
    cols = rhs_own.shape[1]
    step = 256
    for at in range(0, cols, step):
        lanes = slice(at, min(at + step, cols))
        out = dot(picked[:, 0:rows], rhs_own[:, lanes]) + dot(picked[:, rows:], rhs_other[:, lanes])
        out = out.astype(BF16)
        send[:, lanes] = out[: half * block]
        keep[:, lanes] = out[half * block :]


def weight_grad(place, scal, lhs, lhs_other, rhs, bit):
    rhs_other = place.swap_core(rhs)
    rows, m = lhs.shape
    cols = rhs.shape[1]
    chips = place.dp_width // 2
    block = m // place.dp_width
    shape = (m // 4, cols)
    if block % 16 == 0:
        return call(
            functools.partial(grad_kernel, bit - 1, block, chips),
            [(scal, "s"), (lhs, "v"), (lhs_other, "v"), (rhs, "v"), (rhs_other, "v")],
            [(shape, BF16), (shape, BF16)],
            [pltpu.VMEM((m, 2 * rows), BF16), pltpu.VMEM((m // 2, 2 * rows), BF16)],
            2 * rows * m * cols,
        )
    both = jnp.concatenate([lhs, lhs_other], 0).reshape(2 * rows, chips, 2, block)
    half = lax.dynamic_index_in_dim(both, place.core, 2, keepdims=False).reshape(2 * rows, m // 2)
    right = jnp.concatenate([rhs, rhs_other], 0)
    grad = lax.dot_general(half, right, (((0,), (0,)), ((), ())), preferred_element_type=F32).astype(BF16)
    grad = grad.reshape(chips >> bit, 2, m // 2 // (chips >> bit) // 2, cols)
    mine = (place.dp >> bit) % 2
    pick = lambda v: lax.dynamic_index_in_dim(grad, v, 1, keepdims=False).reshape(shape)
    return pick(1 - mine), pick(mine)


def local(
    tokens, cotangent, lengths, repeats, w_qkv, w_out, w_up, w_down, bias_qv, bias_proj, bias_up, gains, shifts
):
    place = Place()
    rows = 2 * tokens.shape[1]
    counts = jnp.stack([lengths, repeats])
    other_counts = place.swap_core(counts)
    counts = jnp.where(place.core == place.z // 2, counts, other_counts)
    counts = lax.dynamic_index_in_dim(counts, place.z % 2, 1, keepdims=False)
    zero = jnp.zeros((), jnp.int32)
    scal = jnp.stack([place.core, counts[0], counts[1], place.z % 2, place.dp // 2, zero, zero, zero])
    scal = scal.astype(jnp.int32)
    got = place.to_chip(tokens)
    cot = place.to_chip(cotangent)
    dma = pltpu.SemaphoreType.DMA
    wide, tall = (rows, D), (rows, FF)

    low, kv = call(
        first_kernel,
        [(scal, "s"), (got[0], "v"), (got[1], "v"), (w_qkv, "a"), (bias_qv, "v")],
        [(wide, BF16), ((rows, 2 * D), BF16)],
        [pltpu.VMEM((D, 2 * D), BF16), dma((1,))],
        4 * rows * D * D,
    )
    stream = low
    kept = []
    for layer in range(LAYERS):
        last = layer == LAYERS - 1
        kv_other = place.swap_core(kv)
        (q,) = call(
            functools.partial(query_kernel, layer),
            [(low, "v"), (w_qkv, "a"), (bias_qv, "v")],
            [(wide, BF16)],
            [pltpu.VMEM((D, D), BF16), dma((1,))],
            2 * rows * D * D,
        )
        operands = [(scal, "s"), (stream, "v"), (q, "v"), (kv, "v"), (kv_other, "v")]
        operands += [(w_out, "a"), (w_up, "a"), (w_down, "a"), (w_qkv, "a")]
        operands += [(bias_qv, "v"), (bias_proj, "v"), (bias_up, "v"), (gains, "v"), (shifts, "v")]
        outputs = [(wide, BF16), ((16, rows), F32), (wide, F32), ((rows, 128), F32)]
        outputs += [(wide, BF16), (tall, BF16), (tall, BF16)]
        if last:
            operands += [(cot[0], "v"), (cot[1], "v")]
            outputs += [(wide, BF16), (wide, BF16), (wide, F32), ((8, D), F32)]
        else:
            outputs += [(wide, F32), ((rows, 128), F32), (wide, F32), (wide, BF16), ((rows, 2 * D), BF16)]
        scratch = [pltpu.VMEM((D, D), BF16), pltpu.VMEM((D, FF), BF16), pltpu.VMEM((FF, D), BF16)]
        scratch += [pltpu.VMEM((D, 2 * D), BF16), pltpu.VMEM((D, rows), BF16), pltpu.VMEM((D, 2 * rows), BF16)]
        scratch += [pltpu.VMEM((D, rows), BF16), pltpu.VMEM(wide, F32), dma((4,))]
        got_back = call(
            functools.partial(layer_kernel, layer, last),
            operands,
            outputs,
            scratch,
            2 * rows * D * (D + 2 * FF + 2 * D) + 8 * rows * rows * D,
            rows * FF * 2 + HEADS * 2 * rows * rows,
        )
        att, lse, hat1, inv1, normed_low, active, slope = got_back[:7]
        pick = dict(low=low, q=q, kv=kv, kv_other=kv_other, att=att, lse=lse, hat1=hat1, inv1=inv1)
        pick.update(normed_low=normed_low, active=active, slope=slope)
        for name in ("low", "att", "normed_low", "active"):
            pick[name + "_other"] = place.swap_core(pick[name])
        if last:
            hidden_low, mixed, grad_two, small_two = got_back[7:]
        else:
            pick["hat2"], pick["inv2"], stream, low, kv = got_back[7:]
        kept.append(pick)
    hidden = place.from_chip(hidden_low).astype(F32)

    big = [None] * LAYERS
    small = [None] * LAYERS
    for layer in reversed(range(LAYERS)):
        k = kept[layer]
        down = weight_grad(place, scal, k["active"], k["active_other"], mixed, 1)
        grad_down = place.scatter_sum(*down, 1)
        grad_before, small_up = call(
            functools.partial(up_back_kernel, layer),
            [(mixed, "v"), (k["slope"], "v"), (w_down, "a")],
            [(tall, BF16), ((1, FF), F32)],
            [pltpu.VMEM((FF // FF_STEP, FF_STEP, D), BF16), dma((FF // FF_STEP,))],
            2 * rows * D * FF,
        )
        up = weight_grad(place, scal, k["normed_low"], k["normed_low_other"], grad_before, 2)
        grad_up = place.scatter_sum(*up, 2)
        scratch = [pltpu.VMEM((D, FF), BF16), pltpu.VMEM((D, D), BF16), pltpu.VMEM(wide, BF16)]
        scratch += [pltpu.VMEM((D, rows), BF16), pltpu.VMEM((D, rows), BF16), pltpu.VMEM((D, 2 * rows), BF16)]
        scratch += [pltpu.VMEM((D, rows), BF16), dma((2,))]
        grad_one, branch, grad_q, dkv, dkv_send, small_one = call(
            functools.partial(attention_back_kernel, layer),
            [(scal, "s"), (grad_before, "v"), (grad_two, "v"), (k["hat1"], "v"), (k["inv1"], "v"), (k["q"], "v")]
            + [(k["kv"], "v"), (k["kv_other"], "v"), (k["lse"], "v"), (w_up, "a"), (w_out, "a"), (gains, "v")],
            [(wide, F32), (wide, BF16), (wide, BF16), ((rows, 2 * D), F32), ((rows, 2 * D), BF16), ((8, D), F32)],
            scratch,
            2 * rows * D * (FF + D) + 20 * rows * rows * D,
            HEADS * 2 * rows * rows,
        )
        dkv_got = place.swap_core(dkv_send)
        out = weight_grad(place, scal, k["att"], k["att_other"], branch, 1 + layer % 2)
        grad_out = place.scatter_sum(*out, 1 + layer % 2)
        operands = [(grad_q, "v"), (dkv, "v"), (dkv_got, "v"), (grad_one, "v"), (w_qkv, "a")]
        outputs = [((rows, 3 * D), BF16), ((8, D), F32)]
        small_down = small_two
        if layer > 0:
            operands += [(kept[layer - 1]["hat2"], "v"), (kept[layer - 1]["inv2"], "v"), (gains, "v")]
            outputs += [(wide, BF16), (wide, F32), ((8, D), F32)]
        else:
            outputs += [(wide, BF16)]
        got_back = call(
            functools.partial(input_back_kernel, layer),
            operands,
            outputs,
            [pltpu.VMEM((D, 3 * D), BF16), dma((1,))],
            6 * rows * D * D,
        )
        packed, small_in = got_back[:2]
        if layer > 0:
            mixed, grad_two, small_two = got_back[2:]
        else:
            grad_low = got_back[2]
        qkv = weight_grad(place, scal, k["low"], k["low_other"], packed, 1 + layer % 2)
        grad_qkv = place.scatter_sum(*qkv, 1 + layer % 2)
        big[layer] = (grad_qkv, grad_out, grad_up, grad_down)
        table = [small_in[0], small_in[1], small_one[0], small_down[0]]
        table += [small_one[1], small_down[1], small_one[2], small_down[2], small_up[0]]
        small[layer] = jnp.concatenate(table)
    grad_tokens = place.from_chip(grad_low).astype(F32)
    total = place.all_sum(jnp.stack(small))
    table = total[:, : 8 * D].reshape(LAYERS, 8, D)
    stacked = [jnp.stack([big[layer][k] for layer in range(LAYERS)]) for k in range(4)]
    return (
        hidden,
        grad_tokens,
        *stacked,
        table[:, 0:2],
        table[:, 2:4],
        total[:, 8 * D :],
        table[:, 4:6],
        table[:, 6:8],
    )


def solution(mesh):
    rows = P("dp", "seq", None)
    blocks = P(None, "dp", "seq")
    return jax.shard_map(
        local,
        mesh=mesh,
        in_specs=(rows, rows, P("dp"), P("dp")) + (P(),) * 9,
        out_specs=(rows, rows) + (blocks,) * 4 + (P(),) * 5,
        check_vma=False,
    )
```

```python
import functools
import math

import jax
import jax.numpy as jnp
from jax import lax
from jax.experimental import pallas as pl
from jax.experimental.pallas import tpu as pltpu
from jax.sharding import PartitionSpec as P

D = 768
FF = 3072
HEADS = 12
HEAD = 64
PAIR = 2 * HEAD
LAYERS = 2
EPS = 1e-05
MASKED = -1000000000.0
SCALE = 1.0 / HEAD**0.5
F32 = jnp.float32
BF16 = jnp.bfloat16
FF_STEP = 1024
ERFCX_POINT = 0.48
ERFCX = (
    0.270751081,
    0.27211497,
    0.227394229,
    0.241744859,
    -0.115868816,
    0.444806334,
    -0.579913037,
    0.294191549,
    -0.05522118,
)
ACTIVE, NORMED, ATT, LOW = 0, FF, FF + D, FF + 2 * D
ACTS = FF + 3 * D
CORE, LOW_Z, CHIP, OWN_SEQ, Z = range(5)
SENDS = 4


class Place:
    def __init__(self):
        self.dp_width = lax.axis_size("dp")
        self.seq_width = lax.axis_size("seq")
        self.dp = lax.axis_index("dp")
        self.z = lax.axis_index("seq")
        self.core = self.dp % 2
        self.chips = self.dp_width // 2
        self.dp_bits = self.dp_width.bit_length() - 2
        self.seq_bits = self.seq_width.bit_length() - 1
        own_seq = (self.core == self.z // 2).astype(jnp.int32)
        self.vector = jnp.stack([self.core, self.z % 2, self.dp // 2, own_seq, self.z]).astype(jnp.int32)

    def swap_dp(self, value, bit):
        pairs = [(i, i ^ (1 << bit)) for i in range(self.dp_width)]
        return lax.ppermute(value, "dp", pairs)

    def swap_core(self, value):
        return self.swap_dp(value, 0)

    def swap_seq(self, value, bit):
        pairs = [(i, i ^ (1 << bit)) for i in range(self.seq_width)]
        return lax.ppermute(value, "seq", pairs)

    def spread_pairs(self, flip, back):
        pairs = []
        for dp in range(self.dp_width):
            chip, core = dp // 2, dp % 2
            for z in range(self.seq_width):
                s = (z % 2) ^ flip
                src = dp * self.seq_width + z
                dst = (2 * chip + z // 2) * self.seq_width + 2 * core + s
                pairs.append((dst, src) if back else (src, dst))
        return pairs

    def to_chip(self, value):
        low = self.z % 2
        first = lax.dynamic_index_in_dim(value, low, 0, keepdims=False)
        second = lax.dynamic_index_in_dim(value, 1 - low, 0, keepdims=False)
        got0 = lax.ppermute(first, ("dp", "seq"), self.spread_pairs(0, False))
        got1 = lax.ppermute(second, ("dp", "seq"), self.spread_pairs(1, False))
        return got0, got1

    def from_chip(self, first, second):
        got0 = lax.ppermute(first, ("dp", "seq"), self.spread_pairs(0, True))
        got1 = lax.ppermute(second, ("dp", "seq"), self.spread_pairs(1, True))
        even = self.z % 2 == 0
        return jnp.stack([jnp.where(even, got0, got1), jnp.where(even, got1, got0)], 0).astype(F32)

    def all_sum(self, value):
        value = value + self.swap_core(value)
        for bit in range(1, self.dp_bits + 1):
            value = value + self.swap_dp(value, bit)
        for bit in range(self.seq_bits):
            value = value + self.swap_seq(value, bit)
        return value

    def halve(self, blocks, axis, mine, swap):
        keep = lax.dynamic_index_in_dim(blocks, mine, axis, keepdims=False)
        send = lax.dynamic_index_in_dim(blocks, 1 - mine, axis, keepdims=False)
        got = swap(send)
        return (keep.astype(F32) + got.astype(F32)).astype(BF16)

    def scatter_plain(self, lhs, lhs_other, rhs, rhs_other):
        rows, m = lhs.shape
        cols = rhs.shape[1]
        block = m // self.dp_width
        both = jnp.concatenate([lhs, lhs_other], 0).reshape(2 * rows, self.chips, 2, block)
        half = lax.dynamic_index_in_dim(both, self.core, 2, keepdims=False).reshape(2 * rows, m // 2)
        right = jnp.concatenate([rhs, rhs_other], 0)
        grad = lax.dot_general(half, right, (((0,), (0,)), ((), ())), preferred_element_type=F32).astype(BF16)
        blocks = grad.reshape((2,) * self.dp_bits + (block, cols))
        for bit in range(self.dp_bits, 0, -1):
            mine = (self.dp >> bit) % 2
            blocks = self.halve(blocks, 0, mine, functools.partial(self.swap_dp, bit=bit))
        blocks = blocks.reshape(block, self.seq_width, cols // self.seq_width).transpose(1, 0, 2)
        blocks = blocks.reshape((2,) * self.seq_bits + (block, cols // self.seq_width))
        for bit in range(self.seq_bits - 1, -1, -1):
            mine = (self.z >> bit) % 2
            blocks = self.halve(blocks, 0, mine, functools.partial(self.swap_seq, bit=bit))
        return blocks.astype(F32)


class Chain:
    def __init__(self):
        self.last = None

    def call(self, body, operands, outputs, scratch, vmem=12, after=()):
        spaces = {"v": pltpu.VMEM, "h": pltpu.HBM, "s": pltpu.SMEM}
        count = len(operands)
        arrays = [pltpu.with_memory_space_constraint(a, pltpu.HBM) if p == "h" else a for a, p in operands]
        specs = [pl.BlockSpec(memory_space=spaces[p]) for _, p in operands]
        ahead = list(after) + ([] if self.last is None else [self.last])
        arrays += ahead
        specs += [pl.BlockSpec(memory_space=pl.ANY)] * len(ahead)

        def inner(*refs):
            return body(*refs[:count], *refs[count + len(ahead) :])

        results = pl.pallas_call(
            inner,
            out_shape=[jax.ShapeDtypeStruct(s, d) for s, d in outputs],
            in_specs=specs,
            out_specs=[pl.BlockSpec(memory_space=pltpu.VMEM) for _ in outputs],
            scratch_shapes=scratch,
            compiler_params=pltpu.CompilerParams(vmem_limit_bytes=vmem << 20),
            cost_estimate=pl.CostEstimate(flops=1024, bytes_accessed=1024, transcendentals=0),
        )(*arrays)
        self.last = results[0]
        return results


def dot(left, right):
    return jnp.dot(left, right, preferred_element_type=F32)


def dot_back(left, right):
    return lax.dot_general(left, right, (((1,), (1,)), ((), ())), preferred_element_type=F32)


def norm_parts(summed):
    average = jnp.mean(summed, -1, keepdims=True)
    centered = summed - average
    variance = jnp.mean(centered * centered, -1, keepdims=True)
    inverse = lax.rsqrt(variance + EPS)
    return centered * inverse, inverse


def norm_back(grad, hat, inverse, gain_row):
    scaled = grad * gain_row
    mean_one = jnp.mean(scaled, -1, keepdims=True)
    mean_hat = jnp.mean(scaled * hat, -1, keepdims=True)
    out = (scaled - mean_one - hat * mean_hat) * inverse
    return out, jnp.sum(grad * hat, 0, keepdims=True), jnp.sum(grad, 0, keepdims=True)


def gelu_parts(before):
    size = jnp.abs(before) * (0.5**0.5)
    spread = jnp.exp(-0.5 * before * before)
    t = 1.0 / (1.0 + ERFCX_POINT * size)
    poly = jnp.full_like(t, ERFCX[-1])
    for factor in ERFCX[-2::-1]:
        poly = poly * t + factor
    tail = 0.5 * (poly * t) * spread
    cdf = jnp.where(before >= 0.0, 1.0 - tail, tail)
    return before * cdf, cdf + before * (spread * 0.3989422804014327)


def load(pairs, sems):
    copies = [pltpu.make_async_copy(src, dst, sems.at[k]) for k, (src, dst) in enumerate(pairs)]
    for copy in copies:
        copy.start()
    return copies


def row(ref, *index):
    return ref[index[:-1] + (pl.ds(index[-1], 1), slice(None))].astype(F32)


def key_masks(scal, length_row, rows):
    spot = lax.broadcasted_iota(jnp.int32, (rows, rows), 0)
    own = (spot + scal[CORE] * rows).astype(F32) < length_row
    other = (spot + (1 - scal[CORE]) * rows).astype(F32) < length_row
    return own, other


def head_lanes(value, h, axis):
    spot = lax.broadcasted_iota(jnp.int32, value.shape, axis) // HEAD
    return jnp.where(spot == h, value, jnp.zeros_like(value))


def join(flag, first, second, out):
    half = first.shape[0]

    @pl.when(flag == 0)
    def _():
        out[0:half] = first[...].astype(out.dtype)
        out[half : 2 * half] = second[...].astype(out.dtype)

    @pl.when(flag != 0)
    def _():
        out[0:half] = second[...].astype(out.dtype)
        out[half : 2 * half] = first[...].astype(out.dtype)


def part(flag, value, first, second):
    half = first.shape[0]

    @pl.when(flag == 0)
    def _():
        first[...] = value[0:half]
        second[...] = value[half : 2 * half]

    @pl.when(flag != 0)
    def _():
        first[...] = value[half : 2 * half]
        second[...] = value[0:half]


def project(layer, low, w, bias_qv, q, kv):
    rows = low.shape[0]
    kv[0:rows, :D] = dot(low[...], w[:, D : 2 * D]).astype(BF16)
    kv[0:rows, D:] = (dot(low[...], w[:, 2 * D :]) + row(bias_qv, layer, 1)).astype(BF16)
    full = (dot(low[...], w[:, :D]) + row(bias_qv, layer, 0)).astype(BF16)
    q[...] = full * jnp.asarray(SCALE, BF16)


def first_kernel(scal, lengths, repeats, got0, got1, w_qkv, bias_qv, low, q, kv, w, sems):
    (copy,) = load([(w_qkv.at[0], w)], sems)
    join(scal[LOW_Z], got0, got1, low)
    rows = low.shape[0]
    spot = lax.broadcasted_iota(jnp.int32, (16, 2 * D), 0)
    facts = [lengths[0] // 16, lengths[0] % 16, lengths[1] // 16, lengths[1] % 16, repeats[0], repeats[1]]
    table = jnp.zeros((16, 2 * D), F32)
    for k, fact in enumerate(facts):
        table = jnp.where(spot == k, fact.astype(F32), table)
    kv[rows : rows + 16] = table.astype(BF16)
    copy.wait()
    project(0, low, w, bias_qv, q, kv)


def layer_kernel(layer, last, *refs):
    (scal, x, q, kv_own, kv_other, w_out, w_up, w_down) = refs[:8]
    (bias_proj, bias_up, gains, shifts) = refs[8:12]
    refs = refs[12:]
    if last:
        (meta, cot0, cot1) = refs[:3]
        refs = refs[3:]
    else:
        (w_qkv, bias_qv) = refs[:2]
        refs = refs[2:]
    (acts, lse, hat1, inv1, slope) = refs[:5]
    refs = refs[5:]
    if last:
        out0, out1, mixed, grad_two, small = refs[:5]
        refs = refs[5:]
    else:
        hat2, inv2, out, low, q_next, kv_next, meta = refs[:7]
        refs = refs[7:]
    (wo, wu, wd, w, qt, vt, ot, acc, sems) = refs
    rows = q.shape[0]
    moves = [(w_out.at[layer], wo), (w_up.at[layer], wu), (w_down.at[layer], wd)]
    if not last:
        moves.append((w_qkv.at[layer + 1], w))
        here = scal[OWN_SEQ] == 1
        facts = jnp.where(here, kv_own[rows:, :D].astype(F32), kv_other[rows:, :D].astype(F32))
        first = scal[LOW_Z] == 0
        meta[0:1] = jnp.where(first, facts[0:1] * 16.0 + facts[1:2], facts[2:3] * 16.0 + facts[3:4])
        meta[1:2] = jnp.where(first, facts[4:5], facts[5:6])
    copies = load(moves, sems)
    acts[:, LOW : LOW + D] = x[...].astype(BF16)
    qt[...] = q[...].T
    vt[:, 0:rows] = kv_own[0:rows, D:].T
    vt[:, rows : 2 * rows] = kv_other[0:rows, D:].T
    valid_own, valid_other = key_masks(scal, meta[0:1, 0:rows], rows)

    def pair(k, carry):
        lanes = pl.ds(pl.multiple_of(k * PAIR, PAIR), PAIR)
        keys_own, keys_other = kv_own[0:rows, lanes], kv_other[0:rows, lanes]
        q_pair = qt[lanes, :]
        for h in range(2):
            q_head = head_lanes(q_pair, h, 0)
            s_own = jnp.where(valid_own, dot(keys_own, q_head), MASKED)
            s_other = jnp.where(valid_other, dot(keys_other, q_head), MASKED)
            top = jnp.maximum(jnp.max(s_own, 0, keepdims=True), jnp.max(s_other, 0, keepdims=True))
            p_own = jnp.exp(s_own - top)
            p_other = jnp.exp(s_other - top)
            total = jnp.sum(p_own, 0, keepdims=True) + jnp.sum(p_other, 0, keepdims=True)
            head = pl.ds(pl.multiple_of(k * PAIR + h * HEAD, HEAD), HEAD)
            o = dot(vt[head, 0:rows], p_own.astype(BF16)) + dot(vt[head, rows : 2 * rows], p_other.astype(BF16))
            ot[head, :] = (o * (1.0 / total)).astype(BF16)
            lse[pl.ds(2 * k + h, 1), :] = top + jnp.log(total)
        return carry

    lax.fori_loop(0, HEADS // 2, pair, 0)
    acts[:, ATT : ATT + D] = ot[...].T
    copies[0].wait()
    h1, i1 = norm_parts(x[...].astype(F32) + (dot(acts[:, ATT : ATT + D], wo[...]) + row(bias_proj, layer, 0)))
    hat1[...] = h1
    inv1[...] = jnp.broadcast_to(i1, inv1.shape)
    normed = h1 * row(gains, layer, 0) + row(shifts, layer, 0)
    acts[:, NORMED : NORMED + D] = normed.astype(BF16)
    acc[...] = normed + row(bias_proj, layer, 1)
    copies[1].wait()
    copies[2].wait()
    for k in range(FF // FF_STEP):
        cols = slice(k * FF_STEP, (k + 1) * FF_STEP)
        before = dot(acts[:, NORMED : NORMED + D], wu[:, cols]) + bias_up[pl.ds(layer, 1), cols].astype(F32)
        value, steep = gelu_parts(before)
        value = value.astype(BF16)
        acts[:, cols] = value
        slope[:, cols] = steep.astype(BF16)
        acc[...] += dot(value, wd[cols, :])
    h2, i2 = norm_parts(acc[...])
    stream = h2 * row(gains, layer, 1) + row(shifts, layer, 1)
    if not last:
        hat2[...] = h2
        inv2[...] = jnp.broadcast_to(i2, inv2.shape)
        out[...] = stream
        low[...] = stream.astype(BF16)
        copies[3].wait()
        project(layer + 1, low, w, bias_qv, q_next, kv_next)
        return
    part(scal[LOW_Z], stream.astype(BF16), out0, out1)
    join(scal[LOW_Z], cot0, cot1, acc)
    spot = lax.broadcasted_iota(jnp.int32, (rows, D), 0) + scal[CORE] * rows
    grad = acc[...] * jnp.where(spot.astype(F32) < meta[0:1], meta[1:2], 0.0)
    second_back(layer, grad, h2, i2, gains, mixed, grad_two, small)


def second_back(layer, grad, hat, inverse, gains, mixed, grad_two, small):
    two, gain_two, shift_two = norm_back(grad, hat, inverse, row(gains, layer, 1))
    grad_two[...] = two
    mixed[...] = two.astype(BF16)
    small[0:1] = jnp.sum(mixed[...].astype(F32), 0, keepdims=True)
    small[1:2] = gain_two
    small[2:3] = shift_two


def load_down(layer, w_down, wd, sems):
    step = wd.shape[1]
    return load([(w_down.at[layer, pl.ds(k * step, step)], wd.at[k]) for k in range(wd.shape[0])], sems)


def up_back(copies, mixed, slope, grad_before, bias_up_grad, wd):
    step = wd.shape[1]
    for k, out in enumerate(grad_before):
        copies[k].wait()
        cols = slice(k * step, (k + 1) * step)
        value = (dot_back(mixed[...], wd[k]) * slope[:, cols].astype(F32)).astype(BF16)
        out[...] = value
        bias_up_grad[:, cols] = jnp.sum(value.astype(F32), 0, keepdims=True)


def up_back_kernel(layer, mixed, slope, w_down, *refs):
    grad_before, (bias_up_grad, wd, sems) = refs[:-3], refs[-3:]
    up_back(load_down(layer, w_down, wd, sems), mixed, slope, grad_before, bias_up_grad, wd)


def attention_back_kernel(layer, blocks, *refs):
    grad_before, refs = refs[:blocks], refs[blocks:]
    (scal, meta, grad_two, hat1, inv1, q, kv_own, kv_other, lse, w_up, w_out, gains) = refs[:12]
    (grad_one, branch, grad_q, dkv_own, small) = refs[12:17]
    sends, (wu, wo, datt, qt, dot_t, kt, dqt, dkv_other, sems) = refs[17:-9], refs[-9:]
    rows = q.shape[0]
    copies = load([(w_up.at[layer], wu), (w_out.at[layer], wo)], sems)
    qt[...] = q[...].T
    kt[:, 0:rows] = kv_own[0:rows, :D].T
    kt[:, rows : 2 * rows] = kv_other[0:rows, :D].T
    copies[0].wait()
    grad_normed = grad_two[...]
    for k, before in enumerate(grad_before):
        width = before.shape[1]
        grad_normed += dot_back(before[...], wu[:, k * width : (k + 1) * width])
    one, gain_one, shift_one = norm_back(grad_normed, hat1[...], inv1[:, 0:1], row(gains, layer, 0))
    grad_one[...] = one
    branch[...] = one.astype(BF16)
    small[0:1] = jnp.sum(branch[...].astype(F32), 0, keepdims=True)
    small[1:2] = gain_one
    small[2:3] = shift_one
    copies[1].wait()
    datt[...] = dot_back(branch[...], wo[...]).astype(BF16)
    dot_t[...] = datt[...].T
    valid_own, valid_other = key_masks(scal, meta[0:1, 0:rows], rows)

    def pair(k, carry):
        lanes = pl.ds(pl.multiple_of(k * PAIR, PAIR), PAIR)
        v_lanes = pl.ds(pl.multiple_of(D + k * PAIR, PAIR), PAIR)
        keys_own, keys_other = kv_own[0:rows, lanes], kv_other[0:rows, lanes]
        vals_own, vals_other = kv_own[0:rows, v_lanes], kv_other[0:rows, v_lanes]
        sums = None
        for h in range(2):
            qt_head = head_lanes(qt[lanes, :], h, 0)
            dt_head = head_lanes(dot_t[lanes, :], h, 0)
            q_head = head_lanes(q[:, lanes], h, 1)
            d_head = head_lanes(datt[:, lanes], h, 1)
            log_total = lse[pl.ds(2 * k + h, 1), :]
            p_own = jnp.exp(jnp.where(valid_own, dot(keys_own, qt_head), MASKED) - log_total)
            p_other = jnp.exp(jnp.where(valid_other, dot(keys_other, qt_head), MASKED) - log_total)
            dw_own = dot(vals_own, dt_head)
            dw_other = dot(vals_other, dt_head)
            delta = jnp.sum(p_own * dw_own, 0, keepdims=True) + jnp.sum(p_other * dw_other, 0, keepdims=True)
            ds_own = (p_own * (dw_own - delta)).astype(BF16)
            ds_other = (p_other * (dw_other - delta)).astype(BF16)
            head = pl.ds(pl.multiple_of(k * PAIR + h * HEAD, HEAD), HEAD)
            dq = dot(kt[head, 0:rows], ds_own) + dot(kt[head, rows : 2 * rows], ds_other)
            dqt[head, :] = (dq * SCALE).astype(BF16)
            parts = (
                dot(ds_own, q_head),
                dot(ds_other, q_head),
                dot(p_own.astype(BF16), d_head),
                dot(p_other.astype(BF16), d_head),
            )
            sums = parts if sums is None else tuple(a + b for a, b in zip(sums, parts))
        dkv_own[:, lanes] = sums[0]
        dkv_other[:, lanes] = sums[1].astype(BF16)
        dkv_own[:, v_lanes] = sums[2]
        dkv_other[:, v_lanes] = sums[3].astype(BF16)
        return carry

    lax.fori_loop(0, HEADS // 2, pair, 0)
    grad_q[...] = dqt[...].T
    for k, send in enumerate(sends):
        width = send.shape[1]
        send[...] = dkv_other[:, k * width : (k + 1) * width]


def input_back_kernel(layer, seq_width, *refs):
    got, refs = refs[:SENDS], refs[SENDS:]
    (scal, grad_q, dkv_own, grad_one, branch, w_qkv) = refs[:6]
    refs = refs[6:]
    if layer > 0:
        hat2, inv2, gains, slope, w_down = refs[:5]
        refs = refs[5:]
    right, refs = refs[:seq_width], refs[seq_width:]
    if layer > 0:
        grad_before, refs = refs[:seq_width], refs[seq_width:]
        small_in, mixed, grad_two, small, bias_up_grad, w, packed, wd, sems, down_sems = refs
        down_copies = load_down(layer - 1, w_down, wd, down_sems)
    else:
        small_in, out0, out1, w, packed, sems = refs
    (copy,) = load([(w_qkv.at[layer], w)], sems)
    packed[:, :D] = grad_q[...]
    for k, part_got in enumerate(got):
        width = part_got.shape[1]
        cols = slice(k * width, (k + 1) * width)
        packed[:, D + k * width : D + (k + 1) * width] = (dkv_own[:, cols] + part_got[...].astype(F32)).astype(BF16)
    small_in[0:1] = jnp.sum(packed[:, :D].astype(F32), 0, keepdims=True)
    small_in[1:2] = jnp.sum(packed[:, 2 * D :].astype(F32), 0, keepdims=True)
    wide, thin = 3 * D // seq_width, D // seq_width
    for z in range(seq_width):
        right[z][:, 0:wide] = packed[:, z * wide : (z + 1) * wide]
        right[z][:, wide : wide + thin] = branch[:, z * thin : (z + 1) * thin]
    copy.wait()
    grad = grad_one[...] + dot_back(packed[...], w[...])
    if layer > 0:
        second_back(layer - 1, grad, hat2[...], inv2[:, 0:1], gains, mixed, grad_two, small)
        up_back(down_copies, mixed, slope, grad_before, bias_up_grad, wd)
    else:
        part(scal[LOW_Z], grad.astype(BF16), out0, out1)


def spread_bit(i, bit, value):
    return ((i >> bit) << (bit + 1)) | (value << bit) | (i & ((1 << bit) - 1))


def chip_order(bit, scal, chips):
    mine = (scal[CHIP] >> bit) & 1
    return [spread_bit(i, bit, v) for v in (1 - mine, mine) for i in range(chips // 2)]


def turn(own, other, turned):
    rows = own.shape[0]
    turned[:, 0:rows] = own[...].T
    turned[:, rows : 2 * rows] = other[...].T


def pick_rows(turned, picked, order, core, block):
    for i, chip in enumerate(order):
        at = pl.multiple_of((chip * 2 + core) * block, 16)
        picked[i * block : (i + 1) * block, :] = turned[pl.ds(at, block), :]


def put(out, send, keep, z, chips, block, lanes):
    half = chips // 2
    for i in range(chips):
        dst = send if i < half else keep
        dst[i % half, z, :, lanes] = out[i * block : (i + 1) * block].astype(BF16)


def down_kernel(plan, scal, acts, acts_other, mixed, mixed_other, send, keep, turned):
    bit, chips, seq_width, block = plan
    rows = mixed.shape[0]
    turn(mixed, mixed_other, turned)
    width = FF // (2 * chips)
    for i, chip in enumerate(chip_order(bit, scal, chips)):
        cols = pl.ds(pl.multiple_of((chip * 2 + scal[CORE]) * width, 128), width)
        out = dot(turned[:, 0:rows], acts[:, cols]) + dot(turned[:, rows:], acts_other[:, cols])
        out = out.astype(BF16)
        dst = send if i < chips // 2 else keep
        for z in range(seq_width):
            for h in range(2):
                at = (2 * z + h) * block
                dst[i % (chips // 2), z, :, h * width : (h + 1) * width] = out[at : at + block]


def up_kernel(plan, scal, acts, acts_other, *refs):
    bit, chips, seq_width, block = plan
    right, right_other, refs = refs[:seq_width], refs[seq_width : 2 * seq_width], refs[2 * seq_width :]
    send, keep, turned, picked = refs
    rows = acts.shape[0]
    normed = slice(NORMED, NORMED + D)
    turn(acts.at[:, normed], acts_other.at[:, normed], turned)
    pick_rows(turned, picked, chip_order(bit, scal, chips), scal[CORE], block)
    wide = FF // seq_width
    for z in range(seq_width):
        out = dot(picked[:, 0:rows], right[z][...]) + dot(picked[:, rows:], right_other[z][...])
        put(out, send, keep, z, chips, block, slice(0, wide))


def oq_parts(low_rows, att_rows, right, right_other, wide):
    rows = right.shape[0]
    q_part = dot(low_rows[:, 0:rows], right[:, :wide]) + dot(low_rows[:, rows:], right_other[:, :wide])
    o_part = dot(att_rows[:, 0:rows], right[:, wide:]) + dot(att_rows[:, rows:], right_other[:, wide:])
    return q_part, o_part


def oq_half_kernel(plan, scal, acts, acts_other, *refs):
    bits, chips, seq_width, block = plan
    right, right_other, refs = refs[:seq_width], refs[seq_width : 2 * seq_width], refs[2 * seq_width :]
    outs = refs[:4]
    turned_low, turned_att, low_rows, att_rows = refs[4:]
    turn(acts.at[:, LOW : LOW + D], acts_other.at[:, LOW : LOW + D], turned_low)
    turn(acts.at[:, ATT : ATT + D], acts_other.at[:, ATT : ATT + D], turned_att)
    width = FF // seq_width
    wide = 3 * D // seq_width
    half = seq_width // 2
    for part_at in range(2):
        send, keep = outs[2 * part_at : 2 * part_at + 2]
        order = chip_order(bits[part_at], scal, chips)
        pick_rows(turned_low, low_rows.at[part_at], order, scal[CORE], block)
        pick_rows(turned_att, att_rows.at[part_at], order, scal[CORE], block)
        for z in range(part_at * half, (part_at + 1) * half):
            q_part, o_part = oq_parts(low_rows.at[part_at], att_rows.at[part_at], right[z], right_other[z], wide)
            put(q_part, send, keep, z % half, chips, block, slice(0, wide))
            put(o_part, send, keep, z % half, chips, block, slice(wide, width))


def add_kernel(groups, splits, scal, *refs):
    keeps, gots = refs[0 : 2 * groups : 2], refs[1 : 2 * groups : 2]
    send, keep = refs[2 * groups : 2 * groups + 2]
    at = 0
    for got, kept, (bit, entry, shift) in zip(gots, keeps, splits):
        count = kept.shape[0]
        mine = (scal[entry] >> shift) & 1
        for i in range(count // 2):
            for dst, v in ((send, 1 - mine), (keep, mine)):
                src = spread_bit(i, bit, v)
                dst[at + i] = (kept[src].astype(F32) + got[src].astype(F32)).astype(BF16)
        at += count // 2


def pack_kernel(*refs):
    out = refs[-1]
    for layer in range(LAYERS):
        first, one, two, up = refs[4 * layer : 4 * layer + 4]
        at = 12 * layer
        out[at : at + 2] = first[0:2]
        for k in range(3):
            out[at + 2 + 2 * k : at + 3 + 2 * k] = one[k : k + 1]
            out[at + 3 + 2 * k : at + 4 + 2 * k] = two[k : k + 1]
        for k in range(FF // D):
            out[at + 8 + k : at + 9 + k] = up[:, k * D : (k + 1) * D]


def last_kernel(plan, *refs):
    seq_width, block = plan
    pairs = refs[: 4 * LAYERS]
    grad_qkv, grad_out, grad_up, grad_down = refs[4 * LAYERS :][:4]
    wide = 3 * D // seq_width
    for layer in range(LAYERS):
        du, du_got, oq, oq_got = pairs[4 * layer : 4 * layer + 4]
        down = du[0].astype(F32) + du_got[0].astype(F32)
        width = down.shape[1] // 2
        grad_down[layer, 0:width, 0:block] = down[:, :width].T
        grad_down[layer, 0:width, block : 2 * block] = down[:, width:].T
        grad_up[layer] = du[1].astype(F32) + du_got[1].astype(F32)
        last = oq[0].astype(F32) + oq_got[0].astype(F32)
        grad_qkv[layer] = last[:, :wide]
        grad_out[layer] = last[:, wide:]


class Bundles:
    def __init__(self, place, chain, rows):
        self.place, self.chain, self.rows = place, chain, rows
        self.block = D // place.dp_width
        self.fast = place.chips == 4 and place.seq_width == 4 and self.block % 16 == 0
        self.cols = FF // place.seq_width

    def shape(self, *lead):
        return (lead + (self.block, self.cols), BF16)

    def run(self, *members, vmem=24, after=()):
        operands, outputs, scratch = [], [], []
        for _, own, out, temp in members:
            operands += [(a, "v") for a in own]
            outputs += out
            scratch += [pltpu.VMEM(shape, BF16) for shape in temp]

        def body(scal, *refs):
            ins, outs, temps = refs[: len(operands)], refs[len(operands) :][: len(outputs)], refs[len(operands) :]
            temps = temps[len(outputs) :]
            for member, own, out, temp in members:
                member(scal, *ins[: len(own)], *outs[: len(out)], *temps[: len(temp)])
                ins, outs, temps = ins[len(own) :], outs[len(out) :], temps[len(temp) :]

        results = self.chain.call(body, [(self.place.vector, "s")] + operands, outputs, scratch, vmem, after)
        parts = []
        for _, _, out, _ in members:
            parts.append(results[: len(out)])
            results = results[len(out) :]
        return parts if len(members) > 1 else parts[0]

    def down(self, acts, acts_other, mixed, mixed_other, bit):
        plan = (bit, self.place.chips, self.place.seq_width, self.block)
        out = self.shape(self.place.chips // 2, self.place.seq_width)
        operands = [acts, acts_other, mixed, mixed_other]
        return functools.partial(down_kernel, plan), operands, [out] * 2, [(D, 2 * self.rows)]

    def up(self, acts, acts_other, right, right_other, bit):
        plan = (bit, self.place.chips, self.place.seq_width, self.block)
        out = self.shape(self.place.chips // 2, self.place.seq_width)
        operands = [acts, acts_other, *right, *right_other]
        scratch = [(D, 2 * self.rows), (D // 2, 2 * self.rows)]
        return functools.partial(up_kernel, plan), operands, [out] * 2, scratch

    def oq_half(self, acts, acts_other, right, right_other):
        plan = ((0, 1), self.place.chips, self.place.seq_width, self.block)
        out = self.shape(self.place.chips // 2, self.place.seq_width // 2)
        operands = [acts, acts_other, *right, *right_other]
        scratch = [(D, 2 * self.rows)] * 2 + [(2, D // 2, 2 * self.rows)] * 2
        return functools.partial(oq_half_kernel, plan), operands, [out] * 4, scratch

    def add(self, pairs, splits):
        flat = [v.reshape((-1, self.block, self.cols)) for pair in pairs for v in pair]
        out = self.shape(sum(v.shape[0] for v in flat[::2]) // 2)
        return functools.partial(add_kernel, len(pairs), splits), flat, [out, out], []


def local(
    tokens, cotangent, lengths, repeats, w_qkv, w_out, w_up, w_down, bias_qv, bias_proj, bias_up, gains, shifts
):
    place = Place()
    chain = Chain()
    rows = 2 * tokens.shape[1]
    bundles = Bundles(place, chain, rows)
    scal = (place.vector, "s")
    dma = pltpu.SemaphoreType.DMA
    wide, tall = (rows, D), (rows, FF)
    part_shape = ((rows // 2, D), BF16)
    weight = {"qkv": (w_qkv, "h"), "out": (w_out, "h"), "up": (w_up, "h"), "down": (w_down, "h")}
    tables = {"qv": (bias_qv, "v"), "proj": (bias_proj, "v"), "up": (bias_up, "v")}
    tables.update(gains=(gains, "v"), shifts=(shifts, "v"))
    swap = place.swap_core

    got = place.to_chip(tokens)
    low, q, kv = chain.call(
        first_kernel,
        [scal, (lengths, "s"), (repeats, "s"), (got[0], "v"), (got[1], "v"), weight["qkv"], tables["qv"]],
        [(wide, BF16), (wide, BF16), ((rows + 16, 2 * D), BF16)],
        [pltpu.VMEM((D, 3 * D), BF16), dma((1,))],
        16,
    )
    cot = place.to_chip(cotangent)
    stream, kept = low, []
    for layer in range(LAYERS):
        last = layer == LAYERS - 1
        kv_other = swap(kv)
        operands = [scal, (stream, "v"), (q, "v"), (kv, "v"), (kv_other, "v")]
        operands += [weight["out"], weight["up"], weight["down"]]
        operands += [tables["proj"], tables["up"], tables["gains"], tables["shifts"]]
        outputs = [((rows, ACTS), BF16), ((16, rows), F32), (wide, F32), ((rows, 128), F32), (tall, BF16)]
        if last:
            operands += [(meta, "v"), (cot[0], "v"), (cot[1], "v")]
            outputs += [part_shape, part_shape, (wide, BF16), (wide, F32), ((8, D), F32)]
        else:
            operands += [weight["qkv"], tables["qv"]]
            outputs += [(wide, F32), ((rows, 128), F32), (wide, F32), (wide, BF16), (wide, BF16)]
            outputs += [((rows, 2 * D), BF16), ((8, D), F32)]
        scratch = [pltpu.VMEM((D, D), BF16), pltpu.VMEM((D, FF), BF16), pltpu.VMEM((FF, D), BF16)]
        scratch += [pltpu.VMEM((D, 3 * D), BF16), pltpu.VMEM((D, rows), BF16), pltpu.VMEM((D, 2 * rows), BF16)]
        scratch += [pltpu.VMEM((D, rows), BF16), pltpu.VMEM(wide, F32), dma((4,))]
        results = chain.call(functools.partial(layer_kernel, layer, last), operands, outputs, scratch, 32)
        acts, lse, hat1, inv1, slope = results[:5]
        values = dict(q=q, kv=kv, kv_other=kv_other, acts=acts, lse=lse, hat1=hat1, inv1=inv1, slope=slope)
        if last:
            out0, out1, mixed, grad_two, small_two = results[5:]
        else:
            values["hat2"], values["inv2"], stream, low, q, kv, meta = results[5:]
        values["acts_other"] = swap(acts)
        kept.append(values)
    hidden = place.from_chip(out0, out1)

    seqs = place.seq_width
    block_shape = ((rows, FF // seqs), BF16)
    swap_all = lambda values: [swap(v) for v in values]

    def up_back_first(layer, mixed):
        results = chain.call(
            functools.partial(up_back_kernel, layer),
            [(mixed, "v"), (kept[layer]["slope"], "v"), weight["down"]],
            [block_shape] * seqs + [((1, FF), F32)],
            [pltpu.VMEM((seqs, FF // seqs, D), BF16), dma((seqs,))],
            16,
        )
        return results[:seqs], results[seqs]

    def attention_back(layer, grad_before, grad_two):
        k = kept[layer]
        scratch = [pltpu.VMEM((D, FF), BF16), pltpu.VMEM((D, D), BF16), pltpu.VMEM(wide, BF16)]
        scratch += [pltpu.VMEM((D, rows), BF16), pltpu.VMEM((D, rows), BF16), pltpu.VMEM((D, 2 * rows), BF16)]
        scratch += [pltpu.VMEM((D, rows), BF16), pltpu.VMEM((rows, 2 * D), BF16), dma((2,))]
        operands = [(v, "v") for v in grad_before] + [scal, (meta, "v"), (grad_two, "v")]
        operands += [(k[name], "v") for name in ("hat1", "inv1", "q", "kv", "kv_other", "lse")]
        operands += [weight["up"], weight["out"], tables["gains"]]
        outputs = [(wide, F32), (wide, BF16), (wide, BF16), ((rows, 2 * D), F32), ((8, D), F32)]
        outputs += [((rows, 2 * D // SENDS), BF16)] * SENDS
        body = functools.partial(attention_back_kernel, layer, seqs)
        return chain.call(body, operands, outputs, scratch, 20)

    def input_back(layer, grad_one, branch, grad_q, dkv, small, *sends):
        operands = [(v, "v") for v in swap_all(sends)]
        operands += [scal, (grad_q, "v"), (dkv, "v"), (grad_one, "v"), (branch, "v"), weight["qkv"]]
        outputs = [((rows, 4 * D // seqs), BF16)] * seqs
        scratch = [pltpu.VMEM((D, 3 * D), BF16), pltpu.VMEM((rows, 3 * D), BF16)]
        if layer > 0:
            before = kept[layer - 1]
            operands += [(before["hat2"], "v"), (before["inv2"], "v"), tables["gains"]]
            operands += [(before["slope"], "v"), weight["down"]]
            outputs += [block_shape] * seqs + [((8, D), F32), (wide, BF16), (wide, F32), ((8, D), F32), ((1, FF), F32)]
            scratch += [pltpu.VMEM((seqs, FF // seqs, D), BF16), dma((1,)), dma((seqs,))]
        else:
            outputs += [((8, D), F32), part_shape, part_shape]
            scratch += [dma((1,))]
        body = functools.partial(input_back_kernel, layer, seqs)
        results = chain.call(body, operands, outputs, scratch, 20)
        return results[:seqs], results[seqs:]

    fast = bundles.fast
    z_wide, z_thin = 3 * D // place.seq_width, D // place.seq_width
    plain = [None] * LAYERS

    def plain_sums(layer, mixed, mixed_other, grad_before, before_other, right, right_other):
        k = kept[layer]
        pick = lambda name, at, width: k[name][:, at : at + width]
        join = lambda values, parts: jnp.concatenate([v[:, parts] for v in values], 1)
        results = []
        for at, parts in ((LOW, slice(0, z_wide)), (ATT, slice(z_wide, None))):
            rhs = [join(v, parts) for v in (right, right_other)]
            results.append(place.scatter_plain(pick("acts", at, D), pick("acts_other", at, D), *rhs))
        results.append(
            place.scatter_plain(
                pick("acts", NORMED, D),
                pick("acts_other", NORMED, D),
                join(grad_before, slice(None)),
                join(before_other, slice(None)),
            )
        )
        results.append(
            place.scatter_plain(pick("acts", ACTIVE, FF), pick("acts_other", ACTIVE, FF), mixed, mixed_other)
        )
        return results

    x_bit, y_bit = (CHIP, 0), (CHIP, 1)
    z_low, z_high = (Z, 0), (Z, 1)

    k1, k0 = kept[1], kept[0]
    acts1, acts0 = (k1["acts"], k1["acts_other"]), (k0["acts"], k0["acts_other"])
    mixed1, mixed1_other = mixed, swap(mixed)
    before1, small_up1 = up_back_first(1, mixed1)
    before1_other = swap_all(before1)
    if fast:
        d1, u1 = bundles.run(
            bundles.down(*acts1, mixed1, mixed1_other, 0), bundles.up(*acts1, before1, before1_other, 1)
        )
        d1_got = place.swap_dp(d1[0], 1)
        u1_got = place.swap_dp(u1[0], 2)
    back = attention_back(1, before1, grad_two)
    small_one1 = back[4]
    right1, results = input_back(1, *back)
    before0, (small_in1, mixed0, grad_two, small_two0, small_up0) = results[:seqs], results[seqs:]
    mixed0_other = swap(mixed0)
    before0_other = swap_all(before0)
    right1_other = swap_all(right1)
    if fast:
        d1, u1 = bundles.run(
            bundles.add([(d1[1], d1_got)], [(2, *y_bit)]),
            bundles.add([(u1[1], u1_got)], [(2, *x_bit)]),
        )
        d1_got = place.swap_dp(d1[0], 2)
        u1_got = place.swap_dp(u1[0], 1)
        d0, u0 = bundles.run(
            bundles.down(*acts0, mixed0, mixed0_other, 0),
            bundles.up(*acts0, before0, before0_other, 1),
            after=right1_other,
        )
        d0_got = place.swap_dp(d0[0], 1)
        u0_got = place.swap_dp(u0[0], 2)
    else:
        plain[1] = plain_sums(1, mixed1, mixed1_other, before1, before1_other, right1, right1_other)
    back = attention_back(0, before0, grad_two)
    small_one0 = back[4]
    if fast:
        du1 = bundles.run(bundles.add([(d1[1], d1_got), (u1[1], u1_got)], [(0, *z_low)] * 2))
        du1_got = place.swap_seq(du1[0], 0)
        oq1a, oq1a_keep, oq1b, oq1b_keep = bundles.run(bundles.oq_half(*acts1, right1, right1_other))
        oq1a_got = place.swap_dp(oq1a, 1)
        oq1b_got = place.swap_dp(oq1b, 2)
    right0, (small_in0, last0, last1) = input_back(0, *back)
    right0_other = swap_all(right0)
    grad_tokens = place.from_chip(last0, last1)
    if fast:
        d0, u0 = bundles.run(
            bundles.add([(d0[1], d0_got)], [(2, *y_bit)]), bundles.add([(u0[1], u0_got)], [(2, *x_bit)])
        )
        d0_got = place.swap_dp(d0[0], 2)
        u0_got = place.swap_dp(u0[0], 1)
        oq0a, oq0a_keep, oq0b, oq0b_keep = bundles.run(bundles.oq_half(*acts0, right0, right0_other))
        oq0a_got = place.swap_dp(oq0a, 1)
        oq0b_got = place.swap_dp(oq0b, 2)
    smalls = []
    for group in ((small_in0, small_one0, small_two0, small_up0), (small_in1, small_one1, small_two, small_up1)):
        smalls += [(v, "v") for v in group]
    (table,) = chain.call(pack_kernel, smalls, [((LAYERS * 12, D), F32)], [])
    if fast:
        half_bits = [(1, *y_bit)], [(1, *x_bit)]
        oq1a, oq1b = bundles.run(
            bundles.add([(oq1a_keep, oq1a_got)], half_bits[0]), bundles.add([(oq1b_keep, oq1b_got)], half_bits[1])
        )
        oq1a_got = place.swap_dp(oq1a[0], 2)
        oq1b_got = place.swap_dp(oq1b[0], 1)
        du1 = bundles.run(bundles.add([(du1[1], du1_got)], [(0, *z_high)]))
        du1_got = place.swap_seq(du1[0], 1)
        oq0a, oq0b = bundles.run(
            bundles.add([(oq0a_keep, oq0a_got)], half_bits[0]), bundles.add([(oq0b_keep, oq0b_got)], half_bits[1])
        )
        oq0a_got = place.swap_dp(oq0a[0], 2)
        oq0b_got = place.swap_dp(oq0b[0], 1)
        oq1 = bundles.run(bundles.add([(oq1a[1], oq1a_got), (oq1b[1], oq1b_got)], [(0, *z_low)] * 2))
        oq1_got = place.swap_seq(oq1[0], 0)
        du0 = bundles.run(bundles.add([(d0[1], d0_got), (u0[1], u0_got)], [(0, *z_low)] * 2))
        du0_got = place.swap_seq(du0[0], 0)
        oq1 = bundles.run(bundles.add([(oq1[1], oq1_got)], [(0, *z_high)]))
        oq1_got = place.swap_seq(oq1[0], 1)
        oq0 = bundles.run(bundles.add([(oq0a[1], oq0a_got), (oq0b[1], oq0b_got)], [(0, *z_low)] * 2))
        oq0_got = place.swap_seq(oq0[0], 0)
        du0 = bundles.run(bundles.add([(du0[1], du0_got)], [(0, *z_high)]))
        du0_got = place.swap_seq(du0[0], 1)
        oq0 = bundles.run(bundles.add([(oq0[1], oq0_got)], [(0, *z_high)]))
        oq0_got = place.swap_seq(oq0[0], 1)
        pairs = []
        for du, du_got, oq, oq_got in ((du0, du0_got, oq0, oq0_got), (du1, du1_got, oq1, oq1_got)):
            pairs += [(du[1], "v"), (du_got, "v"), (oq[1], "v"), (oq_got, "v")]
        block = bundles.block
        shapes = [(block, z_wide), (block, z_thin), (block, bundles.cols), (FF // place.dp_width, z_thin)]
        stacked = chain.call(
            functools.partial(last_kernel, (place.seq_width, block)),
            pairs,
            [((LAYERS,) + shape, F32) for shape in shapes],
            [],
        )
    else:
        plain[0] = plain_sums(0, mixed0, mixed0_other, before0, before0_other, right0, right0_other)
        stacked = [jnp.stack([plain[layer][k] for layer in range(LAYERS)]) for k in range(4)]
    total = place.all_sum(table).reshape(LAYERS, 12, D)
    return (
        hidden,
        grad_tokens,
        *stacked,
        total[:, 0:2],
        total[:, 2:4],
        total[:, 8:12].reshape(LAYERS, FF),
        total[:, 4:6],
        total[:, 6:8],
    )


def solution(mesh):
    rows = P("dp", "seq", None)
    blocks = P(None, "dp", "seq")
    return jax.shard_map(
        local,
        mesh=mesh,
        in_specs=(rows, rows, P("dp"), P("dp")) + (P(),) * 9,
        out_specs=(rows, rows) + (blocks,) * 4 + (P(),) * 5,
        check_vma=False,
    )
```

```python
import functools
import math

import jax
import jax.numpy as jnp
from jax import lax
from jax.experimental import pallas as pl
from jax.experimental.pallas import tpu as pltpu
from jax.sharding import PartitionSpec as P

D = 768
FF = 3072
HEADS = 12
HEAD = 64
PAIR = 2 * HEAD
LAYERS = 2
EPS = 1e-05
MASKED = -1000000000.0
SCALE = 1.0 / HEAD**0.5
F32 = jnp.float32
BF16 = jnp.bfloat16
FF_STEP = 1024
ERFCX_POINT = 0.48
ERFCX = (
    0.270751081,
    0.27211497,
    0.227394229,
    0.241744859,
    -0.115868816,
    0.444806334,
    -0.579913037,
    0.294191549,
    -0.05522118,
)
ACTIVE, NORMED, ATT, LOW = 0, FF, FF + D, FF + 2 * D
ACTS = FF + 3 * D
CORE, LOW_Z, CHIP, OWN_SEQ, Z = range(5)
DIMS = {"x": (CHIP, 0), "y": (CHIP, 1), "z0": (Z, 0), "z1": (Z, 1)}
COSTS = (90, 0)
TAIL = 32
SENDS = 3


class Place:
    def __init__(self):
        self.dp_width = lax.axis_size("dp")
        self.seq_width = lax.axis_size("seq")
        self.dp = lax.axis_index("dp")
        self.z = lax.axis_index("seq")
        self.core = self.dp % 2
        self.chips = self.dp_width // 2
        self.dp_bits = self.dp_width.bit_length() - 2
        self.seq_bits = self.seq_width.bit_length() - 1
        own_seq = (self.core == self.z // 2).astype(jnp.int32)
        self.vector = jnp.stack([self.core, self.z % 2, self.dp // 2, own_seq, self.z]).astype(jnp.int32)

    def swap_dp(self, value, bit):
        pairs = [(i, i ^ (1 << bit)) for i in range(self.dp_width)]
        return lax.ppermute(value, "dp", pairs)

    def swap(self, value, dim):
        if dim == "core":
            return self.swap_core(value)
        entry, bit = DIMS[dim]
        return self.swap_seq(value, bit) if entry == Z else self.swap_dp(value, bit + 1)

    def swap_core(self, value):
        return self.swap_dp(value, 0)

    def swap_seq(self, value, bit):
        pairs = [(i, i ^ (1 << bit)) for i in range(self.seq_width)]
        return lax.ppermute(value, "seq", pairs)

    def spread_pairs(self, flip, back):
        pairs = []
        for dp in range(self.dp_width):
            chip, core = dp // 2, dp % 2
            for z in range(self.seq_width):
                s = (z % 2) ^ flip
                src = dp * self.seq_width + z
                dst = (2 * chip + z // 2) * self.seq_width + 2 * core + s
                pairs.append((dst, src) if back else (src, dst))
        return pairs

    def to_chip(self, *values):
        low = self.z % 2
        pick = lambda at: jnp.stack([lax.dynamic_index_in_dim(value, at, 0, keepdims=False) for value in values])
        first, second = pick(low), pick(1 - low)
        got0 = lax.ppermute(first, ("dp", "seq"), self.spread_pairs(0, False))
        got1 = lax.ppermute(second, ("dp", "seq"), self.spread_pairs(1, False))
        return got0, got1

    def from_chip(self, first, second):
        got0 = lax.ppermute(first, ("dp", "seq"), self.spread_pairs(0, True))
        got1 = lax.ppermute(second, ("dp", "seq"), self.spread_pairs(1, True))
        even = self.z % 2 == 0
        return jnp.stack([jnp.where(even, got0, got1), jnp.where(even, got1, got0)], 0).astype(F32)

    def all_sum(self, value):
        value = value + self.swap_core(value)
        for bit in range(1, self.dp_bits + 1):
            value = value + self.swap_dp(value, bit)
        for bit in range(self.seq_bits):
            value = value + self.swap_seq(value, bit)
        return value

    def halve(self, blocks, axis, mine, swap):
        keep = lax.dynamic_index_in_dim(blocks, mine, axis, keepdims=False)
        send = lax.dynamic_index_in_dim(blocks, 1 - mine, axis, keepdims=False)
        got = swap(send)
        return (keep.astype(F32) + got.astype(F32)).astype(BF16)

    def scatter_plain(self, lhs, lhs_other, rhs, rhs_other):
        rows, m = lhs.shape
        cols = rhs.shape[1]
        block = m // self.dp_width
        both = jnp.concatenate([lhs, lhs_other], 0).reshape(2 * rows, self.chips, 2, block)
        half = lax.dynamic_index_in_dim(both, self.core, 2, keepdims=False).reshape(2 * rows, m // 2)
        right = jnp.concatenate([rhs, rhs_other], 0)
        grad = lax.dot_general(half, right, (((0,), (0,)), ((), ())), preferred_element_type=F32).astype(BF16)
        blocks = grad.reshape((2,) * self.dp_bits + (block, cols))
        for bit in range(self.dp_bits, 0, -1):
            mine = (self.dp >> bit) % 2
            blocks = self.halve(blocks, 0, mine, functools.partial(self.swap_dp, bit=bit))
        blocks = blocks.reshape(block, self.seq_width, cols // self.seq_width).transpose(1, 0, 2)
        blocks = blocks.reshape((2,) * self.seq_bits + (block, cols // self.seq_width))
        for bit in range(self.seq_bits - 1, -1, -1):
            mine = (self.z >> bit) % 2
            blocks = self.halve(blocks, 0, mine, functools.partial(self.swap_seq, bit=bit))
        return blocks.astype(F32)


class Chain:
    def __init__(self):
        self.last = None

    def call(self, body, operands, outputs, scratch, vmem=12, after=(), cost=0):
        spaces = {"v": pltpu.VMEM, "h": pltpu.HBM, "s": pltpu.SMEM, "far": pltpu.VMEM}
        count = len(operands)
        arrays = [pltpu.with_memory_space_constraint(a, pltpu.HBM) if p in ("h", "far") else a for a, p in operands]
        specs = [pl.BlockSpec(memory_space=spaces[p]) for _, p in operands]
        ahead = list(after) + ([] if self.last is None else [self.last])
        arrays += ahead
        specs += [pl.BlockSpec(memory_space=pl.ANY)] * len(ahead)

        def inner(*refs):
            return body(*refs[:count], *refs[count + len(ahead) :])

        results = pl.pallas_call(
            inner,
            out_shape=[pltpu.HBM(s, d) if far else jax.ShapeDtypeStruct(s, d) for s, d, *far in outputs],
            in_specs=specs,
            out_specs=[pl.BlockSpec(memory_space=pltpu.VMEM) for _ in outputs],
            scratch_shapes=scratch,
            compiler_params=pltpu.CompilerParams(vmem_limit_bytes=vmem << 20),
            cost_estimate=pl.CostEstimate(flops=1024 + cost * 10**9, bytes_accessed=1024, transcendentals=0),
        )(*arrays)
        self.last = results[0]
        return results


def dot(left, right):
    return jnp.dot(left, right, preferred_element_type=F32)


def dot_back(left, right):
    return lax.dot_general(left, right, (((1,), (1,)), ((), ())), preferred_element_type=F32)


def norm_parts(summed):
    average = jnp.mean(summed, -1, keepdims=True)
    centered = summed - average
    variance = jnp.mean(centered * centered, -1, keepdims=True)
    inverse = lax.rsqrt(variance + EPS)
    return centered * inverse, inverse


def norm_back(grad, hat, inverse, gain_row):
    scaled = grad * gain_row
    mean_one = jnp.mean(scaled, -1, keepdims=True)
    mean_hat = jnp.mean(scaled * hat, -1, keepdims=True)
    out = (scaled - mean_one - hat * mean_hat) * inverse
    return out, jnp.sum(grad * hat, 0, keepdims=True), jnp.sum(grad, 0, keepdims=True)


def gelu_parts(before):
    size = jnp.abs(before) * (0.5**0.5)
    spread = jnp.exp(-0.5 * before * before)
    t = 1.0 / (1.0 + ERFCX_POINT * size)
    poly = jnp.full_like(t, ERFCX[-1])
    for factor in ERFCX[-2::-1]:
        poly = poly * t + factor
    tail = 0.5 * (poly * t) * spread
    cdf = jnp.where(before >= 0.0, 1.0 - tail, tail)
    return before * cdf, cdf + before * (spread * 0.3989422804014327)


def load(pairs, sems):
    copies = [pltpu.make_async_copy(src, dst, sems.at[k]) for k, (src, dst) in enumerate(pairs)]
    for copy in copies:
        copy.start()
    return copies


def row(ref, *index):
    return ref[index[:-1] + (pl.ds(index[-1], 1), slice(None))].astype(F32)


def key_masks(scal, length_row, rows):
    spot = lax.broadcasted_iota(jnp.int32, (rows, rows), 0)
    own = (spot + scal[CORE] * rows).astype(F32) < length_row
    other = (spot + (1 - scal[CORE]) * rows).astype(F32) < length_row
    return own, other


def head_lanes(value, h, axis):
    spot = lax.broadcasted_iota(jnp.int32, value.shape, axis) // HEAD
    return jnp.where(spot == h, value, jnp.zeros_like(value))


def join(flag, first, second, out):
    half = first.shape[0]

    @pl.when(flag == 0)
    def _():
        out[0:half] = first[...].astype(out.dtype)
        out[half : 2 * half] = second[...].astype(out.dtype)

    @pl.when(flag != 0)
    def _():
        out[0:half] = second[...].astype(out.dtype)
        out[half : 2 * half] = first[...].astype(out.dtype)


def part(flag, value, first, second):
    half = first.shape[0]

    @pl.when(flag == 0)
    def _():
        first[...] = value[0:half]
        second[...] = value[half : 2 * half]

    @pl.when(flag != 0)
    def _():
        first[...] = value[half : 2 * half]
        second[...] = value[0:half]


def project(layer, low, w, bias_qv, q, kv):
    rows = low.shape[0]
    kv[0:rows, :D] = dot(low[...], w[:, D : 2 * D]).astype(BF16)
    kv[0:rows, D:] = (dot(low[...], w[:, 2 * D :]) + row(bias_qv, layer, 1)).astype(BF16)
    full = (dot(low[...], w[:, :D]) + row(bias_qv, layer, 0)).astype(BF16)
    q[...] = full * jnp.asarray(SCALE, BF16)


def first_kernel(scal, lengths, repeats, got0, got1, w_qkv, bias_qv, low, q, kv, w, sems):
    (copy,) = load([(w_qkv.at[0], w)], sems)
    join(scal[LOW_Z], got0.at[0], got1.at[0], low)
    rows = low.shape[0]
    spot = lax.broadcasted_iota(jnp.int32, (16, 2 * D), 0)
    facts = [lengths[0] // 16, lengths[0] % 16, lengths[1] // 16, lengths[1] % 16, repeats[0], repeats[1]]
    table = jnp.zeros((16, 2 * D), F32)
    for k, fact in enumerate(facts):
        table = jnp.where(spot == k, fact.astype(F32), table)
    kv[rows : rows + 16] = table.astype(BF16)
    copy.wait()
    project(0, low, w, bias_qv, q, kv)


def core_halves(core, chips, acts, turned, rows_keep, rows_send, cols_keep, cols_send):
    for which, rows_out, cols_out in ((core, rows_keep, cols_keep), (1 - core, rows_send, cols_send)):
        for k, source in enumerate(turned):
            block = D // (2 * chips)
            for chip in range(chips):
                at = pl.multiple_of((chip * 2 + which) * block, block)
                rows_out[k, chip * block : (chip + 1) * block] = source[pl.ds(at, block), :]
        width = FF // (2 * chips)
        for chip in range(chips):
            at = pl.multiple_of((chip * 2 + which) * width, width)
            cols_out[:, chip * width : (chip + 1) * width] = acts[:, pl.ds(at, width)]


def layer_kernel(layer, last, chips, *refs):
    (scal, x, q, kv_own, kv_other, w_out, w_up, w_down) = refs[:8]
    (bias_proj, bias_up, gains, shifts) = refs[8:12]
    refs = refs[12:]
    if last:
        (meta, cot0, cot1) = refs[:3]
        refs = refs[3:]
    else:
        (w_qkv, bias_qv) = refs[:2]
        refs = refs[2:]
    (lse, hat1, inv1, slope) = refs[:4]
    refs = refs[4:]
    if chips:
        halves, refs = refs[:4], refs[4:]
    else:
        acts, refs = refs[0], refs[1:]
    if last:
        out0, out1, mixed, grad_two, small = refs[:5]
        refs = refs[5:]
    else:
        hat2, inv2, out, low, q_next, kv_next, meta = refs[:7]
        refs = refs[7:]
    (wo, wu, wd, w, qt, vt, ot, acc, sems) = refs[:9]
    rows = q.shape[0]
    if chips:
        acts, normed_t, low_t = refs[9:]
    moves = [(w_out.at[layer], wo), (w_up.at[layer], wu), (w_down.at[layer], wd)]
    if not last:
        moves.append((w_qkv.at[layer + 1], w))
        here = scal[OWN_SEQ] == 1
        facts = jnp.where(here, kv_own[rows:, :D].astype(F32), kv_other[rows:, :D].astype(F32))
        first = scal[LOW_Z] == 0
        meta[0:1] = jnp.where(first, facts[0:1] * 16.0 + facts[1:2], facts[2:3] * 16.0 + facts[3:4])
        meta[1:2] = jnp.where(first, facts[4:5], facts[5:6])
    copies = load(moves, sems)
    acts[:, LOW : LOW + D] = x[...].astype(BF16)
    qt[...] = q[...].T
    vt[:, 0:rows] = kv_own[0:rows, D:].T
    vt[:, rows : 2 * rows] = kv_other[0:rows, D:].T
    valid_own, valid_other = key_masks(scal, meta[0:1, 0:rows], rows)

    def pair(k, carry):
        lanes = pl.ds(pl.multiple_of(k * PAIR, PAIR), PAIR)
        keys_own, keys_other = kv_own[0:rows, lanes], kv_other[0:rows, lanes]
        q_pair = qt[lanes, :]
        for h in range(2):
            q_head = head_lanes(q_pair, h, 0)
            s_own = jnp.where(valid_own, dot(keys_own, q_head), MASKED)
            s_other = jnp.where(valid_other, dot(keys_other, q_head), MASKED)
            top = jnp.maximum(jnp.max(s_own, 0, keepdims=True), jnp.max(s_other, 0, keepdims=True))
            p_own = jnp.exp(s_own - top)
            p_other = jnp.exp(s_other - top)
            total = jnp.sum(p_own, 0, keepdims=True) + jnp.sum(p_other, 0, keepdims=True)
            head = pl.ds(pl.multiple_of(k * PAIR + h * HEAD, HEAD), HEAD)
            o = dot(vt[head, 0:rows], p_own.astype(BF16)) + dot(vt[head, rows : 2 * rows], p_other.astype(BF16))
            ot[head, :] = (o * (1.0 / total)).astype(BF16)
            lse[pl.ds(2 * k + h, 1), :] = top + jnp.log(total)
        return carry

    lax.fori_loop(0, HEADS // 2, pair, 0)
    acts[:, ATT : ATT + D] = ot[...].T
    copies[0].wait()
    h1, i1 = norm_parts(x[...].astype(F32) + (dot(acts[:, ATT : ATT + D], wo[...]) + row(bias_proj, layer, 0)))
    hat1[...] = h1
    inv1[...] = jnp.broadcast_to(i1, inv1.shape)
    normed = h1 * row(gains, layer, 0) + row(shifts, layer, 0)
    acts[:, NORMED : NORMED + D] = normed.astype(BF16)
    acc[...] = normed + row(bias_proj, layer, 1)
    copies[1].wait()
    copies[2].wait()
    for k in range(FF // FF_STEP):
        cols = slice(k * FF_STEP, (k + 1) * FF_STEP)
        before = dot(acts[:, NORMED : NORMED + D], wu[:, cols]) + bias_up[pl.ds(layer, 1), cols].astype(F32)
        value, steep = gelu_parts(before)
        value = value.astype(BF16)
        acts[:, cols] = value
        slope[:, cols] = steep.astype(BF16)
        acc[...] += dot(value, wd[cols, :])
    if chips:
        low_t[...] = acts[:, LOW : LOW + D].T
        normed_t[...] = acts[:, NORMED : NORMED + D].T
        core_halves(scal[CORE], chips, acts, (normed_t, ot, low_t), *halves)
    h2, i2 = norm_parts(acc[...])
    stream = h2 * row(gains, layer, 1) + row(shifts, layer, 1)
    if not last:
        hat2[...] = h2
        inv2[...] = jnp.broadcast_to(i2, inv2.shape)
        out[...] = stream
        low[...] = stream.astype(BF16)
        copies[3].wait()
        project(layer + 1, low, w, bias_qv, q_next, kv_next)
        return
    part(scal[LOW_Z], stream.astype(BF16), out0, out1)
    join(scal[LOW_Z], cot0.at[1], cot1.at[1], acc)
    spot = lax.broadcasted_iota(jnp.int32, (rows, D), 0) + scal[CORE] * rows
    grad = acc[...] * jnp.where(spot.astype(F32) < meta[0:1], meta[1:2], 0.0)
    second_back(layer, grad, h2, i2, gains, mixed, grad_two, small)


def second_back(layer, grad, hat, inverse, gains, mixed, grad_two, small):
    two, gain_two, shift_two = norm_back(grad, hat, inverse, row(gains, layer, 1))
    grad_two[...] = two
    mixed[...] = two.astype(BF16)
    small[0:1] = jnp.sum(mixed[...].astype(F32), 0, keepdims=True)
    small[1:2] = gain_two
    small[2:3] = shift_two


def load_down(layer, w_down, wd, sems):
    step = wd.shape[1]
    return load([(w_down.at[layer, pl.ds(k * step, step)], wd.at[k]) for k in range(wd.shape[0])], sems)


def up_back(copies, mixed, slope, grad_before, bias_up_grad, wd):
    step = wd.shape[1]
    for k, out in enumerate(grad_before):
        copies[k].wait()
        cols = slice(k * step, (k + 1) * step)
        value = (dot_back(mixed[...], wd[k]) * slope[:, cols].astype(F32)).astype(BF16)
        out[...] = value
        bias_up_grad[:, cols] = jnp.sum(value.astype(F32), 0, keepdims=True)


def up_back_kernel(layer, mixed, slope, w_down, *refs):
    grad_before, (bias_up_grad, wd, sems) = refs[:-3], refs[-3:]
    up_back(load_down(layer, w_down, wd, sems), mixed, slope, grad_before, bias_up_grad, wd)


def attention_back_kernel(layer, blocks, *refs):
    grad_before, refs = refs[:blocks], refs[blocks:]
    (scal, meta, grad_two, hat1, inv1, q, kv_own, kv_other, lse, w_up, w_out, gains) = refs[:12]
    (grad_one, branch, grad_q, dkv_own, small) = refs[12:17]
    sends, (wu, wo, datt, qt, dot_t, kt, dqt, dkv_other, sems) = refs[17:-9], refs[-9:]
    rows = q.shape[0]
    copies = load([(w_up.at[layer], wu), (w_out.at[layer], wo)], sems)
    qt[...] = q[...].T
    kt[:, 0:rows] = kv_own[0:rows, :D].T
    kt[:, rows : 2 * rows] = kv_other[0:rows, :D].T
    copies[0].wait()
    grad_normed = grad_two[...]
    for k, before in enumerate(grad_before):
        width = before.shape[1]
        grad_normed += dot_back(before[...], wu[:, k * width : (k + 1) * width])
    one, gain_one, shift_one = norm_back(grad_normed, hat1[...], inv1[:, 0:1], row(gains, layer, 0))
    grad_one[...] = one
    branch[...] = one.astype(BF16)
    small[0:1] = jnp.sum(branch[...].astype(F32), 0, keepdims=True)
    small[1:2] = gain_one
    small[2:3] = shift_one
    copies[1].wait()
    datt[...] = dot_back(branch[...], wo[...]).astype(BF16)
    dot_t[...] = datt[...].T
    valid_own, valid_other = key_masks(scal, meta[0:1, 0:rows], rows)

    def pair(k, carry):
        lanes = pl.ds(pl.multiple_of(k * PAIR, PAIR), PAIR)
        v_lanes = pl.ds(pl.multiple_of(D + k * PAIR, PAIR), PAIR)
        keys_own, keys_other = kv_own[0:rows, lanes], kv_other[0:rows, lanes]
        vals_own, vals_other = kv_own[0:rows, v_lanes], kv_other[0:rows, v_lanes]
        sums = None
        for h in range(2):
            qt_head = head_lanes(qt[lanes, :], h, 0)
            dt_head = head_lanes(dot_t[lanes, :], h, 0)
            q_head = head_lanes(q[:, lanes], h, 1)
            d_head = head_lanes(datt[:, lanes], h, 1)
            log_total = lse[pl.ds(2 * k + h, 1), :]
            p_own = jnp.exp(jnp.where(valid_own, dot(keys_own, qt_head), MASKED) - log_total)
            p_other = jnp.exp(jnp.where(valid_other, dot(keys_other, qt_head), MASKED) - log_total)
            dw_own = dot(vals_own, dt_head)
            dw_other = dot(vals_other, dt_head)
            delta = jnp.sum(p_own * dw_own, 0, keepdims=True) + jnp.sum(p_other * dw_other, 0, keepdims=True)
            ds_own = (p_own * (dw_own - delta)).astype(BF16)
            ds_other = (p_other * (dw_other - delta)).astype(BF16)
            head = pl.ds(pl.multiple_of(k * PAIR + h * HEAD, HEAD), HEAD)
            dq = dot(kt[head, 0:rows], ds_own) + dot(kt[head, rows : 2 * rows], ds_other)
            dqt[head, :] = (dq * SCALE).astype(BF16)
            parts = (
                dot(ds_own, q_head),
                dot(ds_other, q_head),
                dot(p_own.astype(BF16), d_head),
                dot(p_other.astype(BF16), d_head),
            )
            sums = parts if sums is None else tuple(a + b for a, b in zip(sums, parts))
        dkv_own[:, lanes] = sums[0]
        dkv_other[:, lanes] = sums[1].astype(BF16)
        dkv_own[:, v_lanes] = sums[2]
        dkv_other[:, v_lanes] = sums[3].astype(BF16)
        return carry

    lax.fori_loop(0, HEADS // 2, pair, 0)
    grad_q[...] = dqt[...].T
    for k, send in enumerate(sends):
        width = send.shape[1]
        send[...] = dkv_other[:, k * width : (k + 1) * width]


def input_back_kernel(layer, seq_width, *refs):
    got, refs = refs[:SENDS], refs[SENDS:]
    (scal, grad_q, dkv_own, grad_one, branch, w_qkv) = refs[:6]
    refs = refs[6:]
    if layer > 0:
        hat2, inv2, gains, slope, w_down = refs[:5]
        refs = refs[5:]
    right, refs = refs[0], refs[1:]
    if layer > 0:
        grad_before, refs = refs[:seq_width], refs[seq_width:]
        small_in, mixed, grad_two, small, bias_up_grad, w, packed, wd, sems, down_sems = refs
        down_copies = load_down(layer - 1, w_down, wd, down_sems)
    else:
        small_in, out0, out1, w, packed, sems = refs
    (copy,) = load([(w_qkv.at[layer], w)], sems)
    packed[:, :D] = grad_q[...]
    for k, part_got in enumerate(got):
        width = part_got.shape[1]
        cols = slice(k * width, (k + 1) * width)
        packed[:, D + k * width : D + (k + 1) * width] = (dkv_own[:, cols] + part_got[...].astype(F32)).astype(BF16)
    small_in[0:1] = jnp.sum(packed[:, :D].astype(F32), 0, keepdims=True)
    small_in[1:2] = jnp.sum(packed[:, 2 * D :].astype(F32), 0, keepdims=True)
    wide, thin = 3 * D // seq_width, D // seq_width
    for z in range(seq_width):
        at = z * (wide + thin)
        right[:, at : at + wide] = packed[:, z * wide : (z + 1) * wide]
        right[:, at + wide : at + wide + thin] = branch[:, z * thin : (z + 1) * thin]
    copy.wait()
    grad = grad_one[...] + dot_back(packed[...], w[...])
    if layer > 0:
        second_back(layer - 1, grad, hat2[...], inv2[:, 0:1], gains, mixed, grad_two, small)
        up_back(down_copies, mixed, slope, grad_before, bias_up_grad, wd)
    else:
        part(scal[LOW_Z], grad.astype(BF16), out0, out1)


def spread_bit(i, bit, value):
    return ((i >> bit) << (bit + 1)) | (value << bit) | (i & ((1 << bit) - 1))


def chip_order(first, scal, chips):
    if first == "z0":
        return list(range(chips))
    bit = DIMS[first][1]
    mine = (scal[CHIP] >> bit) & 1
    return [spread_bit(i, bit, v) for v in (1 - mine, mine) for i in range(chips // 2)]


def pick_rows(source, order, block, out):
    for i, chip in enumerate(order):
        at = pl.multiple_of(chip * block, block)
        out[i * block : (i + 1) * block, :] = source[pl.ds(at, block), :]


def put(first, scal, chips, z, parts, block, send, keep):
    def store(dst, at, rows):
        for value, lanes in parts:
            dst[at[0], at[1], :, lanes] = value[rows]

    spots = [slice(i * block, (i + 1) * block) for i in range(chips)]
    if first != "z0":
        half = chips // 2
        for i in range(chips):
            store(send if i < half else keep, (i % half, z), spots[i])
        return

    @pl.when(scal[LOW_Z] == z % 2)
    def _():
        for i in range(chips):
            store(keep, (i, z // 2), spots[i])

    @pl.when(scal[LOW_Z] != z % 2)
    def _():
        for i in range(chips):
            store(send, (i, z // 2), spots[i])


def down_kernel(plan, scal, cols, cols_other, mixed, mixed_other, send, keep, turned):
    first, chips, seq_width, block = plan
    rows = mixed.shape[0]
    turned[:, 0:rows] = mixed[...].T
    turned[:, rows : 2 * rows] = mixed_other[...].T
    width = FF // (2 * chips)
    half = chips // 2
    for i, chip in enumerate(chip_order(first, scal, chips)):
        lanes = pl.ds(pl.multiple_of(chip * width, width), width)
        out = dot(turned[:, 0:rows], cols[:, lanes]) + dot(turned[:, rows:], cols_other[:, lanes])
        out = out.astype(BF16)
        dst = send if i < half else keep
        for z in range(seq_width):
            for h in range(2):
                at = (2 * z + h) * block
                dst[i % half, z, :, h * width : (h + 1) * width] = out[at : at + block]


def up_kernel(plan, scal, lhs, lhs_other, *refs):
    first, chips, seq_width, block = plan
    right, right_other, refs = refs[:seq_width], refs[seq_width : 2 * seq_width], refs[2 * seq_width :]
    send, keep, own, other = refs
    order = chip_order(first, scal, chips)
    pick_rows(lhs.at[0], order, block, own)
    pick_rows(lhs_other.at[0], order, block, other)
    for z in range(seq_width):
        out = dot(own[...], right[z][...]) + dot(other[...], right_other[z][...])
        put(first, scal, chips, z, [(out.astype(BF16), slice(None))], block, send, keep)


def oq_kernel(plan, scal, lhs, lhs_other, right, right_other, *refs):
    firsts, chips, seq_width, block = plan
    outs, (low_own, low_other, att_own, att_other) = refs[: 2 * len(firsts)], refs[2 * len(firsts) :]
    wide, width = 3 * D // seq_width, FF // seq_width
    count = seq_width // len(firsts)
    for k, first in enumerate(firsts):
        order = chip_order(first, scal, chips)
        for at, source, own in ((2, lhs, low_own), (2, lhs_other, low_other), (1, lhs, att_own), (1, lhs_other, att_other)):
            pick_rows(source.at[at], order, block, own.at[k])
        for z in range(count):
            at = (k * count + z) * width
            q_cols, o_cols = slice(at, at + wide), slice(at + wide, at + width)
            q_part = dot(low_own[k], right[:, q_cols]) + dot(low_other[k], right_other[:, q_cols])
            o_part = dot(att_own[k], right[:, o_cols]) + dot(att_other[k], right_other[:, o_cols])
            parts = [(q_part.astype(BF16), slice(0, wide)), (o_part.astype(BF16), slice(wide, None))]
            put(first, scal, chips, z, parts, block, outs[2 * k], outs[2 * k + 1])


def tail_sum(table, got):
    if got.dtype == F32:
        return table[...] + got[...]
    count = table.shape[0]
    rows = got.shape[0]
    return table[...].astype(BF16).astype(F32) + got[rows - TAIL : rows, :][0:count].astype(F32)


def add_kernel(groups, splits, block, scal, *refs):
    keeps, gots = refs[0 : 2 * groups : 2], refs[1 : 2 * groups : 2]
    refs = refs[2 * groups :]
    if len(refs) > 2:
        table, table_got, send, keep, table_out = refs
        table_out[...] = tail_sum(table, table_got)
        send[send.shape[0] - TAIL :, :] = jnp.zeros((TAIL, send.shape[1]), BF16)
        send[send.shape[0] - TAIL : send.shape[0] - TAIL + table.shape[0], :] = table_out[...].astype(BF16)
    else:
        send, keep = refs
    at = 0
    for got, kept, (bit, entry, shift) in zip(gots, keeps, splits):
        count = kept.shape[0] // block
        mine = (scal[entry] >> shift) & 1
        for i in range(count // 2):
            for dst, v in ((send, 1 - mine), (keep, mine)):
                src = pl.ds(pl.multiple_of(spread_bit(i, bit, v) * block, block), block)
                dst[at * block : (at + 1) * block] = (kept[src].astype(F32) + got[src].astype(F32)).astype(BF16)
            at += 1


def pack_kernel(*refs):
    out = refs[-1]
    for layer in range(LAYERS):
        first, one, two, up = refs[4 * layer : 4 * layer + 4]
        at = 12 * layer
        out[at : at + 2] = first[0:2]
        for k in range(3):
            out[at + 2 + 2 * k : at + 3 + 2 * k] = one[k : k + 1]
            out[at + 3 + 2 * k : at + 4 + 2 * k] = two[k : k + 1]
        for k in range(FF // D):
            out[at + 8 + k : at + 9 + k] = up[:, k * D : (k + 1) * D]


def finish_kernel(scal, one, two, out):
    out[...] = (one[...].astype(F32) + two[...].astype(F32)).astype(out.dtype)


def last_kernel(plan, *refs):
    seq_width, block, places, tail = plan
    table, grad_qkv, grad_out, grad_up, grad_down, total = refs[-6:]
    total[...] = tail_sum(table, refs[tail])
    wide = 3 * D // seq_width
    for layer in range(LAYERS):
        sums = []
        for flow, at in places[layer]:
            rows = slice(at * block, (at + 1) * block)
            sums.append(sum(refs[k][rows].astype(F32) for k in flow))
        down, up, oq = sums
        width = down.shape[1] // 2
        grad_down[layer, 0:width, 0:block] = down[:, :width].T
        grad_down[layer, 0:width, block : 2 * block] = down[:, width:].T
        grad_up[layer] = up
        grad_qkv[layer] = oq[:, :wide]
        grad_out[layer] = oq[:, wide:]


class Bundles:
    def __init__(self, place, chain, rows):
        self.place, self.chain, self.rows = place, chain, rows
        self.block = D // place.dp_width
        self.fast = place.chips == 4 and place.seq_width == 4 and self.block % 16 == 0
        self.cols = FF // place.seq_width

    def shape(self, *lead):
        return lead + (self.block, self.cols), BF16

    def run(self, *members, vmem=14, after=(), cost=0):
        operands, outputs, scratch = [], [], []
        for _, own, out, temp in members:
            operands += [a if isinstance(a, tuple) else (a, "v") for a in own]
            outputs += out
            scratch += [pltpu.VMEM(shape, BF16) for shape in temp]

        def body(scal, *refs):
            ins, outs, temps = refs[: len(operands)], refs[len(operands) :][: len(outputs)], refs[len(operands) :]
            temps = temps[len(outputs) :]
            for member, own, out, temp in members:
                member(scal, *ins[: len(own)], *outs[: len(out)], *temps[: len(temp)])
                ins, outs, temps = ins[len(own) :], outs[len(out) :], temps[len(temp) :]

        results = self.chain.call(body, [(self.place.vector, "s")] + operands, outputs, scratch, vmem, after, cost)
        parts = []
        for _, _, out, _ in members:
            parts.append(results[: len(out)])
            results = results[len(out) :]
        return parts if len(members) > 1 else parts[0]

    def first(self, first, count):
        chips, seqs = self.place.chips, count
        if first == "z0":
            return self.shape(chips, seqs // 2), ["y", "x", "z1"][: 2 + (seqs > 2)]
        left = ["x" if first == "y" else "y"] + ["z1", "z0"][-1 if seqs == 2 else 0 :]
        return self.shape(chips // 2, seqs), left

    def down(self, first, halves, mixed, mixed_other):
        plan = (first, self.place.chips, self.place.seq_width, self.block)
        out, left = self.first(first, self.place.seq_width)
        operands = [halves[1][0], halves[1][1], mixed, mixed_other]
        member = functools.partial(down_kernel, plan), operands, [out] * 2, [(D, 2 * self.rows)]
        return member, [(first, left)]

    def up(self, first, halves, right, right_other):
        plan = (first, self.place.chips, self.place.seq_width, self.block)
        out, left = self.first(first, self.place.seq_width)
        operands = [*halves[0], *right, *right_other]
        scratch = [(D // 2, self.rows)] * 2
        return (functools.partial(up_kernel, plan), operands, [out] * 2, scratch), [(first, left)]

    def oq(self, firsts, halves, right, right_other):
        plan = (firsts, self.place.chips, self.place.seq_width, self.block)
        kinds = [self.first(first, self.place.seq_width // len(firsts)) for first in firsts]
        outs = [out for out, _ in kinds for _ in range(2)]
        operands = [*halves[0], right, right_other]
        scratch = [(len(firsts), D // 2, self.rows)] * 4
        member = functools.partial(oq_kernel, plan), operands, outs, scratch
        return member, [(first, left) for first, (_, left) in zip(firsts, kinds)]

    def make(self, *members, far=False):
        where = ("far",) if far else ()
        calls = [(body, ins, [out + where for out in outs], temps) for (body, ins, outs, temps), _ in members]
        results = self.run(*calls)
        flows = []
        for (_, kinds), out in zip(members, results if len(members) > 1 else [results]):
            for k, (first, left) in enumerate(kinds):
                flows.append(Flow(self.place, out[2 * k], out[2 * k + 1], first, left, *where))
        return flows

    def finish(self, flow):
        return "finish", flow

    def add(self, *steps, after=(), cost=0):
        members = []
        for flows, dim, *more in steps:
            if flows == "finish":
                members.append((finish_kernel, [dim.keep, dim.got], [(dim.keep.shape, BF16)], []))
                continue
            operands = [(v, flow.place) for flow in flows for v in (flow.keep, flow.got)]
            splits = [(len(flow.left) - 1 - flow.left.index(dim), *DIMS[dim]) for flow in flows]
            rows = sum(flow.keep.shape[0] for flow in flows) // 2
            send, outs = rows, []
            if more and isinstance(more[-1], tuple):
                operands += more[-1]
                send, outs = rows + TAIL, [(more[-1][0].shape, F32)]
            outs = [((send, self.cols), BF16), ((rows, self.cols), BF16)] + outs
            members.append((functools.partial(add_kernel, len(flows), splits, self.block), operands, outs, []))
        results = self.run(*members, vmem=12, after=after, cost=cost)
        made = []
        for (flows, dim, *more), out in zip(steps, results if len(members) > 1 else [results]):
            if flows == "finish":
                made.append(out[0])
                continue
            left = [name for name in more if isinstance(name, str)] + [name for name in flows[0].left if name != dim]
            made.append(Flow(self.place, out[0], out[1], dim, left))
            made += out[2:]
        return made if len(made) > 1 else made[0]


class Flow:
    def __init__(self, place, send, keep, dim, left, where="v"):
        flat = lambda value: value.reshape(-1, value.shape[-1])
        self.keep, self.left, self.place = flat(keep), left, where
        self.got = place.swap(flat(send), dim)


def local(
    tokens, cotangent, lengths, repeats, w_qkv, w_out, w_up, w_down, bias_qv, bias_proj, bias_up, gains, shifts
):
    place = Place()
    chain = Chain()
    rows = 2 * tokens.shape[1]
    bundles = Bundles(place, chain, rows)
    scal = (place.vector, "s")
    dma = pltpu.SemaphoreType.DMA
    wide, tall = (rows, D), (rows, FF)
    part_shape = ((rows // 2, D), BF16)
    weight = {"qkv": (w_qkv, "h"), "out": (w_out, "h"), "up": (w_up, "h"), "down": (w_down, "h")}
    tables = {"qv": (bias_qv, "v"), "proj": (bias_proj, "v"), "up": (bias_up, "v")}
    tables.update(gains=(gains, "v"), shifts=(shifts, "v"))
    swap = place.swap_core
    fast = bundles.fast

    got = place.to_chip(tokens, cotangent)
    low, q, kv = chain.call(
        first_kernel,
        [scal, (lengths, "s"), (repeats, "s"), (got[0], "v"), (got[1], "v"), weight["qkv"], tables["qv"]],
        [(wide, BF16), (wide, BF16), ((rows + 16, 2 * D), BF16)],
        [pltpu.VMEM((D, 3 * D), BF16), dma((1,))],
        16,
    )
    stream, kept = low, []
    for layer in range(LAYERS):
        last = layer == LAYERS - 1
        kv_other = swap(kv)
        operands = [scal, (stream, "v"), (q, "v"), (kv, "v"), (kv_other, "v")]
        operands += [weight["out"], weight["up"], weight["down"]]
        operands += [tables["proj"], tables["up"], tables["gains"], tables["shifts"]]
        far = () if last else ("far",)
        outputs = [((16, rows), F32), (wide, F32, *far), ((rows, 128), F32), (tall, BF16, *far)]
        if fast:
            halves = ((3, D // 2, rows), BF16), ((rows, FF // 2), BF16)
            outputs += [halves[0] + far, halves[0], halves[1] + far, halves[1]]
        else:
            outputs += [((rows, ACTS), BF16)]
        if last:
            operands += [(meta, "v"), (got[0], "v"), (got[1], "v")]
            outputs += [part_shape, part_shape, (wide, BF16), (wide, F32), ((8, D), F32)]
        else:
            operands += [weight["qkv"], tables["qv"]]
            outputs += [(wide, F32, "far"), ((rows, 128), F32), (wide, F32), (wide, BF16), (wide, BF16)]
            outputs += [((rows, 2 * D), BF16), ((8, D), F32)]
        scratch = [pltpu.VMEM((D, D), BF16), pltpu.VMEM((D, FF), BF16), pltpu.VMEM((FF, D), BF16)]
        scratch += [pltpu.VMEM((D, 3 * D), BF16), pltpu.VMEM((D, rows), BF16), pltpu.VMEM((D, 2 * rows), BF16)]
        scratch += [pltpu.VMEM((D, rows), BF16), pltpu.VMEM(wide, F32), dma((4,))]
        if fast:
            scratch += [pltpu.VMEM((rows, ACTS), BF16), pltpu.VMEM((D, rows), BF16), pltpu.VMEM((D, rows), BF16)]
        body = functools.partial(layer_kernel, layer, last, place.chips if fast else 0)
        results = chain.call(body, operands, outputs, scratch, 32)
        lse, hat1, inv1, slope = results[:4]
        values = dict(q=q, kv=kv, kv_other=kv_other, lse=lse, hat1=hat1, inv1=inv1, slope=slope)
        if fast:
            rows_keep, rows_send, cols_keep, cols_send = results[4:8]
            values["halves"] = (rows_keep, swap(rows_send)), (cols_keep, swap(cols_send))
        else:
            values["acts"], values["acts_other"] = results[4], swap(results[4])
        results = results[8 if fast else 5 :]
        if last:
            out0, out1, mixed, grad_two, small_two = results
        else:
            values["hat2"], values["inv2"], stream, low, q, kv, meta = results
        kept.append(values)

    seqs = place.seq_width
    block_shape = ((rows, FF // seqs), BF16)
    swap_all = lambda values: [swap(v) for v in values]

    def up_back_first(layer, mixed):
        *before, small = chain.call(
            functools.partial(up_back_kernel, layer),
            [(mixed, "v"), (kept[layer]["slope"], "v"), weight["down"]],
            [block_shape] * seqs + [((1, FF), F32)],
            [pltpu.VMEM((seqs, FF // seqs, D), BF16), dma((seqs,))],
            16,
        )
        return before, small

    def attention_back(layer, grad_before, grad_two):
        k = kept[layer]
        scratch = [pltpu.VMEM((D, FF), BF16), pltpu.VMEM((D, D), BF16), pltpu.VMEM(wide, BF16)]
        scratch += [pltpu.VMEM((D, rows), BF16), pltpu.VMEM((D, rows), BF16), pltpu.VMEM((D, 2 * rows), BF16)]
        scratch += [pltpu.VMEM((D, rows), BF16), pltpu.VMEM((rows, 2 * D), BF16), dma((2,))]
        operands = [(v, "v") for v in grad_before] + [scal, (meta, "v"), (grad_two, "v")]
        far = "v" if layer == LAYERS - 1 else "far"
        operands += [(k["hat1"], far), (k["inv1"], "v")]
        operands += [(k[name], far) for name in ("q", "kv", "kv_other")] + [(k["lse"], "v")]
        operands += [weight["up"], weight["out"], tables["gains"]]
        outputs = [(wide, F32), (wide, BF16), (wide, BF16), ((rows, 2 * D), F32), ((8, D), F32)]
        outputs += [((rows, 2 * D // SENDS), BF16)] * SENDS
        body = functools.partial(attention_back_kernel, layer, seqs)
        return chain.call(body, operands, outputs, scratch, 20, cost=COSTS[layer])

    def input_back(layer, grad_one, branch, grad_q, dkv, small, *sends, after=()):
        operands = [(swap(v), "v") for v in sends]
        operands += [scal, (grad_q, "v"), (dkv, "v"), (grad_one, "v"), (branch, "v"), weight["qkv"]]
        outputs = [((rows, 4 * D), BF16)]
        scratch = [pltpu.VMEM((D, 3 * D), BF16), pltpu.VMEM((rows, 3 * D), BF16)]
        if layer > 0:
            before = kept[layer - 1]
            operands += [(before["hat2"], "far"), (before["inv2"], "v"), tables["gains"]]
            operands += [(before["slope"], "far"), weight["down"]]
            outputs += [block_shape] * seqs + [((8, D), F32), (wide, BF16), (wide, F32), ((8, D), F32), ((1, FF), F32)]
            scratch += [pltpu.VMEM((seqs, FF // seqs, D), BF16), dma((1,)), dma((seqs,))]
        else:
            outputs += [((8, D), F32), part_shape, part_shape]
            scratch += [dma((1,))]
        body = functools.partial(input_back_kernel, layer, seqs)
        return chain.call(body, operands, outputs, scratch, 20, after)

    z_wide, z_thin = 3 * D // place.seq_width, D // place.seq_width
    plain = [None] * LAYERS

    def plain_sums(layer, mixed, mixed_other, grad_before, before_other, right, right_other):
        k = kept[layer]
        pick = lambda name, at, width: k[name][:, at : at + width]
        split = lambda v: v.reshape(rows, place.seq_width, z_wide + z_thin)
        results = []
        for at, parts in ((LOW, slice(0, z_wide)), (ATT, slice(z_wide, None))):
            rhs = [split(v)[:, :, parts].reshape(rows, -1) for v in (right, right_other)]
            results.append(place.scatter_plain(pick("acts", at, D), pick("acts_other", at, D), *rhs))
        results.append(
            place.scatter_plain(
                pick("acts", NORMED, D),
                pick("acts_other", NORMED, D),
                jnp.concatenate(grad_before, 1),
                jnp.concatenate(before_other, 1),
            )
        )
        results.append(
            place.scatter_plain(pick("acts", ACTIVE, FF), pick("acts_other", ACTIVE, FF), mixed, mixed_other)
        )
        return results

    k1, k0 = kept[1], kept[0]
    halves1, halves0 = (k["halves"] if fast else None for k in (k1, k0))
    mixed1, mixed1_other = mixed, swap(mixed)
    before1, small_up1 = up_back_first(1, mixed1)
    before1_other = swap_all(before1)
    if fast:
        d1, u1 = bundles.make(
            bundles.down("x", halves1, mixed1, mixed1_other),
            bundles.up("y", halves1, before1, before1_other),
            far=True,
        )
    back = attention_back(1, before1, grad_two)
    small_one1 = back[4]
    hidden = place.from_chip(out0, out1)
    right1, *results = input_back(1, *back)
    before0, (small_in1, mixed0, grad_two, small_two0, small_up0) = results[:seqs], results[seqs:]
    mixed0_other = swap(mixed0)
    before0_other = swap_all(before0)
    right1_other = swap(right1)
    if fast:
        d1, u1 = bundles.add(([d1], "y"), ([u1], "x"))
        d0, u0 = bundles.make(
            bundles.down("x", halves0, mixed0, mixed0_other), bundles.up("y", halves0, before0, before0_other)
        )
    else:
        plain[1] = plain_sums(1, mixed1, mixed1_other, before1, before1_other, right1, right1_other)
    back = attention_back(0, before0, grad_two)
    small_one0 = back[4]
    if fast:
        du1 = bundles.add(([d1, u1], "z0", "g"))
        oq1a, oq1b = bundles.make(bundles.oq(("x", "y"), halves1, right1, right1_other))
    right0, small_in0, last0, last1 = input_back(0, *back)
    right0_other = swap(right0)
    grad_tokens = place.from_chip(last0, last1)
    smalls = []
    for group in ((small_in0, small_one0, small_two0, small_up0), (small_in1, small_one1, small_two, small_up1)):
        smalls += [(v, "v") for v in group]
    (table,) = chain.call(pack_kernel, smalls, [((LAYERS * 12, D), F32)], [])
    if fast:
        du1 = bundles.add(([du1], "z1"), after=[hidden])
        d0, u0, table = bundles.add(([d0], "z0"), ([u0], "x", (table, swap(table))), cost=40)
        oq0a, oq0b = bundles.make(bundles.oq(("x", "y"), halves0, right0, right0_other))
        oq1a, oq1b = bundles.add(([oq1a], "y"), ([oq1b], "x"), after=[grad_tokens])
        d0 = bundles.add(([d0], "y"))
        u0_got = u0.got
        u0, du1 = bundles.add(([u0], "z0"), bundles.finish(du1))
        oq0a, table, oq0b = bundles.add(([oq0a], "y", (table, u0_got)), ([oq0b], "x"))
        du0 = bundles.add(([d0, u0], "z1", "g"))
        oq1 = bundles.add(([oq1a, oq1b], "z0", "z1"))
        oq0, table, oq1 = bundles.add(([oq0a, oq0b], "z0", "z1", (table, oq0a.got)), ([oq1], "z1"))
        oq0, table = bundles.add(([oq0], "z1", (table, oq0.got)))
        places = (((1, 2), 0), ((1, 2), 1), ((3, 4), 0)), (((0,), 0), ((0,), 1), ((5, 6), 0))
        pairs = [(v, "v") for v in (du1, du0.keep, du0.got, oq0.keep, oq0.got, oq1.keep, oq1.got, table)]
        block = bundles.block
        shapes = [(block, z_wide), (block, z_thin), (block, bundles.cols), (FF // place.dp_width, z_thin)]
        *stacked, total = chain.call(
            functools.partial(last_kernel, (place.seq_width, block, places, 4)),
            pairs,
            [((LAYERS,) + shape, F32) for shape in shapes] + [(table.shape, F32)],
            [],
        )
    else:
        plain[0] = plain_sums(0, mixed0, mixed0_other, before0, before0_other, right0, right0_other)
        total = place.all_sum(table)
        stacked = [jnp.stack([plain[layer][k] for layer in range(LAYERS)]) for k in range(4)]
    total = total.reshape(LAYERS, 12, D)
    return (
        hidden,
        grad_tokens,
        *stacked,
        total[:, 0:2],
        total[:, 2:4],
        total[:, 8:12].reshape(LAYERS, FF),
        total[:, 4:6],
        total[:, 6:8],
    )


def solution(mesh):
    rows = P("dp", "seq", None)
    blocks = P(None, "dp", "seq")
    return jax.shard_map(
        local,
        mesh=mesh,
        in_specs=(rows, rows, P("dp"), P("dp")) + (P(),) * 9,
        out_specs=(rows, rows) + (blocks,) * 4 + (P(),) * 5,
        check_vma=False,
    )
```

```python
import functools
import math

import jax
import jax.numpy as jnp
from jax import lax
from jax.experimental import pallas as pl
from jax.experimental.pallas import tpu as pltpu
from jax.sharding import PartitionSpec as P

D = 768
FF = 3072
HEADS = 12
HEAD = 64
PAIR = 2 * HEAD
LAYERS = 2
EPS = 1e-05
MASKED = -1000000000.0
SCALE = 1.0 / HEAD**0.5
F32 = jnp.float32
BF16 = jnp.bfloat16
FF_STEP = 1024
ERFCX_POINT = 0.48
ERFCX = (
    0.270751081,
    0.27211497,
    0.227394229,
    0.241744859,
    -0.115868816,
    0.444806334,
    -0.579913037,
    0.294191549,
    -0.05522118,
)
ACTIVE, NORMED, ATT, LOW = 0, FF, FF + D, FF + 2 * D
ACTS = FF + 3 * D
CORE, LOW_Z, CHIP, OWN_SEQ, Z = range(5)
DIMS = {"x": (CHIP, 0), "y": (CHIP, 1), "z0": (Z, 0), "z1": (Z, 1)}
COSTS = {2: 6, 9: 90, 14: 40}
HIDDEN_AT, GRAD_AT = 13, 16
OQ0_FIRST, OQ1_FIRST, D0_FAR, D1_FAR = True, True, False, False
DU1_FIRST, DU1_EARLY, RIGHT_PIECES = False, False, 1
TAIL = 32
SENDS = 3


class Place:
    def __init__(self):
        self.dp_width = lax.axis_size("dp")
        self.seq_width = lax.axis_size("seq")
        self.dp = lax.axis_index("dp")
        self.z = lax.axis_index("seq")
        self.core = self.dp % 2
        self.chips = self.dp_width // 2
        self.dp_bits = self.dp_width.bit_length() - 2
        self.seq_bits = self.seq_width.bit_length() - 1
        own_seq = (self.core == self.z // 2).astype(jnp.int32)
        self.vector = jnp.stack([self.core, self.z % 2, self.dp // 2, own_seq, self.z]).astype(jnp.int32)

    def swap_dp(self, value, bit):
        pairs = [(i, i ^ (1 << bit)) for i in range(self.dp_width)]
        return lax.ppermute(value, "dp", pairs)

    def swap(self, value, dim):
        if dim == "core":
            return self.swap_core(value)
        entry, bit = DIMS[dim]
        return self.swap_seq(value, bit) if entry == Z else self.swap_dp(value, bit + 1)

    def swap_core(self, value):
        return self.swap_dp(value, 0)

    def swap_seq(self, value, bit):
        pairs = [(i, i ^ (1 << bit)) for i in range(self.seq_width)]
        return lax.ppermute(value, "seq", pairs)

    def spread_pairs(self, flip, back):
        pairs = []
        for dp in range(self.dp_width):
            chip, core = dp // 2, dp % 2
            for z in range(self.seq_width):
                s = (z % 2) ^ flip
                src = dp * self.seq_width + z
                dst = (2 * chip + z // 2) * self.seq_width + 2 * core + s
                pairs.append((dst, src) if back else (src, dst))
        return pairs

    def to_chip(self, value):
        low = self.z % 2
        pick = lambda at: lax.dynamic_index_in_dim(value, at, 0, keepdims=False)
        first, second = pick(low), pick(1 - low)
        got0 = lax.ppermute(first, ("dp", "seq"), self.spread_pairs(0, False))
        got1 = lax.ppermute(second, ("dp", "seq"), self.spread_pairs(1, False))
        return got0, got1

    def from_chip(self, first, second):
        got0 = lax.ppermute(first, ("dp", "seq"), self.spread_pairs(0, True))
        got1 = lax.ppermute(second, ("dp", "seq"), self.spread_pairs(1, True))
        even = self.z % 2 == 0
        return jnp.stack([jnp.where(even, got0, got1), jnp.where(even, got1, got0)], 0).astype(F32)

    def all_sum(self, value):
        value = value + self.swap_core(value)
        for bit in range(1, self.dp_bits + 1):
            value = value + self.swap_dp(value, bit)
        for bit in range(self.seq_bits):
            value = value + self.swap_seq(value, bit)
        return value

    def halve(self, blocks, axis, mine, swap):
        keep = lax.dynamic_index_in_dim(blocks, mine, axis, keepdims=False)
        send = lax.dynamic_index_in_dim(blocks, 1 - mine, axis, keepdims=False)
        got = swap(send)
        return (keep.astype(F32) + got.astype(F32)).astype(BF16)

    def scatter_plain(self, lhs, lhs_other, rhs, rhs_other):
        rows, m = lhs.shape
        cols = rhs.shape[1]
        block = m // self.dp_width
        both = jnp.concatenate([lhs, lhs_other], 0).reshape(2 * rows, self.chips, 2, block)
        half = lax.dynamic_index_in_dim(both, self.core, 2, keepdims=False).reshape(2 * rows, m // 2)
        right = jnp.concatenate([rhs, rhs_other], 0)
        grad = lax.dot_general(half, right, (((0,), (0,)), ((), ())), preferred_element_type=F32).astype(BF16)
        blocks = grad.reshape((2,) * self.dp_bits + (block, cols))
        for bit in range(self.dp_bits, 0, -1):
            mine = (self.dp >> bit) % 2
            blocks = self.halve(blocks, 0, mine, functools.partial(self.swap_dp, bit=bit))
        blocks = blocks.reshape(block, self.seq_width, cols // self.seq_width).transpose(1, 0, 2)
        blocks = blocks.reshape((2,) * self.seq_bits + (block, cols // self.seq_width))
        for bit in range(self.seq_bits - 1, -1, -1):
            mine = (self.z >> bit) % 2
            blocks = self.halve(blocks, 0, mine, functools.partial(self.swap_seq, bit=bit))
        return blocks.astype(F32)


class Chain:
    def __init__(self):
        self.last = None
        self.count = 0
        self.early = {}

    def call(self, body, operands, outputs, scratch, vmem=12, after=()):
        cost = COSTS.get(self.count, 0)
        after = [*after, *self.early.get(self.count, ())]
        self.count += 1
        spaces = {"v": pltpu.VMEM, "h": pltpu.HBM, "s": pltpu.SMEM, "far": pltpu.VMEM}
        count = len(operands)
        arrays = [pltpu.with_memory_space_constraint(a, pltpu.HBM) if p in ("h", "far") else a for a, p in operands]
        specs = [pl.BlockSpec(memory_space=spaces[p]) for _, p in operands]
        ahead = list(after) + ([] if self.last is None else [self.last])
        arrays += ahead
        specs += [pl.BlockSpec(memory_space=pl.ANY)] * len(ahead)

        inputs = count + len(ahead)

        def inner(*refs):
            refs[inputs + len(outputs)][...] = jnp.zeros((8, 128), F32)
            return body(*refs[:count], *refs[inputs : inputs + len(outputs)], *refs[inputs + len(outputs) + 1 :])

        shapes = [pltpu.HBM(s, d) if far else jax.ShapeDtypeStruct(s, d) for s, d, *far in outputs]
        results = pl.pallas_call(
            inner,
            out_shape=shapes + [jax.ShapeDtypeStruct((8, 128), F32)],
            in_specs=specs,
            out_specs=[pl.BlockSpec(memory_space=pltpu.VMEM) for _ in range(len(outputs) + 1)],
            scratch_shapes=scratch,
            compiler_params=pltpu.CompilerParams(vmem_limit_bytes=vmem << 20),
            cost_estimate=pl.CostEstimate(flops=1024 + cost * 10**9, bytes_accessed=1024, transcendentals=0),
        )(*arrays)
        *results, self.last = results
        return results


def dot(left, right):
    return jnp.dot(left, right, preferred_element_type=F32)


def dot_back(left, right):
    return lax.dot_general(left, right, (((1,), (1,)), ((), ())), preferred_element_type=F32)


def norm_parts(summed):
    average = jnp.mean(summed, -1, keepdims=True)
    centered = summed - average
    variance = jnp.mean(centered * centered, -1, keepdims=True)
    inverse = lax.rsqrt(variance + EPS)
    return centered * inverse, inverse


def norm_back(grad, hat, inverse, gain_row):
    scaled = grad * gain_row
    mean_one = jnp.mean(scaled, -1, keepdims=True)
    mean_hat = jnp.mean(scaled * hat, -1, keepdims=True)
    out = (scaled - mean_one - hat * mean_hat) * inverse
    return out, jnp.sum(grad * hat, 0, keepdims=True), jnp.sum(grad, 0, keepdims=True)


def gelu_parts(before):
    size = jnp.abs(before) * (0.5**0.5)
    spread = jnp.exp(-0.5 * before * before)
    t = 1.0 / (1.0 + ERFCX_POINT * size)
    poly = jnp.full_like(t, ERFCX[-1])
    for factor in ERFCX[-2::-1]:
        poly = poly * t + factor
    tail = 0.5 * (poly * t) * spread
    cdf = jnp.where(before >= 0.0, 1.0 - tail, tail)
    return before * cdf, cdf + before * (spread * 0.3989422804014327)


def load(pairs, sems):
    copies = [pltpu.make_async_copy(src, dst, sems.at[k]) for k, (src, dst) in enumerate(pairs)]
    for copy in copies:
        copy.start()
    return copies


def row(ref, *index):
    return ref[index[:-1] + (pl.ds(index[-1], 1), slice(None))].astype(F32)


def key_masks(scal, length_row, rows):
    spot = lax.broadcasted_iota(jnp.int32, (rows, rows), 0)
    own = (spot + scal[CORE] * rows).astype(F32) < length_row
    other = (spot + (1 - scal[CORE]) * rows).astype(F32) < length_row
    return own, other


def head_lanes(value, h, axis):
    spot = lax.broadcasted_iota(jnp.int32, value.shape, axis) // HEAD
    return jnp.where(spot == h, value, jnp.zeros_like(value))


def join(flag, first, second, out):
    half = first.shape[0]

    @pl.when(flag == 0)
    def _():
        out[0:half] = first[...].astype(out.dtype)
        out[half : 2 * half] = second[...].astype(out.dtype)

    @pl.when(flag != 0)
    def _():
        out[0:half] = second[...].astype(out.dtype)
        out[half : 2 * half] = first[...].astype(out.dtype)


def part(flag, value, first, second):
    half = first.shape[0]

    @pl.when(flag == 0)
    def _():
        first[...] = value[0:half]
        second[...] = value[half : 2 * half]

    @pl.when(flag != 0)
    def _():
        first[...] = value[half : 2 * half]
        second[...] = value[0:half]


def project(layer, low, w, bias_qv, q, kv):
    rows = low.shape[0]
    kv[0:rows, :D] = dot(low[...], w[:, D : 2 * D]).astype(BF16)
    kv[0:rows, D:] = (dot(low[...], w[:, 2 * D :]) + row(bias_qv, layer, 1)).astype(BF16)
    full = (dot(low[...], w[:, :D]) + row(bias_qv, layer, 0)).astype(BF16)
    q[...] = full * jnp.asarray(SCALE, BF16)


def first_kernel(scal, lengths, repeats, got0, got1, w_qkv, bias_qv, low, q, kv, w, sems):
    (copy,) = load([(w_qkv.at[0], w)], sems)
    join(scal[LOW_Z], got0, got1, low)
    rows = low.shape[0]
    spot = lax.broadcasted_iota(jnp.int32, (16, 2 * D), 0)
    facts = [lengths[0] // 16, lengths[0] % 16, lengths[1] // 16, lengths[1] % 16, repeats[0], repeats[1]]
    table = jnp.zeros((16, 2 * D), F32)
    for k, fact in enumerate(facts):
        table = jnp.where(spot == k, fact.astype(F32), table)
    kv[rows : rows + 16] = table.astype(BF16)
    copy.wait()
    project(0, low, w, bias_qv, q, kv)


def core_halves(core, chips, acts, turned, rows_keep, rows_send, cols_keep, cols_send):
    for which, rows_out, cols_out in ((core, rows_keep, cols_keep), (1 - core, rows_send, cols_send)):
        for k, source in enumerate(turned):
            block = D // (2 * chips)
            for chip in range(chips):
                at = pl.multiple_of((chip * 2 + which) * block, block)
                rows_out[k, chip * block : (chip + 1) * block] = source[pl.ds(at, block), :]
        width = FF // (2 * chips)
        for chip in range(chips):
            at = pl.multiple_of((chip * 2 + which) * width, width)
            cols_out[:, chip * width : (chip + 1) * width] = acts[:, pl.ds(at, width)]


def layer_kernel(layer, last, chips, *refs):
    (scal, x, q, kv_own, kv_other, w_out, w_up, w_down) = refs[:8]
    (bias_proj, bias_up, gains, shifts) = refs[8:12]
    refs = refs[12:]
    if last:
        meta, refs = refs[0], refs[1:]
    else:
        (w_qkv, bias_qv) = refs[:2]
        refs = refs[2:]
    (lse, hat1, inv1, slope, ot) = refs[:5]
    refs = refs[5:]
    if chips:
        halves, refs = refs[:4], refs[4:]
    else:
        acts, refs = refs[0], refs[1:]
    hat2, inv2, refs = refs[0], refs[1], refs[2:]
    if last:
        out0, out1 = refs[:2]
        refs = refs[2:]
    else:
        out, low, q_next, kv_next, meta = refs[:5]
        refs = refs[5:]
    (wo, wu, wd, w, qt, vt, acc, sems) = refs[:8]
    rows = q.shape[0]
    if chips:
        acts, normed_t, low_t = refs[8:]
    moves = [(w_out.at[layer], wo), (w_up.at[layer], wu), (w_down.at[layer], wd)]
    if not last:
        moves.append((w_qkv.at[layer + 1], w))
        here = scal[OWN_SEQ] == 1
        facts = jnp.where(here, kv_own[rows:, :D].astype(F32), kv_other[rows:, :D].astype(F32))
        first = scal[LOW_Z] == 0
        meta[0:1] = jnp.where(first, facts[0:1] * 16.0 + facts[1:2], facts[2:3] * 16.0 + facts[3:4])
        meta[1:2] = jnp.where(first, facts[4:5], facts[5:6])
    copies = load(moves, sems)
    acts[:, LOW : LOW + D] = x[...].astype(BF16)
    qt[...] = q[...].T
    vt[:, 0:rows] = kv_own[0:rows, D:].T
    vt[:, rows : 2 * rows] = kv_other[0:rows, D:].T
    valid_own, valid_other = key_masks(scal, meta[0:1, 0:rows], rows)

    def pair(k, carry):
        lanes = pl.ds(pl.multiple_of(k * PAIR, PAIR), PAIR)
        keys_own, keys_other = kv_own[0:rows, lanes], kv_other[0:rows, lanes]
        q_pair = qt[lanes, :]
        for h in range(2):
            q_head = head_lanes(q_pair, h, 0)
            s_own = jnp.where(valid_own, dot(keys_own, q_head), MASKED)
            s_other = jnp.where(valid_other, dot(keys_other, q_head), MASKED)
            top = jnp.maximum(jnp.max(s_own, 0, keepdims=True), jnp.max(s_other, 0, keepdims=True))
            p_own = jnp.exp(s_own - top)
            p_other = jnp.exp(s_other - top)
            total = jnp.sum(p_own, 0, keepdims=True) + jnp.sum(p_other, 0, keepdims=True)
            head = pl.ds(pl.multiple_of(k * PAIR + h * HEAD, HEAD), HEAD)
            o = dot(vt[head, 0:rows], p_own.astype(BF16)) + dot(vt[head, rows : 2 * rows], p_other.astype(BF16))
            ot[head, :] = (o * (1.0 / total)).astype(BF16)
            lse[pl.ds(2 * k + h, 1), :] = top + jnp.log(total)
        return carry

    lax.fori_loop(0, HEADS // 2, pair, 0)
    acts[:, ATT : ATT + D] = ot[...].T
    copies[0].wait()
    h1, i1 = norm_parts(x[...].astype(F32) + (dot(acts[:, ATT : ATT + D], wo[...]) + row(bias_proj, layer, 0)))
    hat1[...] = h1
    inv1[...] = jnp.broadcast_to(i1, inv1.shape)
    normed = h1 * row(gains, layer, 0) + row(shifts, layer, 0)
    acts[:, NORMED : NORMED + D] = normed.astype(BF16)
    acc[...] = normed + row(bias_proj, layer, 1)
    copies[1].wait()
    copies[2].wait()
    for k in range(FF // FF_STEP):
        cols = slice(k * FF_STEP, (k + 1) * FF_STEP)
        before = dot(acts[:, NORMED : NORMED + D], wu[:, cols]) + bias_up[pl.ds(layer, 1), cols].astype(F32)
        value, steep = gelu_parts(before)
        value = value.astype(BF16)
        acts[:, cols] = value
        slope[:, cols] = steep.astype(BF16)
        acc[...] += dot(value, wd[cols, :])
    if chips:
        low_t[...] = acts[:, LOW : LOW + D].T
        normed_t[...] = acts[:, NORMED : NORMED + D].T
        core_halves(scal[CORE], chips, acts, (normed_t, ot, low_t), *halves)
    h2, i2 = norm_parts(acc[...])
    stream = h2 * row(gains, layer, 1) + row(shifts, layer, 1)
    hat2[...] = h2
    inv2[...] = jnp.broadcast_to(i2, inv2.shape)
    if not last:
        out[...] = stream
        low[...] = stream.astype(BF16)
        copies[3].wait()
        project(layer + 1, low, w, bias_qv, q_next, kv_next)
        return
    part(scal[LOW_Z], stream.astype(BF16), out0, out1)


def second_back(layer, grad, hat, inverse, gains, mixed, grad_two, small):
    two, gain_two, shift_two = norm_back(grad, hat, inverse, row(gains, layer, 1))
    grad_two[...] = two
    mixed[...] = two.astype(BF16)
    small[0:1] = jnp.sum(mixed[...].astype(F32), 0, keepdims=True)
    small[1:2] = gain_two
    small[2:3] = shift_two


def load_down(layer, w_down, wd, sems):
    step = wd.shape[1]
    return load([(w_down.at[layer, pl.ds(k * step, step)], wd.at[k]) for k in range(wd.shape[0])], sems)


def up_back(copies, mixed, slope, grad_before, bias_up_grad, wd):
    step = wd.shape[1]
    for k, out in enumerate(grad_before):
        copies[k].wait()
        cols = slice(k * step, (k + 1) * step)
        value = (dot_back(mixed[...], wd[k]) * slope[:, cols].astype(F32)).astype(BF16)
        out[...] = value
        bias_up_grad[:, cols] = jnp.sum(value.astype(F32), 0, keepdims=True)


def turn_kernel(layer, scal, meta, cot0, cot1, hat2, inv2, gains, slope, w_down, *refs):
    grad_before, (bias_up_grad, mixed, grad_two, small, wd, grad, sems) = refs[:-7], refs[-7:]
    copies = load_down(layer, w_down, wd, sems)
    join(scal[LOW_Z], cot0, cot1, grad)
    rows = grad.shape[0]
    spot = lax.broadcasted_iota(jnp.int32, (rows, D), 0) + scal[CORE] * rows
    scaled = grad[...] * jnp.where(spot.astype(F32) < meta[0:1], meta[1:2], 0.0)
    second_back(layer, scaled, hat2[...], inv2[:, 0:1], gains, mixed, grad_two, small)
    up_back(copies, mixed, slope, grad_before, bias_up_grad, wd)


def attention_back_kernel(layer, blocks, *refs):
    grad_before, refs = refs[:blocks], refs[blocks:]
    (scal, meta, grad_two, hat1, inv1, q, kv_own, kv_other, lse, att_t, w_up, w_out, gains) = refs[:13]
    (grad_one, branch, grad_q, dkv_own, small) = refs[13:18]
    sends, (wu, wo, datt, qt, dot_t, kt, dqt, dkv_other, sems) = refs[18:-9], refs[-9:]
    rows = q.shape[0]
    copies = load([(w_up.at[layer], wu), (w_out.at[layer], wo)], sems)
    qt[...] = q[...].T
    kt[:, 0:rows] = kv_own[0:rows, :D].T
    kt[:, rows : 2 * rows] = kv_other[0:rows, :D].T
    copies[0].wait()
    grad_normed = grad_two[...]
    for k, before in enumerate(grad_before):
        width = before.shape[1]
        grad_normed += dot_back(before[...], wu[:, k * width : (k + 1) * width])
    one, gain_one, shift_one = norm_back(grad_normed, hat1[...], inv1[:, 0:1], row(gains, layer, 0))
    grad_one[...] = one
    branch[...] = one.astype(BF16)
    small[0:1] = jnp.sum(branch[...].astype(F32), 0, keepdims=True)
    small[1:2] = gain_one
    small[2:3] = shift_one
    copies[1].wait()
    datt[...] = dot_back(branch[...], wo[...]).astype(BF16)
    dot_t[...] = datt[...].T
    valid_own, valid_other = key_masks(scal, meta[0:1, 0:rows], rows)

    def pair(k, carry):
        lanes = pl.ds(pl.multiple_of(k * PAIR, PAIR), PAIR)
        v_lanes = pl.ds(pl.multiple_of(D + k * PAIR, PAIR), PAIR)
        keys_own, keys_other = kv_own[0:rows, lanes], kv_other[0:rows, lanes]
        vals_own, vals_other = kv_own[0:rows, v_lanes], kv_other[0:rows, v_lanes]
        sums = None
        for h in range(2):
            qt_head = head_lanes(qt[lanes, :], h, 0)
            dt_head = head_lanes(dot_t[lanes, :], h, 0)
            q_head = head_lanes(q[:, lanes], h, 1)
            d_head = head_lanes(datt[:, lanes], h, 1)
            log_total = lse[pl.ds(2 * k + h, 1), :]
            head = pl.ds(pl.multiple_of(k * PAIR + h * HEAD, HEAD), HEAD)
            delta = jnp.sum(dot_t[head, :].astype(F32) * att_t[head, :].astype(F32), 0, keepdims=True)
            dq = None
            parts = []
            for at, keys, vals, valid in ((0, keys_own, vals_own, valid_own), (rows, keys_other, vals_other, valid_other)):
                p = jnp.exp(jnp.where(valid, dot(keys, qt_head), MASKED) - log_total)
                ds = (p * (dot(vals, dt_head) - delta)).astype(BF16)
                more = dot(kt[head, at : at + rows], ds)
                dq = more if dq is None else dq + more
                parts += [dot(ds, q_head), dot(p.astype(BF16), d_head)]
            dqt[head, :] = (dq * SCALE).astype(BF16)
            parts = (parts[0], parts[2], parts[1], parts[3])
            sums = parts if sums is None else tuple(a + b for a, b in zip(sums, parts))
        dkv_own[:, lanes] = sums[0]
        dkv_other[:, lanes] = sums[1].astype(BF16)
        dkv_own[:, v_lanes] = sums[2]
        dkv_other[:, v_lanes] = sums[3].astype(BF16)
        return carry

    lax.fori_loop(0, HEADS // 2, pair, 0, unroll=2)
    grad_q[...] = dqt[...].T
    for k, send in enumerate(sends):
        width = send.shape[1]
        send[...] = dkv_other[:, k * width : (k + 1) * width]


def input_back_kernel(layer, seq_width, *refs):
    got, refs = refs[:SENDS], refs[SENDS:]
    (scal, grad_q, dkv_own, grad_one, branch, w_qkv) = refs[:6]
    refs = refs[6:]
    if layer > 0:
        hat2, inv2, gains, slope, w_down = refs[:5]
        refs = refs[5:]
    pieces = 1 if layer > 0 else RIGHT_PIECES
    rights, refs = refs[:pieces], refs[pieces:]
    if layer > 0:
        grad_before, refs = refs[:seq_width], refs[seq_width:]
        small_in, mixed, grad_two, small, bias_up_grad, w, packed, wd, sems, down_sems = refs
    else:
        small_in, out0, out1, w, packed, sems = refs
    (copy,) = load([(w_qkv.at[layer], w)], sems)
    if layer > 0:
        down_copies = load_down(layer - 1, w_down, wd, down_sems)
    packed[:, :D] = grad_q[...]
    for k, part_got in enumerate(got):
        width = part_got.shape[1]
        cols = slice(k * width, (k + 1) * width)
        packed[:, D + k * width : D + (k + 1) * width] = (dkv_own[:, cols] + part_got[...].astype(F32)).astype(BF16)
    small_in[0:1] = jnp.sum(packed[:, :D].astype(F32), 0, keepdims=True)
    small_in[1:2] = jnp.sum(packed[:, 2 * D :].astype(F32), 0, keepdims=True)
    wide, thin = 3 * D // seq_width, D // seq_width
    for z in range(seq_width):
        right = rights[z if pieces > 1 else 0]
        at = 0 if pieces > 1 else z * (wide + thin)
        right[:, at : at + wide] = packed[:, z * wide : (z + 1) * wide]
        right[:, at + wide : at + wide + thin] = branch[:, z * thin : (z + 1) * thin]
    copy.wait()
    grad = grad_one[...] + dot_back(packed[...], w[...])
    if layer > 0:
        second_back(layer - 1, grad, hat2[...], inv2[:, 0:1], gains, mixed, grad_two, small)
        up_back(down_copies, mixed, slope, grad_before, bias_up_grad, wd)
    else:
        part(scal[LOW_Z], grad.astype(BF16), out0, out1)


def spread_bit(i, bit, value):
    return ((i >> bit) << (bit + 1)) | (value << bit) | (i & ((1 << bit) - 1))


def chip_order(first, scal, chips):
    if first == "z0":
        return list(range(chips))
    bit = DIMS[first][1]
    mine = (scal[CHIP] >> bit) & 1
    return [spread_bit(i, bit, v) for v in (1 - mine, mine) for i in range(chips // 2)]


def pick_rows(source, order, block, out):
    for i, chip in enumerate(order):
        at = pl.multiple_of(chip * block, block)
        out[i * block : (i + 1) * block, :] = source[pl.ds(at, block), :]


def put(first, scal, chips, z, parts, block, send, keep):
    def store(dst, at, rows):
        for value, lanes in parts:
            dst[at[0], at[1], :, lanes] = value[rows]

    spots = [slice(i * block, (i + 1) * block) for i in range(chips)]
    if first != "z0":
        half = chips // 2
        for i in range(chips):
            store(send if i < half else keep, (i % half, z), spots[i])
        return

    @pl.when(scal[LOW_Z] == z % 2)
    def _():
        for i in range(chips):
            store(keep, (i, z // 2), spots[i])

    @pl.when(scal[LOW_Z] != z % 2)
    def _():
        for i in range(chips):
            store(send, (i, z // 2), spots[i])


def down_kernel(plan, scal, cols, cols_other, mixed, mixed_other, send, keep, turned):
    first, chips, seq_width, block = plan
    rows = mixed.shape[0]
    turned[:, 0:rows] = mixed[...].T
    turned[:, rows : 2 * rows] = mixed_other[...].T
    width = FF // (2 * chips)
    half = chips // 2
    for i, chip in enumerate(chip_order(first, scal, chips)):
        lanes = pl.ds(pl.multiple_of(chip * width, width), width)
        out = dot(turned[:, 0:rows], cols[:, lanes]) + dot(turned[:, rows:], cols_other[:, lanes])
        out = out.astype(BF16)
        dst = send if i < half else keep
        for z in range(seq_width):
            for h in range(2):
                at = (2 * z + h) * block
                dst[i % half, z, :, h * width : (h + 1) * width] = out[at : at + block]


def up_kernel(plan, scal, lhs, lhs_other, *refs):
    first, chips, seq_width, block = plan
    right, right_other, refs = refs[:seq_width], refs[seq_width : 2 * seq_width], refs[2 * seq_width :]
    send, keep, own, other = refs
    order = chip_order(first, scal, chips)
    pick_rows(lhs.at[0], order, block, own)
    pick_rows(lhs_other.at[0], order, block, other)
    for z in range(seq_width):
        out = dot(own[...], right[z][...]) + dot(other[...], right_other[z][...])
        put(first, scal, chips, z, [(out.astype(BF16), slice(None))], block, send, keep)


def oq_kernel(plan, pieces, scal, lhs, lhs_other, *refs):
    firsts, chips, seq_width, block = plan
    rights, others, refs = refs[:pieces], refs[pieces : 2 * pieces], refs[2 * pieces :]
    outs, (low_own, low_other, att_own, att_other) = refs[: 2 * len(firsts)], refs[2 * len(firsts) :]
    wide, width = 3 * D // seq_width, FF // seq_width
    count = seq_width // len(firsts)
    for k, first in enumerate(firsts):
        order = chip_order(first, scal, chips)
        for at, source, own in ((2, lhs, low_own), (2, lhs_other, low_other), (1, lhs, att_own), (1, lhs_other, att_other)):
            pick_rows(source.at[at], order, block, own.at[k])
        for z in range(count):
            spot = k * count + z
            right, right_other = (v[spot if pieces > 1 else 0] for v in (rights, others))
            at = 0 if pieces > 1 else spot * width
            q_cols, o_cols = slice(at, at + wide), slice(at + wide, at + width)
            q_part = dot(low_own[k], right[:, q_cols]) + dot(low_other[k], right_other[:, q_cols])
            o_part = dot(att_own[k], right[:, o_cols]) + dot(att_other[k], right_other[:, o_cols])
            parts = [(q_part.astype(BF16), slice(0, wide)), (o_part.astype(BF16), slice(wide, None))]
            put(first, scal, chips, z, parts, block, outs[2 * k], outs[2 * k + 1])


def tail_sum(table, got):
    if got.dtype == F32:
        return table[...] + got[...]
    count = table.shape[0]
    rows = got.shape[0]
    return table[...].astype(BF16).astype(F32) + got[rows - TAIL : rows, :][0:count].astype(F32)


def add_kernel(groups, splits, block, scal, *refs):
    keeps, gots = refs[0 : 2 * groups : 2], refs[1 : 2 * groups : 2]
    refs = refs[2 * groups :]
    if len(refs) > 2:
        table, table_got, send, keep, table_out = refs
        table_out[...] = tail_sum(table, table_got)
        send[send.shape[0] - TAIL :, :] = jnp.zeros((TAIL, send.shape[1]), BF16)
        send[send.shape[0] - TAIL : send.shape[0] - TAIL + table.shape[0], :] = table_out[...].astype(BF16)
    else:
        send, keep = refs
    at = 0
    for got, kept, (bit, entry, shift) in zip(gots, keeps, splits):
        count = kept.shape[0] // block
        mine = (scal[entry] >> shift) & 1
        for i in range(count // 2):
            for dst, v in ((send, 1 - mine), (keep, mine)):
                src = pl.ds(pl.multiple_of(spread_bit(i, bit, v) * block, block), block)
                dst[at * block : (at + 1) * block] = (kept[src].astype(F32) + got[src].astype(F32)).astype(BF16)
            at += 1


def pack_kernel(*refs):
    out = refs[-1]
    for layer in range(LAYERS):
        first, one, two, up = refs[4 * layer : 4 * layer + 4]
        at = 12 * layer
        out[at : at + 2] = first[0:2]
        for k in range(3):
            out[at + 2 + 2 * k : at + 3 + 2 * k] = one[k : k + 1]
            out[at + 3 + 2 * k : at + 4 + 2 * k] = two[k : k + 1]
        for k in range(FF // D):
            out[at + 8 + k : at + 9 + k] = up[:, k * D : (k + 1) * D]


def finish_kernel(scal, one, two, out):
    out[...] = (one[...].astype(F32) + two[...].astype(F32)).astype(out.dtype)


def last_kernel(plan, *refs):
    seq_width, block, places, tail = plan
    table, grad_qkv, grad_out, grad_up, grad_down, bias_qv, bias_proj, bias_up, gains, shifts = refs[-10:]
    total = tail_sum(table, refs[tail])
    for layer in range(LAYERS):
        at = 12 * layer
        for k, out in enumerate((bias_qv, bias_proj, gains, shifts)):
            out[layer] = total[at + 2 * k : at + 2 * k + 2]
        for k in range(FF // D):
            bias_up[layer : layer + 1, k * D : (k + 1) * D] = total[at + 8 + k : at + 9 + k]
    wide = 3 * D // seq_width
    for layer in range(LAYERS):
        sums = []
        for flow, at in places[layer]:
            rows = slice(at * block, (at + 1) * block)
            sums.append(sum(refs[k][rows].astype(F32) for k in flow))
        down, up, oq = sums
        width = down.shape[1] // 2
        grad_down[layer, 0:block] = down[:, :width]
        grad_down[layer, block : 2 * block] = down[:, width:]
        grad_up[layer] = up
        grad_qkv[layer] = oq[:, :wide]
        grad_out[layer] = oq[:, wide:]


class Bundles:
    def __init__(self, place, chain, rows):
        self.place, self.chain, self.rows = place, chain, rows
        self.block = D // place.dp_width
        self.fast = place.chips == 4 and place.seq_width == 4 and self.block % 16 == 0
        self.cols = FF // place.seq_width

    def shape(self, *lead):
        return lead + (self.block, self.cols), BF16

    def run(self, *members, vmem=14, after=()):
        operands, outputs, scratch = [], [], []
        for _, own, out, temp in members:
            operands += [a if isinstance(a, tuple) else (a, "v") for a in own]
            outputs += out
            scratch += [pltpu.VMEM(shape, BF16) for shape in temp]

        def body(scal, *refs):
            ins, outs, temps = refs[: len(operands)], refs[len(operands) :][: len(outputs)], refs[len(operands) :]
            temps = temps[len(outputs) :]
            for member, own, out, temp in members:
                member(scal, *ins[: len(own)], *outs[: len(out)], *temps[: len(temp)])
                ins, outs, temps = ins[len(own) :], outs[len(out) :], temps[len(temp) :]

        results = self.chain.call(body, [(self.place.vector, "s")] + operands, outputs, scratch, vmem, after)
        parts = []
        for _, _, out, _ in members:
            parts.append(results[: len(out)])
            results = results[len(out) :]
        return parts if len(members) > 1 else parts[0]

    def first(self, first, count):
        chips, seqs = self.place.chips, count
        if first == "z0":
            return self.shape(chips, seqs // 2), ["y", "x", "z1"][: 2 + (seqs > 2)]
        left = ["x" if first == "y" else "y"] + ["z1", "z0"][-1 if seqs == 2 else 0 :]
        return self.shape(chips // 2, seqs), left

    def down(self, first, halves, mixed, mixed_other):
        plan = (first, self.place.chips, self.place.seq_width, self.block)
        out, left = self.first(first, self.place.seq_width)
        operands = [*halves[1], mixed, mixed_other]
        member = functools.partial(down_kernel, plan), operands, [out] * 2, [(D, 2 * self.rows)]
        return member, [(first, left)]

    def up(self, first, halves, right, right_other):
        plan = (first, self.place.chips, self.place.seq_width, self.block)
        out, left = self.first(first, self.place.seq_width)
        operands = [(v, "far") for v in halves[0]] + [*right, *right_other]
        scratch = [(D // 2, self.rows)] * 2
        return (functools.partial(up_kernel, plan), operands, [out] * 2, scratch), [(first, left)]

    def oq(self, firsts, halves, right, right_other):
        plan = (firsts, self.place.chips, self.place.seq_width, self.block)
        kinds = [self.first(first, self.place.seq_width // len(firsts)) for first in firsts]
        outs = [out for out, _ in kinds for _ in range(2)]
        operands = [(v, "far") for v in (*halves[0], *right, *right_other)]
        scratch = [(len(firsts), D // 2, self.rows)] * 4
        member = functools.partial(oq_kernel, plan, len(right)), operands, outs, scratch
        return member, [(first, left) for first, (_, left) in zip(firsts, kinds)]

    def make(self, *members, far=False):
        where = ("far",) if far else ()
        calls = [(body, ins, [out + where for out in outs], temps) for (body, ins, outs, temps), _ in members]
        results = self.run(*calls)
        flows = []
        for (_, kinds), out in zip(members, results if len(members) > 1 else [results]):
            for k, (first, left) in enumerate(kinds):
                flows.append(Flow(self.place, out[2 * k], out[2 * k + 1], first, left, *where))
        return flows

    def finish(self, flow):
        return "finish", flow

    def add(self, *steps, after=()):
        members = []
        for flows, dim, *more in steps:
            if flows == "finish":
                members.append((finish_kernel, [dim.keep, dim.got], [(dim.keep.shape, BF16)], []))
                continue
            operands = [(v, flow.place) for flow in flows for v in (flow.keep, flow.got)]
            splits = [(len(flow.left) - 1 - flow.left.index(dim), *DIMS[dim]) for flow in flows]
            rows = sum(flow.keep.shape[0] for flow in flows) // 2
            send, outs = rows, []
            if more and isinstance(more[-1], tuple):
                operands += more[-1]
                send, outs = rows + TAIL, [(more[-1][0].shape, F32)]
            outs = [((send, self.cols), BF16), ((rows, self.cols), BF16)] + outs
            members.append((functools.partial(add_kernel, len(flows), splits, self.block), operands, outs, []))
        results = self.run(*members, vmem=12, after=after)
        made = []
        for (flows, dim, *more), out in zip(steps, results if len(members) > 1 else [results]):
            if flows == "finish":
                made.append(out[0])
                continue
            left = [name for name in more if isinstance(name, str)] + [name for name in flows[0].left if name != dim]
            made.append(Flow(self.place, out[0], out[1], dim, left))
            made += out[2:]
        return made if len(made) > 1 else made[0]


class Flow:
    def __init__(self, place, send, keep, dim, left, where="v"):
        flat = lambda value: value.reshape(-1, value.shape[-1])
        self.keep, self.left, self.place = flat(keep), left, where
        self.got = place.swap(flat(send), dim)


def local(
    tokens, cotangent, lengths, repeats, w_qkv, w_out, w_up, w_down, bias_qv, bias_proj, bias_up, gains, shifts
):
    place = Place()
    chain = Chain()
    rows = 2 * tokens.shape[1]
    bundles = Bundles(place, chain, rows)
    scal = (place.vector, "s")
    dma = pltpu.SemaphoreType.DMA
    wide, tall = (rows, D), (rows, FF)
    part_shape = ((rows // 2, D), BF16)
    weight = {"qkv": (w_qkv, "h"), "out": (w_out, "h"), "up": (w_up, "h"), "down": (w_down, "h")}
    tables = {"qv": (bias_qv, "v"), "proj": (bias_proj, "v"), "up": (bias_up, "v")}
    tables.update(gains=(gains, "v"), shifts=(shifts, "v"))
    swap = place.swap_core
    fast = bundles.fast

    got = place.to_chip(tokens)
    cot = place.to_chip(cotangent)
    low, q, kv = chain.call(
        first_kernel,
        [scal, (lengths, "s"), (repeats, "s"), (got[0], "v"), (got[1], "v"), weight["qkv"], tables["qv"]],
        [(wide, BF16), (wide, BF16), ((rows + 16, 2 * D), BF16)],
        [pltpu.VMEM((D, 3 * D), BF16), dma((1,))],
        16,
    )
    stream, kept = low, []
    for layer in range(LAYERS):
        last = layer == LAYERS - 1
        kv_other = swap(kv)
        operands = [scal, (stream, "v"), (q, "v"), (kv, "v"), (kv_other, "v")]
        operands += [weight["out"], weight["up"], weight["down"]]
        operands += [tables["proj"], tables["up"], tables["gains"], tables["shifts"]]
        far = () if last else ("far",)
        outputs = [((16, rows), F32), (wide, F32, *far), ((rows, 128), F32), (tall, BF16, *far), ((D, rows), BF16, *far)]
        if fast:
            halves = ((3, D // 2, rows), BF16), ((rows, FF // 2), BF16)
            outputs += [halves[0] + ("far",), halves[0], halves[1] + far, halves[1]]
        else:
            outputs += [((rows, ACTS), BF16)]
        if last:
            operands += [(meta, "v")]
            outputs += [(wide, F32), ((rows, 128), F32), part_shape, part_shape]
        else:
            operands += [weight["qkv"], tables["qv"]]
            outputs += [(wide, F32, "far"), ((rows, 128), F32), (wide, F32), (wide, BF16), (wide, BF16)]
            outputs += [((rows, 2 * D), BF16), ((8, D), F32)]
        scratch = [pltpu.VMEM((D, D), BF16), pltpu.VMEM((D, FF), BF16), pltpu.VMEM((FF, D), BF16)]
        scratch += [pltpu.VMEM((D, 3 * D), BF16), pltpu.VMEM((D, rows), BF16), pltpu.VMEM((D, 2 * rows), BF16)]
        scratch += [pltpu.VMEM(wide, F32), dma((4,))]
        if fast:
            scratch += [pltpu.VMEM((rows, ACTS), BF16), pltpu.VMEM((D, rows), BF16), pltpu.VMEM((D, rows), BF16)]
        body = functools.partial(layer_kernel, layer, last, place.chips if fast else 0)
        results = chain.call(body, operands, outputs, scratch, 32)
        lse, hat1, inv1, slope, att_t = results[:5]
        values = dict(q=q, kv=kv, kv_other=kv_other, lse=lse, hat1=hat1, inv1=inv1, slope=slope, att_t=att_t)
        if fast:
            rows_keep, rows_send, cols_keep, cols_send = results[5:9]
            cols = cols_keep, swap(cols_send)
            values["halves"] = (rows_keep, swap(rows_send)), cols if last else [(v, "far") for v in cols]
        else:
            values["acts"], values["acts_other"] = results[5], swap(results[5])
        results = results[9 if fast else 6 :]
        if last:
            values["hat2"], values["inv2"], out0, out1 = results
        else:
            values["hat2"], values["inv2"], stream, low, q, kv, meta = results
        kept.append(values)

    seqs = place.seq_width
    block_shape = ((rows, FF // seqs), BF16)
    swap_all = lambda values: [swap(v) for v in values]

    def turn(layer):
        k = kept[layer]
        operands = [scal, (meta, "v"), (cot[0], "v"), (cot[1], "v"), (k["hat2"], "v"), (k["inv2"], "v")]
        operands += [tables["gains"], (k["slope"], "v"), weight["down"]]
        outputs = [block_shape] * seqs + [((1, FF), F32), (wide, BF16), (wide, F32), ((8, D), F32)]
        scratch = [pltpu.VMEM((seqs, FF // seqs, D), BF16), pltpu.VMEM(wide, F32), dma((seqs,))]
        results = chain.call(functools.partial(turn_kernel, layer), operands, outputs, scratch, 16)
        return results[:seqs], results[seqs:]

    def attention_back(layer, grad_before, grad_two):
        k = kept[layer]
        scratch = [pltpu.VMEM((D, FF), BF16), pltpu.VMEM((D, D), BF16), pltpu.VMEM(wide, BF16)]
        scratch += [pltpu.VMEM((D, rows), BF16), pltpu.VMEM((D, rows), BF16), pltpu.VMEM((D, 2 * rows), BF16)]
        scratch += [pltpu.VMEM((D, rows), BF16), pltpu.VMEM((rows, 2 * D), BF16), dma((2,))]
        operands = [(v, "v") for v in grad_before] + [scal, (meta, "v"), (grad_two, "v")]
        far = "v" if layer == LAYERS - 1 else "far"
        operands += [(k["hat1"], far), (k["inv1"], "v")]
        operands += [(k[name], far) for name in ("q", "kv", "kv_other")] + [(k["lse"], "v"), (k["att_t"], far)]
        operands += [weight["up"], weight["out"], tables["gains"]]
        outputs = [(wide, F32), (wide, BF16), (wide, BF16), ((rows, 2 * D), F32), ((8, D), F32)]
        outputs += [((rows, 2 * D // SENDS), BF16)] * SENDS
        body = functools.partial(attention_back_kernel, layer, seqs)
        return chain.call(body, operands, outputs, scratch, 20)

    def input_back(layer, grad_one, branch, grad_q, dkv, small, *sends, after=()):
        operands = [(swap(v), "v") for v in sends]
        operands += [scal, (grad_q, "v"), (dkv, "v"), (grad_one, "v"), (branch, "v"), weight["qkv"]]
        split = layer == 0 and RIGHT_PIECES > 1
        outputs = [((rows, 4 * D // seqs), BF16)] * seqs if split else [((rows, 4 * D), BF16, "far")]
        scratch = [pltpu.VMEM((D, 3 * D), BF16), pltpu.VMEM((rows, 3 * D), BF16)]
        if layer > 0:
            before = kept[layer - 1]
            operands += [(before["hat2"], "far"), (before["inv2"], "v"), tables["gains"]]
            operands += [(before["slope"], "far"), weight["down"]]
            outputs += [block_shape] * seqs + [((8, D), F32), (wide, BF16), (wide, F32), ((8, D), F32), ((1, FF), F32)]
            scratch += [pltpu.VMEM((seqs, FF // seqs, D), BF16), dma((1,)), dma((seqs,))]
        else:
            outputs += [((8, D), F32), part_shape, part_shape]
            scratch += [dma((1,))]
        body = functools.partial(input_back_kernel, layer, seqs)
        return chain.call(body, operands, outputs, scratch, 20, after)

    z_wide, z_thin = 3 * D // place.seq_width, D // place.seq_width
    plain = [None] * LAYERS

    def plain_sums(layer, mixed, mixed_other, grad_before, before_other, right, right_other):
        k = kept[layer]
        pick = lambda name, at, width: k[name][:, at : at + width]
        split = lambda v: v.reshape(rows, place.seq_width, z_wide + z_thin)
        results = []
        for at, parts in ((LOW, slice(0, z_wide)), (ATT, slice(z_wide, None))):
            rhs = [split(v)[:, :, parts].reshape(rows, -1) for v in (right, right_other)]
            results.append(place.scatter_plain(pick("acts", at, D), pick("acts_other", at, D), *rhs))
        results.append(
            place.scatter_plain(
                pick("acts", NORMED, D),
                pick("acts_other", NORMED, D),
                jnp.concatenate(grad_before, 1),
                jnp.concatenate(before_other, 1),
            )
        )
        results.append(
            place.scatter_plain(pick("acts", ACTIVE, FF), pick("acts_other", ACTIVE, FF), mixed, mixed_other)
        )
        return results

    k1, k0 = kept[1], kept[0]
    halves1, halves0 = (k["halves"] if fast else None for k in (k1, k0))
    before1, (small_up1, mixed1, grad_two, small_two) = turn(1)
    mixed1_other = swap(mixed1)
    before1_other = swap_all(before1)
    if fast:
        d1, u1 = bundles.make(
            bundles.down("x", halves1, mixed1, mixed1_other),
            bundles.up("y", halves1, before1, before1_other),
            far=D1_FAR,
        )
    back = attention_back(1, before1, grad_two)
    small_one1 = back[4]
    hidden = place.from_chip(out0, out1)
    chain.early[HIDDEN_AT] = [hidden]
    right1, *results = input_back(1, *back)
    before0, (small_in1, mixed0, grad_two, small_two0, small_up0) = results[:seqs], results[seqs:]
    mixed0_other = swap(mixed0)
    before0_other = swap_all(before0)
    right1_other = swap(right1)
    if fast:
        d1, u1 = bundles.add(([d1], "y"), ([u1], "x"))
        d0, u0 = bundles.make(
            bundles.down("x", halves0, mixed0, mixed0_other),
            bundles.up("y", halves0, before0, before0_other),
            far=D0_FAR,
        )
        if DU1_FIRST:
            du1 = bundles.add(([d1, u1], "z0", "g"))
    else:
        plain[1] = plain_sums(1, mixed1, mixed1_other, before1, before1_other, right1, right1_other)
    back = attention_back(0, before0, grad_two)
    small_one0 = back[4]
    if fast and not DU1_FIRST:
        du1 = bundles.add(([d1, u1], "z0", "g"))
    if fast and DU1_EARLY:
        du1 = bundles.add(([du1], "z1"))
    if fast and OQ1_FIRST:
        oq1a, oq1b = bundles.make(bundles.oq(("x", "y"), halves1, [right1], [right1_other]))
    *right0, small_in0, last0, last1 = input_back(0, *back)
    right0_other = swap_all(right0)
    grad_tokens = place.from_chip(last0, last1)
    chain.early.setdefault(GRAD_AT, []).append(grad_tokens)
    if fast and not OQ1_FIRST:
        oq1a, oq1b = bundles.make(bundles.oq(("x", "y"), halves1, [right1], [right1_other]))
    smalls = []
    for group in ((small_in0, small_one0, small_two0, small_up0), (small_in1, small_one1, small_two, small_up1)):
        smalls += [(v, "v") for v in group]
    (table,) = chain.call(pack_kernel, smalls, [((LAYERS * 12, D), F32)], [])
    if fast:
        if not DU1_EARLY:
            du1 = bundles.add(([du1], "z1"))
        d0, u0, table = bundles.add(([d0], "y"), ([u0], "x", (table, swap(table))))
        if OQ0_FIRST:
            oq0a, oq0b = bundles.make(bundles.oq(("x", "y"), halves0, right0, right0_other))
        oq1a, oq1b = bundles.add(([oq1a], "y"), ([oq1b], "x"))
        if not OQ0_FIRST:
            oq0a, oq0b = bundles.make(bundles.oq(("x", "y"), halves0, right0, right0_other))
        u0_got = u0.got
        du0, du1 = bundles.add(([d0, u0], "z0", "g"), bundles.finish(du1))
        oq0a, table, oq0b = bundles.add(([oq0a], "y", (table, u0_got)), ([oq0b], "x"))
        oq1 = bundles.add(([oq1a, oq1b], "z0", "z1"))
        du0 = bundles.add(([du0], "z1"))
        oq0, table, oq1 = bundles.add(([oq0a, oq0b], "z0", "z1", (table, oq0a.got)), ([oq1], "z1"))
        oq0, table = bundles.add(([oq0], "z1", (table, oq0.got)))
        places = (((1, 2), 0), ((1, 2), 1), ((3, 4), 0)), (((0,), 0), ((0,), 1), ((5, 6), 0))
        pairs = [(v, "v") for v in (du1, du0.keep, du0.got, oq0.keep, oq0.got, oq1.keep, oq1.got, table)]
        block = bundles.block
        shapes = [(block, z_wide), (block, z_thin), (block, bundles.cols), (z_thin, FF // place.dp_width)]
        pair = ((LAYERS, 2, D), F32)
        *stacked, bias_qv, bias_proj, bias_up, gains, shifts = chain.call(
            functools.partial(last_kernel, (place.seq_width, block, places, 4)),
            pairs,
            [((LAYERS,) + shape, F32) for shape in shapes] + [pair, pair, ((LAYERS, FF), F32), pair, pair],
            [],
        )
        stacked[3] = stacked[3].transpose(0, 2, 1)
    else:
        plain[0] = plain_sums(0, mixed0, mixed0_other, before0, before0_other, *(jnp.concatenate(v, 1) for v in (right0, right0_other)))
        total = place.all_sum(table).reshape(LAYERS, 12, D)
        bias_qv, bias_proj, gains, shifts = (total[:, 2 * k : 2 * k + 2] for k in range(4))
        bias_up = total[:, 8:].reshape(LAYERS, FF)
        stacked = [jnp.stack([plain[layer][k] for layer in range(LAYERS)]) for k in range(4)]
    return (hidden, grad_tokens, *stacked, bias_qv, bias_proj, bias_up, gains, shifts)


def solution(mesh):
    rows = P("dp", "seq", None)
    blocks = P(None, "dp", "seq")
    return jax.shard_map(
        local,
        mesh=mesh,
        in_specs=(rows, rows, P("dp"), P("dp")) + (P(),) * 9,
        out_specs=(rows, rows) + (blocks,) * 4 + (P(),) * 5,
        check_vma=False,
    )
```

```python
import functools
import math

import jax
import jax.numpy as jnp
from jax import lax
from jax.experimental import pallas as pl
from jax.experimental.pallas import tpu as pltpu
from jax.sharding import PartitionSpec as P

D = 768
FF = 3072
HEADS = 12
HEAD = 64
PAIR = 2 * HEAD
LAYERS = 2
EPS = 1e-05
MASKED = -1000000000.0
SCALE = 1.0 / HEAD**0.5
F32 = jnp.float32
BF16 = jnp.bfloat16
FF_STEP = 1024
ERFCX_POINT = 0.48
ERFCX = (
    0.270751081,
    0.27211497,
    0.227394229,
    0.241744859,
    -0.115868816,
    0.444806334,
    -0.579913037,
    0.294191549,
    -0.05522118,
)
ACTIVE, NORMED, ATT, LOW = 0, FF, FF + D, FF + 2 * D
ACTS = FF + 3 * D
CORE, LOW_Z, CHIP, OWN_SEQ, Z = range(5)
DIMS = {"x": (CHIP, 0), "y": (CHIP, 1), "z0": (Z, 0), "z1": (Z, 1)}
COSTS = {2: 6, 6: 4, 9: 90, 14: 90, 20: 18}
HIDDEN_AT, GRAD_AT = 13, 16
TAIL = 32
SENDS = 3


class Place:
    def __init__(self):
        self.dp_width = lax.axis_size("dp")
        self.seq_width = lax.axis_size("seq")
        self.dp = lax.axis_index("dp")
        self.z = lax.axis_index("seq")
        self.core = self.dp % 2
        self.chips = self.dp_width // 2
        self.dp_bits = self.dp_width.bit_length() - 2
        self.seq_bits = self.seq_width.bit_length() - 1
        own_seq = (self.core == self.z // 2).astype(jnp.int32)
        self.vector = jnp.stack([self.core, self.z % 2, self.dp // 2, own_seq, self.z]).astype(jnp.int32)

    def swap_dp(self, value, bit):
        pairs = [(i, i ^ (1 << bit)) for i in range(self.dp_width)]
        return lax.ppermute(value, "dp", pairs)

    def swap(self, value, dim):
        if dim == "core":
            return self.swap_core(value)
        entry, bit = DIMS[dim]
        return self.swap_seq(value, bit) if entry == Z else self.swap_dp(value, bit + 1)

    def swap_core(self, value):
        return self.swap_dp(value, 0)

    def swap_seq(self, value, bit):
        pairs = [(i, i ^ (1 << bit)) for i in range(self.seq_width)]
        return lax.ppermute(value, "seq", pairs)

    def spread_pairs(self, flip, back):
        pairs = []
        for dp in range(self.dp_width):
            chip, core = dp // 2, dp % 2
            for z in range(self.seq_width):
                s = (z % 2) ^ flip
                src = dp * self.seq_width + z
                dst = (2 * chip + z // 2) * self.seq_width + 2 * core + s
                pairs.append((dst, src) if back else (src, dst))
        return pairs

    def to_chip(self, value):
        low = self.z % 2
        pick = lambda at: lax.dynamic_index_in_dim(value, at, 0, keepdims=False)
        first, second = pick(low), pick(1 - low)
        got0 = lax.ppermute(first, ("dp", "seq"), self.spread_pairs(0, False))
        got1 = lax.ppermute(second, ("dp", "seq"), self.spread_pairs(1, False))
        return got0, got1

    def from_chip(self, first, second):
        got0 = lax.ppermute(first, ("dp", "seq"), self.spread_pairs(0, True))
        got1 = lax.ppermute(second, ("dp", "seq"), self.spread_pairs(1, True))
        even = self.z % 2 == 0
        return jnp.stack([jnp.where(even, got0, got1), jnp.where(even, got1, got0)], 0).astype(F32)

    def all_sum(self, value):
        value = value + self.swap_core(value)
        for bit in range(1, self.dp_bits + 1):
            value = value + self.swap_dp(value, bit)
        for bit in range(self.seq_bits):
            value = value + self.swap_seq(value, bit)
        return value

    def halve(self, blocks, axis, mine, swap):
        keep = lax.dynamic_index_in_dim(blocks, mine, axis, keepdims=False)
        send = lax.dynamic_index_in_dim(blocks, 1 - mine, axis, keepdims=False)
        got = swap(send)
        return (keep.astype(F32) + got.astype(F32)).astype(BF16)

    def scatter_plain(self, lhs, lhs_other, rhs, rhs_other):
        rows, m = lhs.shape
        cols = rhs.shape[1]
        block = m // self.dp_width
        both = jnp.concatenate([lhs, lhs_other], 0).reshape(2 * rows, self.chips, 2, block)
        half = lax.dynamic_index_in_dim(both, self.core, 2, keepdims=False).reshape(2 * rows, m // 2)
        right = jnp.concatenate([rhs, rhs_other], 0)
        grad = lax.dot_general(half, right, (((0,), (0,)), ((), ())), preferred_element_type=F32).astype(BF16)
        blocks = grad.reshape((2,) * self.dp_bits + (block, cols))
        for bit in range(self.dp_bits, 0, -1):
            mine = (self.dp >> bit) % 2
            blocks = self.halve(blocks, 0, mine, functools.partial(self.swap_dp, bit=bit))
        blocks = blocks.reshape(block, self.seq_width, cols // self.seq_width).transpose(1, 0, 2)
        blocks = blocks.reshape((2,) * self.seq_bits + (block, cols // self.seq_width))
        for bit in range(self.seq_bits - 1, -1, -1):
            mine = (self.z >> bit) % 2
            blocks = self.halve(blocks, 0, mine, functools.partial(self.swap_seq, bit=bit))
        return blocks.astype(F32)


class Chain:
    def __init__(self):
        self.last = None
        self.count = 0
        self.early = {}

    def call(self, body, operands, outputs, scratch, vmem=12, after=()):
        cost = COSTS.get(self.count, 0)
        after = [*after, *self.early.get(self.count, ())]
        self.count += 1
        spaces = {"v": pltpu.VMEM, "h": pltpu.HBM, "s": pltpu.SMEM, "far": pltpu.VMEM}
        count = len(operands)
        arrays = [pltpu.with_memory_space_constraint(a, pltpu.HBM) if p in ("h", "far") else a for a, p in operands]
        specs = [pl.BlockSpec(memory_space=spaces[p]) for _, p in operands]
        ahead = list(after) + ([] if self.last is None else [self.last])
        arrays += ahead
        specs += [pl.BlockSpec(memory_space=pl.ANY)] * len(ahead)

        inputs = count + len(ahead)

        def inner(*refs):
            refs[inputs + len(outputs)][...] = jnp.zeros((8, 128), F32)
            return body(*refs[:count], *refs[inputs : inputs + len(outputs)], *refs[inputs + len(outputs) + 1 :])

        shapes = [pltpu.HBM(s, d) if far else jax.ShapeDtypeStruct(s, d) for s, d, *far in outputs]
        results = pl.pallas_call(
            inner,
            out_shape=shapes + [jax.ShapeDtypeStruct((8, 128), F32)],
            in_specs=specs,
            out_specs=[pl.BlockSpec(memory_space=pltpu.VMEM) for _ in range(len(outputs) + 1)],
            scratch_shapes=scratch,
            compiler_params=pltpu.CompilerParams(vmem_limit_bytes=vmem << 20),
            cost_estimate=pl.CostEstimate(flops=1024 + cost * 10**9, bytes_accessed=1024, transcendentals=0),
        )(*arrays)
        *results, self.last = results
        return results


def dot(left, right):
    return jnp.dot(left, right, preferred_element_type=F32)


def dot_back(left, right):
    return lax.dot_general(left, right, (((1,), (1,)), ((), ())), preferred_element_type=F32)


def norm_parts(summed):
    average = jnp.mean(summed, -1, keepdims=True)
    centered = summed - average
    variance = jnp.mean(centered * centered, -1, keepdims=True)
    inverse = lax.rsqrt(variance + EPS)
    return centered * inverse, inverse


def norm_back(grad, hat, inverse, gain_row):
    scaled = grad * gain_row
    mean_one = jnp.mean(scaled, -1, keepdims=True)
    mean_hat = jnp.mean(scaled * hat, -1, keepdims=True)
    out = (scaled - mean_one - hat * mean_hat) * inverse
    return out, jnp.sum(grad * hat, 0, keepdims=True), jnp.sum(grad, 0, keepdims=True)


def gelu_parts(before):
    size = jnp.abs(before) * (0.5**0.5)
    spread = jnp.exp(-0.5 * before * before)
    t = 1.0 / (1.0 + ERFCX_POINT * size)
    poly = jnp.full_like(t, ERFCX[-1])
    for factor in ERFCX[-2::-1]:
        poly = poly * t + factor
    tail = 0.5 * (poly * t) * spread
    cdf = jnp.where(before >= 0.0, 1.0 - tail, tail)
    return before * cdf, cdf + before * (spread * 0.3989422804014327)


def load(pairs, sems):
    copies = [pltpu.make_async_copy(src, dst, sems.at[k]) for k, (src, dst) in enumerate(pairs)]
    for copy in copies:
        copy.start()
    return copies


def row(ref, *index):
    return ref[index[:-1] + (pl.ds(index[-1], 1), slice(None))].astype(F32)


def key_masks(scal, length_row, rows):
    spot = lax.broadcasted_iota(jnp.int32, (rows, rows), 0)
    own = (spot + scal[CORE] * rows).astype(F32) < length_row
    other = (spot + (1 - scal[CORE]) * rows).astype(F32) < length_row
    return own, other


def head_lanes(value, h, axis):
    spot = lax.broadcasted_iota(jnp.int32, value.shape, axis) // HEAD
    return jnp.where(spot == h, value, jnp.zeros_like(value))


def join(flag, first, second, out):
    half = first.shape[0]

    @pl.when(flag == 0)
    def _():
        out[0:half] = first[...].astype(out.dtype)
        out[half : 2 * half] = second[...].astype(out.dtype)

    @pl.when(flag != 0)
    def _():
        out[0:half] = second[...].astype(out.dtype)
        out[half : 2 * half] = first[...].astype(out.dtype)


def part(flag, value, first, second):
    half = first.shape[0]

    @pl.when(flag == 0)
    def _():
        first[...] = value[0:half]
        second[...] = value[half : 2 * half]

    @pl.when(flag != 0)
    def _():
        first[...] = value[half : 2 * half]
        second[...] = value[0:half]


def project(layer, low, w, bias_qv, q, kv):
    rows = low.shape[0]
    kv[0:rows, :D] = dot(low[...], w[:, D : 2 * D]).astype(BF16)
    kv[0:rows, D:] = (dot(low[...], w[:, 2 * D :]) + row(bias_qv, layer, 1)).astype(BF16)
    full = (dot(low[...], w[:, :D]) + row(bias_qv, layer, 0)).astype(BF16)
    q[...] = full * jnp.asarray(SCALE, BF16)


def first_kernel(scal, lengths, repeats, got0, got1, w_qkv, bias_qv, low, q, kv, w, sems):
    (copy,) = load([(w_qkv.at[0], w)], sems)
    join(scal[LOW_Z], got0, got1, low)
    rows = low.shape[0]
    spot = lax.broadcasted_iota(jnp.int32, (16, 2 * D), 0)
    facts = [lengths[0] // 16, lengths[0] % 16, lengths[1] // 16, lengths[1] % 16, repeats[0], repeats[1]]
    table = jnp.zeros((16, 2 * D), F32)
    for k, fact in enumerate(facts):
        table = jnp.where(spot == k, fact.astype(F32), table)
    kv[rows : rows + 16] = table.astype(BF16)
    copy.wait()
    project(0, low, w, bias_qv, q, kv)


def core_halves(core, chips, acts, turned, rows_keep, rows_send, cols_keep, cols_send):
    for which, rows_out, cols_out in ((core, rows_keep, cols_keep), (1 - core, rows_send, cols_send)):
        for k, source in enumerate(turned):
            block = D // (2 * chips)
            for chip in range(chips):
                at = pl.multiple_of((chip * 2 + which) * block, block)
                rows_out[k, chip * block : (chip + 1) * block] = source[pl.ds(at, block), :]
        width = FF // (2 * chips)
        for chip in range(chips):
            at = pl.multiple_of((chip * 2 + which) * width, width)
            cols_out[:, chip * width : (chip + 1) * width] = acts[:, pl.ds(at, width)]


def layer_kernel(layer, last, chips, *refs):
    (scal, x, q, kv_own, kv_other, w_out, w_up, w_down) = refs[:8]
    (bias_proj, bias_up, gains, shifts) = refs[8:12]
    refs = refs[12:]
    if last:
        meta, refs = refs[0], refs[1:]
    else:
        (w_qkv, bias_qv) = refs[:2]
        refs = refs[2:]
    (lse, hat1, inv1, slope, ot) = refs[:5]
    refs = refs[5:]
    if chips:
        halves, refs = refs[:4], refs[4:]
    else:
        acts, refs = refs[0], refs[1:]
    hat2, inv2, refs = refs[0], refs[1], refs[2:]
    if last:
        out0, out1 = refs[:2]
        refs = refs[2:]
    else:
        out, low, q_next, kv_next, meta = refs[:5]
        refs = refs[5:]
    (wo, wu, wd, w, qt, vt, acc, sems) = refs[:8]
    rows = q.shape[0]
    if chips:
        acts, normed_t, low_t = refs[8:]
    moves = [(w_out.at[layer], wo), (w_up.at[layer], wu), (w_down.at[layer], wd)]
    if not last:
        moves.append((w_qkv.at[layer + 1], w))
        here = scal[OWN_SEQ] == 1
        facts = jnp.where(here, kv_own[rows:, :D].astype(F32), kv_other[rows:, :D].astype(F32))
        first = scal[LOW_Z] == 0
        meta[0:1] = jnp.where(first, facts[0:1] * 16.0 + facts[1:2], facts[2:3] * 16.0 + facts[3:4])
        meta[1:2] = jnp.where(first, facts[4:5], facts[5:6])
    copies = load(moves, sems)
    acts[:, LOW : LOW + D] = x[...].astype(BF16)
    qt[...] = q[...].T
    vt[:, 0:rows] = kv_own[0:rows, D:].T
    vt[:, rows : 2 * rows] = kv_other[0:rows, D:].T
    valid_own, valid_other = key_masks(scal, meta[0:1, 0:rows], rows)

    def pair(k, carry):
        lanes = pl.ds(pl.multiple_of(k * PAIR, PAIR), PAIR)
        keys_own, keys_other = kv_own[0:rows, lanes], kv_other[0:rows, lanes]
        q_pair = qt[lanes, :]
        for h in range(2):
            q_head = head_lanes(q_pair, h, 0)
            s_own = jnp.where(valid_own, dot(keys_own, q_head), MASKED)
            s_other = jnp.where(valid_other, dot(keys_other, q_head), MASKED)
            top = jnp.maximum(jnp.max(s_own, 0, keepdims=True), jnp.max(s_other, 0, keepdims=True))
            p_own = jnp.exp(s_own - top)
            p_other = jnp.exp(s_other - top)
            total = jnp.sum(p_own, 0, keepdims=True) + jnp.sum(p_other, 0, keepdims=True)
            head = pl.ds(pl.multiple_of(k * PAIR + h * HEAD, HEAD), HEAD)
            o = dot(vt[head, 0:rows], p_own.astype(BF16)) + dot(vt[head, rows : 2 * rows], p_other.astype(BF16))
            ot[head, :] = (o * (1.0 / total)).astype(BF16)
            lse[pl.ds(2 * k + h, 1), :] = top + jnp.log(total)
        return carry

    lax.fori_loop(0, HEADS // 2, pair, 0)
    acts[:, ATT : ATT + D] = ot[...].T
    copies[0].wait()
    h1, i1 = norm_parts(x[...].astype(F32) + (dot(acts[:, ATT : ATT + D], wo[...]) + row(bias_proj, layer, 0)))
    hat1[...] = h1
    inv1[...] = jnp.broadcast_to(i1, inv1.shape)
    normed = h1 * row(gains, layer, 0) + row(shifts, layer, 0)
    acts[:, NORMED : NORMED + D] = normed.astype(BF16)
    acc[...] = normed + row(bias_proj, layer, 1)
    copies[1].wait()
    copies[2].wait()
    for k in range(FF // FF_STEP):
        cols = slice(k * FF_STEP, (k + 1) * FF_STEP)
        before = dot(acts[:, NORMED : NORMED + D], wu[:, cols]) + bias_up[pl.ds(layer, 1), cols].astype(F32)
        value, steep = gelu_parts(before)
        value = value.astype(BF16)
        acts[:, cols] = value
        slope[:, cols] = steep.astype(BF16)
        acc[...] += dot(value, wd[cols, :])
    if chips:
        low_t[...] = acts[:, LOW : LOW + D].T
        normed_t[...] = acts[:, NORMED : NORMED + D].T
        core_halves(scal[CORE], chips, acts, (normed_t, ot, low_t), *halves)
    h2, i2 = norm_parts(acc[...])
    stream = h2 * row(gains, layer, 1) + row(shifts, layer, 1)
    hat2[...] = h2
    inv2[...] = jnp.broadcast_to(i2, inv2.shape)
    if not last:
        out[...] = stream
        low[...] = stream.astype(BF16)
        copies[3].wait()
        project(layer + 1, low, w, bias_qv, q_next, kv_next)
        return
    part(scal[LOW_Z], stream.astype(BF16), out0, out1)


def second_back(layer, grad, hat, inverse, gains, mixed, grad_two, small):
    two, gain_two, shift_two = norm_back(grad, hat, inverse, row(gains, layer, 1))
    grad_two[...] = two
    mixed[...] = two.astype(BF16)
    small[0:1] = jnp.sum(mixed[...].astype(F32), 0, keepdims=True)
    small[1:2] = gain_two
    small[2:3] = shift_two


def load_down(layer, w_down, wd, sems):
    step = wd.shape[1]
    return load([(w_down.at[layer, pl.ds(k * step, step)], wd.at[k]) for k in range(wd.shape[0])], sems)


def up_back(copies, mixed, slope, grad_before, bias_up_grad, wd):
    step = wd.shape[1]
    for k, out in enumerate(grad_before):
        copies[k].wait()
        cols = slice(k * step, (k + 1) * step)
        value = (dot_back(mixed[...], wd[k]) * slope[:, cols].astype(F32)).astype(BF16)
        out[...] = value
        bias_up_grad[:, cols] = jnp.sum(value.astype(F32), 0, keepdims=True)


def turn_kernel(layer, scal, meta, cot0, cot1, hat2, inv2, gains, slope, w_down, *refs):
    grad_before, (bias_up_grad, mixed, grad_two, small, wd, grad, sems) = refs[:-7], refs[-7:]
    copies = load_down(layer, w_down, wd, sems)
    join(scal[LOW_Z], cot0, cot1, grad)
    rows = grad.shape[0]
    spot = lax.broadcasted_iota(jnp.int32, (rows, D), 0) + scal[CORE] * rows
    scaled = grad[...] * jnp.where(spot.astype(F32) < meta[0:1], meta[1:2], 0.0)
    second_back(layer, scaled, hat2[...], inv2[:, 0:1], gains, mixed, grad_two, small)
    up_back(copies, mixed, slope, grad_before, bias_up_grad, wd)


def attention_back_kernel(layer, blocks, *refs):
    grad_before, refs = refs[:blocks], refs[blocks:]
    (scal, meta, grad_two, hat1, inv1, q, kv_own, kv_other, lse, att_t, w_up, w_out, gains) = refs[:13]
    (grad_one, branch, grad_q, dkv_own, small) = refs[13:18]
    sends, (wu, wo, datt, qt, dot_t, kt, dqt, dkv_other, sems) = refs[18:-9], refs[-9:]
    rows = q.shape[0]
    copies = load([(w_up.at[layer], wu), (w_out.at[layer], wo)], sems)
    qt[...] = q[...].T
    kt[:, 0:rows] = kv_own[0:rows, :D].T
    kt[:, rows : 2 * rows] = kv_other[0:rows, :D].T
    copies[0].wait()
    grad_normed = grad_two[...]
    for k, before in enumerate(grad_before):
        width = before.shape[1]
        grad_normed += dot_back(before[...], wu[:, k * width : (k + 1) * width])
    one, gain_one, shift_one = norm_back(grad_normed, hat1[...], inv1[:, 0:1], row(gains, layer, 0))
    grad_one[...] = one
    branch[...] = one.astype(BF16)
    small[0:1] = jnp.sum(branch[...].astype(F32), 0, keepdims=True)
    small[1:2] = gain_one
    small[2:3] = shift_one
    copies[1].wait()
    datt[...] = dot_back(branch[...], wo[...]).astype(BF16)
    dot_t[...] = datt[...].T
    valid_own, valid_other = key_masks(scal, meta[0:1, 0:rows], rows)

    def pair(k, carry):
        lanes = pl.ds(pl.multiple_of(k * PAIR, PAIR), PAIR)
        v_lanes = pl.ds(pl.multiple_of(D + k * PAIR, PAIR), PAIR)
        keys_own, keys_other = kv_own[0:rows, lanes], kv_other[0:rows, lanes]
        vals_own, vals_other = kv_own[0:rows, v_lanes], kv_other[0:rows, v_lanes]
        sums = None
        for h in range(2):
            qt_head = head_lanes(qt[lanes, :], h, 0)
            dt_head = head_lanes(dot_t[lanes, :], h, 0)
            q_head = head_lanes(q[:, lanes], h, 1)
            d_head = head_lanes(datt[:, lanes], h, 1)
            log_total = lse[pl.ds(2 * k + h, 1), :]
            head = pl.ds(pl.multiple_of(k * PAIR + h * HEAD, HEAD), HEAD)
            delta = jnp.sum(dot_t[head, :].astype(F32) * att_t[head, :].astype(F32), 0, keepdims=True)
            dq = None
            parts = []
            for at, keys, vals, valid in ((0, keys_own, vals_own, valid_own), (rows, keys_other, vals_other, valid_other)):
                p = jnp.exp(jnp.where(valid, dot(keys, qt_head), MASKED) - log_total)
                ds = (p * (dot(vals, dt_head) - delta)).astype(BF16)
                more = dot(kt[head, at : at + rows], ds)
                dq = more if dq is None else dq + more
                parts += [dot(ds, q_head), dot(p.astype(BF16), d_head)]
            dqt[head, :] = (dq * SCALE).astype(BF16)
            parts = (parts[0], parts[2], parts[1], parts[3])
            sums = parts if sums is None else tuple(a + b for a, b in zip(sums, parts))
        dkv_own[:, lanes] = sums[0]
        dkv_other[:, lanes] = sums[1].astype(BF16)
        dkv_own[:, v_lanes] = sums[2]
        dkv_other[:, v_lanes] = sums[3].astype(BF16)
        return carry

    lax.fori_loop(0, HEADS // 2, pair, 0, unroll=2)
    grad_q[...] = dqt[...].T
    for k, send in enumerate(sends):
        width = send.shape[1]
        send[...] = dkv_other[:, k * width : (k + 1) * width]


def input_back_kernel(layer, seq_width, *refs):
    got, refs = refs[:SENDS], refs[SENDS:]
    (scal, grad_q, dkv_own, grad_one, branch, w_qkv) = refs[:6]
    refs = refs[6:]
    if layer > 0:
        hat2, inv2, gains, slope, w_down = refs[:5]
        refs = refs[5:]
    right, refs = refs[0], refs[1:]
    if layer > 0:
        grad_before, refs = refs[:seq_width], refs[seq_width:]
        small_in, mixed, grad_two, small, bias_up_grad, w, packed, wd, sems, down_sems = refs
    else:
        small_in, out0, out1, w, packed, sems = refs
    (copy,) = load([(w_qkv.at[layer], w)], sems)
    if layer > 0:
        down_copies = load_down(layer - 1, w_down, wd, down_sems)
    packed[:, :D] = grad_q[...]
    for k, part_got in enumerate(got):
        width = part_got.shape[1]
        cols = slice(k * width, (k + 1) * width)
        packed[:, D + k * width : D + (k + 1) * width] = (dkv_own[:, cols] + part_got[...].astype(F32)).astype(BF16)
    small_in[0:1] = jnp.sum(packed[:, :D].astype(F32), 0, keepdims=True)
    small_in[1:2] = jnp.sum(packed[:, 2 * D :].astype(F32), 0, keepdims=True)
    wide, thin = 3 * D // seq_width, D // seq_width
    for z in range(seq_width):
        at = z * (wide + thin)
        right[:, at : at + wide] = packed[:, z * wide : (z + 1) * wide]
        right[:, at + wide : at + wide + thin] = branch[:, z * thin : (z + 1) * thin]
    copy.wait()
    grad = grad_one[...] + dot_back(packed[...], w[...])
    if layer > 0:
        second_back(layer - 1, grad, hat2[...], inv2[:, 0:1], gains, mixed, grad_two, small)
        up_back(down_copies, mixed, slope, grad_before, bias_up_grad, wd)
    else:
        part(scal[LOW_Z], grad.astype(BF16), out0, out1)


def spread_bit(i, bit, value):
    return ((i >> bit) << (bit + 1)) | (value << bit) | (i & ((1 << bit) - 1))


def chip_order(first, scal, chips):
    if first == "z0":
        return list(range(chips))
    bit = DIMS[first][1]
    mine = (scal[CHIP] >> bit) & 1
    return [spread_bit(i, bit, v) for v in (1 - mine, mine) for i in range(chips // 2)]


def pick_rows(source, order, block, out):
    for i, chip in enumerate(order):
        at = pl.multiple_of(chip * block, block)
        out[i * block : (i + 1) * block, :] = source[pl.ds(at, block), :]


def put(first, scal, chips, z, parts, block, send, keep):
    def store(dst, at, rows):
        for value, lanes in parts:
            dst[at[0], at[1], :, lanes] = value[rows]

    spots = [slice(i * block, (i + 1) * block) for i in range(chips)]
    if first != "z0":
        half = chips // 2
        for i in range(chips):
            store(send if i < half else keep, (i % half, z), spots[i])
        return

    @pl.when(scal[LOW_Z] == z % 2)
    def _():
        for i in range(chips):
            store(keep, (i, z // 2), spots[i])

    @pl.when(scal[LOW_Z] != z % 2)
    def _():
        for i in range(chips):
            store(send, (i, z // 2), spots[i])


def down_kernel(plan, scal, cols, cols_other, mixed, mixed_other, send, keep, turned):
    first, chips, seq_width, block = plan
    rows = mixed.shape[0]
    turned[:, 0:rows] = mixed[...].T
    turned[:, rows : 2 * rows] = mixed_other[...].T
    width = FF // (2 * chips)
    half = chips // 2
    for i, chip in enumerate(chip_order(first, scal, chips)):
        lanes = pl.ds(pl.multiple_of(chip * width, width), width)
        out = dot(turned[:, 0:rows], cols[:, lanes]) + dot(turned[:, rows:], cols_other[:, lanes])
        out = out.astype(BF16)
        dst = send if i < half else keep
        for z in range(seq_width):
            for h in range(2):
                at = (2 * z + h) * block
                dst[i % half, z, :, h * width : (h + 1) * width] = out[at : at + block]


def up_kernel(plan, scal, lhs, lhs_other, *refs):
    first, chips, seq_width, block = plan
    right, right_other, refs = refs[:seq_width], refs[seq_width : 2 * seq_width], refs[2 * seq_width :]
    send, keep, own, other = refs
    order = chip_order(first, scal, chips)
    pick_rows(lhs.at[0], order, block, own)
    pick_rows(lhs_other.at[0], order, block, other)
    for z in range(seq_width):
        out = dot(own[...], right[z][...]) + dot(other[...], right_other[z][...])
        put(first, scal, chips, z, [(out.astype(BF16), slice(None))], block, send, keep)


def oq_kernel(plan, scal, lhs, lhs_other, right, right_other, *refs):
    firsts, chips, seq_width, block = plan
    outs, (low_own, low_other, att_own, att_other) = refs[: 2 * len(firsts)], refs[2 * len(firsts) :]
    wide, width = 3 * D // seq_width, FF // seq_width
    count = seq_width // len(firsts)
    for k, first in enumerate(firsts):
        order = chip_order(first, scal, chips)
        for at, source, own in ((2, lhs, low_own), (2, lhs_other, low_other), (1, lhs, att_own), (1, lhs_other, att_other)):
            pick_rows(source.at[at], order, block, own.at[k])
        for z in range(count):
            at = (k * count + z) * width
            q_cols, o_cols = slice(at, at + wide), slice(at + wide, at + width)
            q_part = dot(low_own[k], right[:, q_cols]) + dot(low_other[k], right_other[:, q_cols])
            o_part = dot(att_own[k], right[:, o_cols]) + dot(att_other[k], right_other[:, o_cols])
            parts = [(q_part.astype(BF16), slice(0, wide)), (o_part.astype(BF16), slice(wide, None))]
            put(first, scal, chips, z, parts, block, outs[2 * k], outs[2 * k + 1])


def tail_sum(table, got):
    if got.dtype == F32:
        return table[...] + got[...]
    count = table.shape[0]
    rows = got.shape[0]
    return table[...].astype(BF16).astype(F32) + got[rows - TAIL : rows, :][0:count].astype(F32)


def add_kernel(groups, splits, block, scal, *refs):
    keeps, gots = refs[0 : 2 * groups : 2], refs[1 : 2 * groups : 2]
    refs = refs[2 * groups :]
    if len(refs) > 2:
        table, table_got, send, keep, table_out = refs
        table_out[...] = tail_sum(table, table_got)
        send[send.shape[0] - TAIL :, :] = jnp.zeros((TAIL, send.shape[1]), BF16)
        send[send.shape[0] - TAIL : send.shape[0] - TAIL + table.shape[0], :] = table_out[...].astype(BF16)
    else:
        send, keep = refs
    at = 0
    for got, kept, (bit, entry, shift) in zip(gots, keeps, splits):
        count = kept.shape[0] // block
        mine = (scal[entry] >> shift) & 1
        for i in range(count // 2):
            for dst, v in ((send, 1 - mine), (keep, mine)):
                src = pl.ds(pl.multiple_of(spread_bit(i, bit, v) * block, block), block)
                dst[at * block : (at + 1) * block] = (kept[src].astype(F32) + got[src].astype(F32)).astype(BF16)
            at += 1


def pack_kernel(*refs):
    out = refs[-1]
    for layer in range(LAYERS):
        first, one, two, up = refs[4 * layer : 4 * layer + 4]
        at = 12 * layer
        out[at : at + 2] = first[0:2]
        for k in range(3):
            out[at + 2 + 2 * k : at + 3 + 2 * k] = one[k : k + 1]
            out[at + 3 + 2 * k : at + 4 + 2 * k] = two[k : k + 1]
        for k in range(FF // D):
            out[at + 8 + k : at + 9 + k] = up[:, k * D : (k + 1) * D]


def finish_kernel(scal, one, two, out):
    out[...] = (one[...].astype(F32) + two[...].astype(F32)).astype(out.dtype)


def last_kernel(plan, *refs):
    seq_width, block, places, tail = plan
    table, grad_qkv, grad_out, grad_up, grad_down, bias_qv, bias_proj, bias_up, gains, shifts = refs[-10:]
    total = tail_sum(table, refs[tail])
    for layer in range(LAYERS):
        at = 12 * layer
        for k, out in enumerate((bias_qv, bias_proj, gains, shifts)):
            out[layer] = total[at + 2 * k : at + 2 * k + 2]
        for k in range(FF // D):
            bias_up[layer : layer + 1, k * D : (k + 1) * D] = total[at + 8 + k : at + 9 + k]
    wide = 3 * D // seq_width
    for layer in range(LAYERS):
        sums = []
        for flow, at in places[layer]:
            rows = slice(at * block, (at + 1) * block)
            sums.append(sum(refs[k][rows].astype(F32) for k in flow))
        down, up, oq = sums
        width = down.shape[1] // 2
        grad_down[layer, 0:block] = down[:, :width]
        grad_down[layer, block : 2 * block] = down[:, width:]
        grad_up[layer] = up
        grad_qkv[layer] = oq[:, :wide]
        grad_out[layer] = oq[:, wide:]


class Bundles:
    def __init__(self, place, chain, rows):
        self.place, self.chain, self.rows = place, chain, rows
        self.block = D // place.dp_width
        self.fast = place.chips == 4 and place.seq_width == 4 and self.block % 16 == 0
        self.cols = FF // place.seq_width

    def shape(self, *lead):
        return lead + (self.block, self.cols), BF16

    def run(self, *members, vmem=14, after=()):
        operands, outputs, scratch = [], [], []
        for _, own, out, temp in members:
            operands += [a if isinstance(a, tuple) else (a, "v") for a in own]
            outputs += out
            scratch += [pltpu.VMEM(shape, BF16) for shape in temp]

        def body(scal, *refs):
            ins, outs, temps = refs[: len(operands)], refs[len(operands) :][: len(outputs)], refs[len(operands) :]
            temps = temps[len(outputs) :]
            for member, own, out, temp in members:
                member(scal, *ins[: len(own)], *outs[: len(out)], *temps[: len(temp)])
                ins, outs, temps = ins[len(own) :], outs[len(out) :], temps[len(temp) :]

        results = self.chain.call(body, [(self.place.vector, "s")] + operands, outputs, scratch, vmem, after)
        parts = []
        for _, _, out, _ in members:
            parts.append(results[: len(out)])
            results = results[len(out) :]
        return parts if len(members) > 1 else parts[0]

    def first(self, first, count):
        chips, seqs = self.place.chips, count
        if first == "z0":
            return self.shape(chips, seqs // 2), ["y", "x", "z1"][: 2 + (seqs > 2)]
        left = ["x" if first == "y" else "y"] + ["z1", "z0"][-1 if seqs == 2 else 0 :]
        return self.shape(chips // 2, seqs), left

    def down(self, first, halves, mixed, mixed_other):
        plan = (first, self.place.chips, self.place.seq_width, self.block)
        out, left = self.first(first, self.place.seq_width)
        operands = [*halves[1], mixed, mixed_other]
        member = functools.partial(down_kernel, plan), operands, [out] * 2, [(D, 2 * self.rows)]
        return member, [(first, left)]

    def up(self, first, halves, right, right_other):
        plan = (first, self.place.chips, self.place.seq_width, self.block)
        out, left = self.first(first, self.place.seq_width)
        operands = [(v, "far") for v in halves[0]] + [*right, *right_other]
        scratch = [(D // 2, self.rows)] * 2
        return (functools.partial(up_kernel, plan), operands, [out] * 2, scratch), [(first, left)]

    def oq(self, firsts, halves, right, right_other):
        plan = (firsts, self.place.chips, self.place.seq_width, self.block)
        kinds = [self.first(first, self.place.seq_width // len(firsts)) for first in firsts]
        outs = [out for out, _ in kinds for _ in range(2)]
        operands = [(v, "far") for v in (*halves[0], right, right_other)]
        scratch = [(len(firsts), D // 2, self.rows)] * 4
        member = functools.partial(oq_kernel, plan), operands, outs, scratch
        return member, [(first, left) for first, (_, left) in zip(firsts, kinds)]

    def make(self, *members, far=False):
        where = ("far",) if far else ()
        calls = [(body, ins, [out + where for out in outs], temps) for (body, ins, outs, temps), _ in members]
        results = self.run(*calls)
        flows = []
        for (_, kinds), out in zip(members, results if len(members) > 1 else [results]):
            for k, (first, left) in enumerate(kinds):
                flows.append(Flow(self.place, out[2 * k], out[2 * k + 1], first, left, *where))
        return flows

    def finish(self, flow):
        return "finish", flow

    def add(self, *steps, after=()):
        members = []
        for flows, dim, *more in steps:
            if flows == "finish":
                members.append((finish_kernel, [dim.keep, dim.got], [(dim.keep.shape, BF16)], []))
                continue
            operands = [(v, flow.place) for flow in flows for v in (flow.keep, flow.got)]
            splits = [(len(flow.left) - 1 - flow.left.index(dim), *DIMS[dim]) for flow in flows]
            rows = sum(flow.keep.shape[0] for flow in flows) // 2
            send, outs = rows, []
            if more and isinstance(more[-1], tuple):
                operands += more[-1]
                send, outs = rows + TAIL, [(more[-1][0].shape, F32)]
            outs = [((send, self.cols), BF16), ((rows, self.cols), BF16)] + outs
            members.append((functools.partial(add_kernel, len(flows), splits, self.block), operands, outs, []))
        results = self.run(*members, vmem=12, after=after)
        made = []
        for (flows, dim, *more), out in zip(steps, results if len(members) > 1 else [results]):
            if flows == "finish":
                made.append(out[0])
                continue
            left = [name for name in more if isinstance(name, str)] + [name for name in flows[0].left if name != dim]
            made.append(Flow(self.place, out[0], out[1], dim, left))
            made += out[2:]
        return made if len(made) > 1 else made[0]


class Flow:
    def __init__(self, place, send, keep, dim, left, where="v"):
        flat = lambda value: value.reshape(-1, value.shape[-1])
        self.keep, self.left, self.place = flat(keep), left, where
        self.got = place.swap(flat(send), dim)


def local(
    tokens, cotangent, lengths, repeats, w_qkv, w_out, w_up, w_down, bias_qv, bias_proj, bias_up, gains, shifts
):
    place = Place()
    chain = Chain()
    rows = 2 * tokens.shape[1]
    bundles = Bundles(place, chain, rows)
    scal = (place.vector, "s")
    dma = pltpu.SemaphoreType.DMA
    wide, tall = (rows, D), (rows, FF)
    part_shape = ((rows // 2, D), BF16)
    weight = {"qkv": (w_qkv, "h"), "out": (w_out, "h"), "up": (w_up, "h"), "down": (w_down, "h")}
    tables = {"qv": (bias_qv, "v"), "proj": (bias_proj, "v"), "up": (bias_up, "v")}
    tables.update(gains=(gains, "v"), shifts=(shifts, "v"))
    swap = place.swap_core
    fast = bundles.fast

    got = place.to_chip(tokens)
    cot = place.to_chip(cotangent)
    low, q, kv = chain.call(
        first_kernel,
        [scal, (lengths, "s"), (repeats, "s"), (got[0], "v"), (got[1], "v"), weight["qkv"], tables["qv"]],
        [(wide, BF16), (wide, BF16), ((rows + 16, 2 * D), BF16)],
        [pltpu.VMEM((D, 3 * D), BF16), dma((1,))],
        16,
    )
    stream, kept = low, []
    for layer in range(LAYERS):
        last = layer == LAYERS - 1
        kv_other = swap(kv)
        operands = [scal, (stream, "v"), (q, "v"), (kv, "v"), (kv_other, "v")]
        operands += [weight["out"], weight["up"], weight["down"]]
        operands += [tables["proj"], tables["up"], tables["gains"], tables["shifts"]]
        far = () if last else ("far",)
        outputs = [((16, rows), F32), (wide, F32, *far), ((rows, 128), F32), (tall, BF16, *far), ((D, rows), BF16, *far)]
        if fast:
            halves = ((3, D // 2, rows), BF16), ((rows, FF // 2), BF16)
            outputs += [halves[0] + ("far",), halves[0], halves[1] + far, halves[1]]
        else:
            outputs += [((rows, ACTS), BF16)]
        if last:
            operands += [(meta, "v")]
            outputs += [(wide, F32), ((rows, 128), F32), part_shape, part_shape]
        else:
            operands += [weight["qkv"], tables["qv"]]
            outputs += [(wide, F32, "far"), ((rows, 128), F32), (wide, F32), (wide, BF16), (wide, BF16)]
            outputs += [((rows, 2 * D), BF16), ((8, D), F32)]
        scratch = [pltpu.VMEM((D, D), BF16), pltpu.VMEM((D, FF), BF16), pltpu.VMEM((FF, D), BF16)]
        scratch += [pltpu.VMEM((D, 3 * D), BF16), pltpu.VMEM((D, rows), BF16), pltpu.VMEM((D, 2 * rows), BF16)]
        scratch += [pltpu.VMEM(wide, F32), dma((4,))]
        if fast:
            scratch += [pltpu.VMEM((rows, ACTS), BF16), pltpu.VMEM((D, rows), BF16), pltpu.VMEM((D, rows), BF16)]
        body = functools.partial(layer_kernel, layer, last, place.chips if fast else 0)
        results = chain.call(body, operands, outputs, scratch, 32)
        lse, hat1, inv1, slope, att_t = results[:5]
        values = dict(q=q, kv=kv, kv_other=kv_other, lse=lse, hat1=hat1, inv1=inv1, slope=slope, att_t=att_t)
        if fast:
            rows_keep, rows_send, cols_keep, cols_send = results[5:9]
            cols = cols_keep, swap(cols_send)
            values["halves"] = (rows_keep, swap(rows_send)), cols if last else [(v, "far") for v in cols]
        else:
            values["acts"], values["acts_other"] = results[5], swap(results[5])
        results = results[9 if fast else 6 :]
        if last:
            values["hat2"], values["inv2"], out0, out1 = results
        else:
            values["hat2"], values["inv2"], stream, low, q, kv, meta = results
        kept.append(values)

    seqs = place.seq_width
    block_shape = ((rows, FF // seqs), BF16)
    swap_all = lambda values: [swap(v) for v in values]

    def turn(layer):
        k = kept[layer]
        operands = [scal, (meta, "v"), (cot[0], "v"), (cot[1], "v"), (k["hat2"], "v"), (k["inv2"], "v")]
        operands += [tables["gains"], (k["slope"], "v"), weight["down"]]
        outputs = [block_shape] * seqs + [((1, FF), F32), (wide, BF16), (wide, F32), ((8, D), F32)]
        scratch = [pltpu.VMEM((seqs, FF // seqs, D), BF16), pltpu.VMEM(wide, F32), dma((seqs,))]
        results = chain.call(functools.partial(turn_kernel, layer), operands, outputs, scratch, 16)
        return results[:seqs], results[seqs:]

    def attention_back(layer, grad_before, grad_two):
        k = kept[layer]
        scratch = [pltpu.VMEM((D, FF), BF16), pltpu.VMEM((D, D), BF16), pltpu.VMEM(wide, BF16)]
        scratch += [pltpu.VMEM((D, rows), BF16), pltpu.VMEM((D, rows), BF16), pltpu.VMEM((D, 2 * rows), BF16)]
        scratch += [pltpu.VMEM((D, rows), BF16), pltpu.VMEM((rows, 2 * D), BF16), dma((2,))]
        operands = [(v, "v") for v in grad_before] + [scal, (meta, "v"), (grad_two, "v")]
        far = "v" if layer == LAYERS - 1 else "far"
        operands += [(k["hat1"], far), (k["inv1"], "v")]
        operands += [(k[name], far) for name in ("q", "kv", "kv_other")] + [(k["lse"], "v"), (k["att_t"], far)]
        operands += [weight["up"], weight["out"], tables["gains"]]
        outputs = [(wide, F32), (wide, BF16), (wide, BF16), ((rows, 2 * D), F32), ((8, D), F32)]
        outputs += [((rows, 2 * D // SENDS), BF16)] * SENDS
        body = functools.partial(attention_back_kernel, layer, seqs)
        return chain.call(body, operands, outputs, scratch, 20)

    def input_back(layer, grad_one, branch, grad_q, dkv, small, *sends, after=()):
        operands = [(swap(v), "v") for v in sends]
        operands += [scal, (grad_q, "v"), (dkv, "v"), (grad_one, "v"), (branch, "v"), weight["qkv"]]
        outputs = [((rows, 4 * D), BF16, "far")]
        scratch = [pltpu.VMEM((D, 3 * D), BF16), pltpu.VMEM((rows, 3 * D), BF16)]
        if layer > 0:
            before = kept[layer - 1]
            operands += [(before["hat2"], "far"), (before["inv2"], "v"), tables["gains"]]
            operands += [(before["slope"], "far"), weight["down"]]
            outputs += [block_shape] * seqs + [((8, D), F32), (wide, BF16), (wide, F32), ((8, D), F32), ((1, FF), F32)]
            scratch += [pltpu.VMEM((seqs, FF // seqs, D), BF16), dma((1,)), dma((seqs,))]
        else:
            outputs += [((8, D), F32), part_shape, part_shape]
            scratch += [dma((1,))]
        body = functools.partial(input_back_kernel, layer, seqs)
        return chain.call(body, operands, outputs, scratch, 20, after)

    z_wide, z_thin = 3 * D // place.seq_width, D // place.seq_width
    plain = [None] * LAYERS

    def plain_sums(layer, mixed, mixed_other, grad_before, before_other, right, right_other):
        k = kept[layer]
        pick = lambda name, at, width: k[name][:, at : at + width]
        split = lambda v: v.reshape(rows, place.seq_width, z_wide + z_thin)
        results = []
        for at, parts in ((LOW, slice(0, z_wide)), (ATT, slice(z_wide, None))):
            rhs = [split(v)[:, :, parts].reshape(rows, -1) for v in (right, right_other)]
            results.append(place.scatter_plain(pick("acts", at, D), pick("acts_other", at, D), *rhs))
        results.append(
            place.scatter_plain(
                pick("acts", NORMED, D),
                pick("acts_other", NORMED, D),
                jnp.concatenate(grad_before, 1),
                jnp.concatenate(before_other, 1),
            )
        )
        results.append(
            place.scatter_plain(pick("acts", ACTIVE, FF), pick("acts_other", ACTIVE, FF), mixed, mixed_other)
        )
        return results

    k1, k0 = kept[1], kept[0]
    halves1, halves0 = (k["halves"] if fast else None for k in (k1, k0))
    before1, (small_up1, mixed1, grad_two, small_two) = turn(1)
    mixed1_other = swap(mixed1)
    before1_other = swap_all(before1)
    if fast:
        d1, u1 = bundles.make(
            bundles.down("x", halves1, mixed1, mixed1_other),
            bundles.up("y", halves1, before1, before1_other),
        )
    back = attention_back(1, before1, grad_two)
    small_one1 = back[4]
    hidden = place.from_chip(out0, out1)
    chain.early[HIDDEN_AT] = [hidden]
    right1, *results = input_back(1, *back)
    before0, (small_in1, mixed0, grad_two, small_two0, small_up0) = results[:seqs], results[seqs:]
    mixed0_other = swap(mixed0)
    before0_other = swap_all(before0)
    right1_other = swap(right1)
    if fast:
        d1, u1 = bundles.add(([d1], "y"), ([u1], "x"))
        d0, u0 = bundles.make(
            bundles.down("x", halves0, mixed0, mixed0_other),
            bundles.up("y", halves0, before0, before0_other),
        )
    else:
        plain[1] = plain_sums(1, mixed1, mixed1_other, before1, before1_other, right1, right1_other)
    back = attention_back(0, before0, grad_two)
    small_one0 = back[4]
    if fast:
        du1 = bundles.add(([d1, u1], "z0", "g"))
        oq1a, oq1b = bundles.make(bundles.oq(("x", "y"), halves1, right1, right1_other))
    right0, small_in0, last0, last1 = input_back(0, *back)
    right0_other = swap(right0)
    grad_tokens = place.from_chip(last0, last1)
    chain.early.setdefault(GRAD_AT, []).append(grad_tokens)
    smalls = []
    for group in ((small_in0, small_one0, small_two0, small_up0), (small_in1, small_one1, small_two, small_up1)):
        smalls += [(v, "v") for v in group]
    (table,) = chain.call(pack_kernel, smalls, [((LAYERS * 12, D), F32)], [])
    if fast:
        du1 = bundles.add(([du1], "z1"))
        d0, u0, table = bundles.add(([d0], "y"), ([u0], "x", (table, swap(table))))
        u0_got = u0.got
        oq0a, oq0b = bundles.make(bundles.oq(("x", "y"), halves0, right0, right0_other))
        oq1a, oq1b = bundles.add(([oq1a], "y"), ([oq1b], "x"))
        du0, du1 = bundles.add(([d0, u0], "z0", "g"), bundles.finish(du1))
        oq0a, table, oq0b = bundles.add(([oq0a], "y", (table, u0_got)), ([oq0b], "x"))
        oq1 = bundles.add(([oq1a, oq1b], "z0", "z1"))
        du0 = bundles.add(([du0], "z1"))
        oq0, table, oq1 = bundles.add(([oq0a, oq0b], "z0", "z1", (table, oq0a.got)), ([oq1], "z1"))
        oq0, table = bundles.add(([oq0], "z1", (table, oq0.got)))
        places = (((1, 2), 0), ((1, 2), 1), ((3, 4), 0)), (((0,), 0), ((0,), 1), ((5, 6), 0))
        pairs = [(v, "v") for v in (du1, du0.keep, du0.got, oq0.keep, oq0.got, oq1.keep, oq1.got, table)]
        block = bundles.block
        shapes = [(block, z_wide), (block, z_thin), (block, bundles.cols), (z_thin, FF // place.dp_width)]
        pair = ((LAYERS, 2, D), F32)
        *stacked, bias_qv, bias_proj, bias_up, gains, shifts = chain.call(
            functools.partial(last_kernel, (place.seq_width, block, places, 4)),
            pairs,
            [((LAYERS,) + shape, F32) for shape in shapes] + [pair, pair, ((LAYERS, FF), F32), pair, pair],
            [],
        )
        stacked[3] = stacked[3].transpose(0, 2, 1)
    else:
        plain[0] = plain_sums(0, mixed0, mixed0_other, before0, before0_other, right0, right0_other)
        total = place.all_sum(table).reshape(LAYERS, 12, D)
        bias_qv, bias_proj, gains, shifts = (total[:, 2 * k : 2 * k + 2] for k in range(4))
        bias_up = total[:, 8:].reshape(LAYERS, FF)
        stacked = [jnp.stack([plain[layer][k] for layer in range(LAYERS)]) for k in range(4)]
    return (hidden, grad_tokens, *stacked, bias_qv, bias_proj, bias_up, gains, shifts)


def solution(mesh):
    rows = P("dp", "seq", None)
    blocks = P(None, "dp", "seq")
    return jax.shard_map(
        local,
        mesh=mesh,
        in_specs=(rows, rows, P("dp"), P("dp")) + (P(),) * 9,
        out_specs=(rows, rows) + (blocks,) * 4 + (P(),) * 5,
        check_vma=False,
    )
```

```python
import functools
import math

import jax
import jax.numpy as jnp
from jax import lax
from jax.experimental import pallas as pl
from jax.experimental.pallas import tpu as pltpu
from jax.sharding import PartitionSpec as P

D = 768
FF = 3072
HEADS = 12
HEAD = 64
PAIR = 2 * HEAD
LAYERS = 2
EPS = 1e-05
MASKED = -1000000000.0
SCALE = 1.0 / HEAD**0.5
F32 = jnp.float32
BF16 = jnp.bfloat16
FF_STEP = 1024
ERFCX_POINT = 0.48
ERFCX = (
    0.270751081,
    0.27211497,
    0.227394229,
    0.241744859,
    -0.115868816,
    0.444806334,
    -0.579913037,
    0.294191549,
    -0.05522118,
)
ACTIVE, NORMED, ATT, LOW = 0, FF, FF + D, FF + 2 * D
ACTS = FF + 3 * D
CORE, LOW_Z, CHIP, OWN_SEQ, Z = range(5)
DIMS = {"x": (CHIP, 0), "y": (CHIP, 1), "z0": (Z, 0), "z1": (Z, 1)}
COSTS = {2: 6, 6: 4, 9: 90, 14: 90, 20: 18}
HIDDEN_AT, GRAD_AT = 13, 16
TAIL = 32
SENDS = 3


class Place:
    def __init__(self):
        self.dp_width = lax.axis_size("dp")
        self.seq_width = lax.axis_size("seq")
        self.dp = lax.axis_index("dp")
        self.z = lax.axis_index("seq")
        self.core = self.dp % 2
        self.chips = self.dp_width // 2
        self.dp_bits = self.dp_width.bit_length() - 2
        self.seq_bits = self.seq_width.bit_length() - 1
        own_seq = (self.core == self.z // 2).astype(jnp.int32)
        self.vector = jnp.stack([self.core, self.z % 2, self.dp // 2, own_seq, self.z]).astype(jnp.int32)

    def swap_dp(self, value, bit):
        pairs = [(i, i ^ (1 << bit)) for i in range(self.dp_width)]
        return lax.ppermute(value, "dp", pairs)

    def swap(self, value, dim):
        if dim == "core":
            return self.swap_core(value)
        entry, bit = DIMS[dim]
        return self.swap_seq(value, bit) if entry == Z else self.swap_dp(value, bit + 1)

    def swap_core(self, value):
        return self.swap_dp(value, 0)

    def swap_seq(self, value, bit):
        pairs = [(i, i ^ (1 << bit)) for i in range(self.seq_width)]
        return lax.ppermute(value, "seq", pairs)

    def spread_pairs(self, flip, back):
        pairs = []
        for dp in range(self.dp_width):
            chip, core = dp // 2, dp % 2
            for z in range(self.seq_width):
                s = (z % 2) ^ flip
                src = dp * self.seq_width + z
                dst = (2 * chip + z // 2) * self.seq_width + 2 * core + s
                pairs.append((dst, src) if back else (src, dst))
        return pairs

    def to_chip(self, value):
        low = self.z % 2
        pick = lambda at: lax.dynamic_index_in_dim(value, at, 0, keepdims=False)
        first, second = pick(low), pick(1 - low)
        got0 = lax.ppermute(first, ("dp", "seq"), self.spread_pairs(0, False))
        got1 = lax.ppermute(second, ("dp", "seq"), self.spread_pairs(1, False))
        return got0, got1

    def from_chip(self, first, second):
        got0 = lax.ppermute(first, ("dp", "seq"), self.spread_pairs(0, True))
        got1 = lax.ppermute(second, ("dp", "seq"), self.spread_pairs(1, True))
        even = self.z % 2 == 0
        return jnp.stack([jnp.where(even, got0, got1), jnp.where(even, got1, got0)], 0).astype(F32)

    def all_sum(self, value):
        value = value + self.swap_core(value)
        for bit in range(1, self.dp_bits + 1):
            value = value + self.swap_dp(value, bit)
        for bit in range(self.seq_bits):
            value = value + self.swap_seq(value, bit)
        return value

    def halve(self, blocks, axis, mine, swap):
        keep = lax.dynamic_index_in_dim(blocks, mine, axis, keepdims=False)
        send = lax.dynamic_index_in_dim(blocks, 1 - mine, axis, keepdims=False)
        got = swap(send)
        return (keep.astype(F32) + got.astype(F32)).astype(BF16)

    def scatter_plain(self, lhs, lhs_other, rhs, rhs_other):
        rows, m = lhs.shape
        cols = rhs.shape[1]
        block = m // self.dp_width
        both = jnp.concatenate([lhs, lhs_other], 0).reshape(2 * rows, self.chips, 2, block)
        half = lax.dynamic_index_in_dim(both, self.core, 2, keepdims=False).reshape(2 * rows, m // 2)
        right = jnp.concatenate([rhs, rhs_other], 0)
        grad = lax.dot_general(half, right, (((0,), (0,)), ((), ())), preferred_element_type=F32).astype(BF16)
        blocks = grad.reshape((2,) * self.dp_bits + (block, cols))
        for bit in range(self.dp_bits, 0, -1):
            mine = (self.dp >> bit) % 2
            blocks = self.halve(blocks, 0, mine, functools.partial(self.swap_dp, bit=bit))
        blocks = blocks.reshape(block, self.seq_width, cols // self.seq_width).transpose(1, 0, 2)
        blocks = blocks.reshape((2,) * self.seq_bits + (block, cols // self.seq_width))
        for bit in range(self.seq_bits - 1, -1, -1):
            mine = (self.z >> bit) % 2
            blocks = self.halve(blocks, 0, mine, functools.partial(self.swap_seq, bit=bit))
        return blocks.astype(F32)


class Chain:
    def __init__(self):
        self.last = None
        self.count = 0
        self.early = {}

    def call(self, body, operands, outputs, scratch, vmem=12, after=()):
        cost = COSTS.get(self.count, 0)
        after = [*after, *self.early.get(self.count, ())]
        self.count += 1
        spaces = {"v": pltpu.VMEM, "h": pltpu.HBM, "s": pltpu.SMEM, "far": pltpu.VMEM}
        count = len(operands)
        arrays = [pltpu.with_memory_space_constraint(a, pltpu.HBM) if p in ("h", "far") else a for a, p in operands]
        specs = [pl.BlockSpec(memory_space=spaces[p]) for _, p in operands]
        ahead = list(after) + ([] if self.last is None else [self.last])
        arrays += ahead
        specs += [pl.BlockSpec(memory_space=pl.ANY)] * len(ahead)

        inputs = count + len(ahead)

        def inner(*refs):
            refs[inputs + len(outputs)][...] = jnp.zeros((8, 128), F32)
            return body(*refs[:count], *refs[inputs : inputs + len(outputs)], *refs[inputs + len(outputs) + 1 :])

        shapes = [pltpu.HBM(s, d) if far else jax.ShapeDtypeStruct(s, d) for s, d, *far in outputs]
        results = pl.pallas_call(
            inner,
            out_shape=shapes + [jax.ShapeDtypeStruct((8, 128), F32)],
            in_specs=specs,
            out_specs=[pl.BlockSpec(memory_space=pltpu.VMEM) for _ in range(len(outputs) + 1)],
            scratch_shapes=scratch,
            compiler_params=pltpu.CompilerParams(vmem_limit_bytes=vmem << 20),
            cost_estimate=pl.CostEstimate(flops=1024 + cost * 10**9, bytes_accessed=1024, transcendentals=0),
        )(*arrays)
        *results, self.last = results
        return results


def dot(left, right):
    return jnp.dot(left, right, preferred_element_type=F32)


def dot_back(left, right):
    return lax.dot_general(left, right, (((1,), (1,)), ((), ())), preferred_element_type=F32)


def norm_parts(summed):
    average = jnp.mean(summed, -1, keepdims=True)
    centered = summed - average
    variance = jnp.mean(centered * centered, -1, keepdims=True)
    inverse = lax.rsqrt(variance + EPS)
    return centered * inverse, inverse


def norm_back(grad, hat, inverse, gain_row):
    scaled = grad * gain_row
    mean_one = jnp.mean(scaled, -1, keepdims=True)
    mean_hat = jnp.mean(scaled * hat, -1, keepdims=True)
    out = (scaled - mean_one - hat * mean_hat) * inverse
    return out, jnp.sum(grad * hat, 0, keepdims=True), jnp.sum(grad, 0, keepdims=True)


def gelu_parts(before):
    size = jnp.abs(before) * (0.5**0.5)
    spread = jnp.exp(-0.5 * before * before)
    t = 1.0 / (1.0 + ERFCX_POINT * size)
    poly = jnp.full_like(t, ERFCX[-1])
    for factor in ERFCX[-2::-1]:
        poly = poly * t + factor
    tail = 0.5 * (poly * t) * spread
    cdf = jnp.where(before >= 0.0, 1.0 - tail, tail)
    return before * cdf, cdf + before * (spread * 0.3989422804014327)


def load(pairs, sems):
    copies = [pltpu.make_async_copy(src, dst, sems.at[k]) for k, (src, dst) in enumerate(pairs)]
    for copy in copies:
        copy.start()
    return copies


def row(ref, *index):
    return ref[index[:-1] + (pl.ds(index[-1], 1), slice(None))].astype(F32)


def key_masks(scal, length_row, rows):
    spot = lax.broadcasted_iota(jnp.int32, (rows, rows), 0)
    own = (spot + scal[CORE] * rows).astype(F32) < length_row
    other = (spot + (1 - scal[CORE]) * rows).astype(F32) < length_row
    return own, other


def head_lanes(value, h, axis):
    spot = lax.broadcasted_iota(jnp.int32, value.shape, axis) // HEAD
    return jnp.where(spot == h, value, jnp.zeros_like(value))


def join(flag, first, second, out):
    half = first.shape[0]

    @pl.when(flag == 0)
    def _():
        out[0:half] = first[...].astype(out.dtype)
        out[half : 2 * half] = second[...].astype(out.dtype)

    @pl.when(flag != 0)
    def _():
        out[0:half] = second[...].astype(out.dtype)
        out[half : 2 * half] = first[...].astype(out.dtype)


def part(flag, value, first, second):
    half = first.shape[0]

    @pl.when(flag == 0)
    def _():
        first[...] = value[0:half]
        second[...] = value[half : 2 * half]

    @pl.when(flag != 0)
    def _():
        first[...] = value[half : 2 * half]
        second[...] = value[0:half]


def project(layer, low, w, bias_qv, q, kv):
    rows = low.shape[0]
    kv[0:rows, :D] = dot(low[...], w[:, D : 2 * D]).astype(BF16)
    kv[0:rows, D:] = (dot(low[...], w[:, 2 * D :]) + row(bias_qv, layer, 1)).astype(BF16)
    full = (dot(low[...], w[:, :D]) + row(bias_qv, layer, 0)).astype(BF16)
    q[...] = full * jnp.asarray(SCALE, BF16)


def first_kernel(scal, lengths, repeats, got0, got1, w_qkv, bias_qv, low, q, kv, w, sems):
    (copy,) = load([(w_qkv.at[0], w)], sems)
    join(scal[LOW_Z], got0, got1, low)
    rows = low.shape[0]
    spot = lax.broadcasted_iota(jnp.int32, (16, 2 * D), 0)
    facts = [lengths[0] // 16, lengths[0] % 16, lengths[1] // 16, lengths[1] % 16, repeats[0], repeats[1]]
    table = jnp.zeros((16, 2 * D), F32)
    for k, fact in enumerate(facts):
        table = jnp.where(spot == k, fact.astype(F32), table)
    kv[rows : rows + 16] = table.astype(BF16)
    copy.wait()
    project(0, low, w, bias_qv, q, kv)


def core_halves(core, chips, acts, turned, rows_keep, rows_send, cols_keep, cols_send):
    for which, rows_out, cols_out in ((core, rows_keep, cols_keep), (1 - core, rows_send, cols_send)):
        for k, source in enumerate(turned):
            block = D // (2 * chips)
            for chip in range(chips):
                at = pl.multiple_of((chip * 2 + which) * block, block)
                rows_out[k, chip * block : (chip + 1) * block] = source[pl.ds(at, block), :]
        width = FF // (2 * chips)
        for chip in range(chips):
            at = pl.multiple_of((chip * 2 + which) * width, width)
            cols_out[:, chip * width : (chip + 1) * width] = acts[:, pl.ds(at, width)]


def layer_kernel(layer, last, chips, *refs):
    (scal, x, q, kv_own, kv_other, w_out, w_up, w_down) = refs[:8]
    (bias_proj, bias_up, gains, shifts) = refs[8:12]
    refs = refs[12:]
    if last:
        meta, refs = refs[0], refs[1:]
    else:
        (w_qkv, bias_qv) = refs[:2]
        refs = refs[2:]
    (lse, hat1, inv1, slope, ot) = refs[:5]
    refs = refs[5:]
    if chips:
        halves, refs = refs[:4], refs[4:]
    else:
        acts, refs = refs[0], refs[1:]
    hat2, inv2, refs = refs[0], refs[1], refs[2:]
    if last:
        out0, out1 = refs[:2]
        refs = refs[2:]
    else:
        out, low, q_next, kv_next, meta = refs[:5]
        refs = refs[5:]
    (wo, wu, wd, w, qt, vt, acc, sems) = refs[:8]
    rows = q.shape[0]
    if chips:
        acts, normed_t, low_t = refs[8:]
    moves = [(w_out.at[layer], wo), (w_up.at[layer], wu), (w_down.at[layer], wd)]
    if not last:
        moves.append((w_qkv.at[layer + 1], w))
        here = scal[OWN_SEQ] == 1
        facts = jnp.where(here, kv_own[rows:, :D].astype(F32), kv_other[rows:, :D].astype(F32))
        first = scal[LOW_Z] == 0
        meta[0:1] = jnp.where(first, facts[0:1] * 16.0 + facts[1:2], facts[2:3] * 16.0 + facts[3:4])
        meta[1:2] = jnp.where(first, facts[4:5], facts[5:6])
    copies = load(moves, sems)
    acts[:, LOW : LOW + D] = x[...].astype(BF16)
    qt[...] = q[...].T
    vt[:, 0:rows] = kv_own[0:rows, D:].T
    vt[:, rows : 2 * rows] = kv_other[0:rows, D:].T
    valid_own, valid_other = key_masks(scal, meta[0:1, 0:rows], rows)

    def pair(k, carry):
        lanes = pl.ds(pl.multiple_of(k * PAIR, PAIR), PAIR)
        keys_own, keys_other = kv_own[0:rows, lanes], kv_other[0:rows, lanes]
        q_pair = qt[lanes, :]
        for h in range(2):
            q_head = head_lanes(q_pair, h, 0)
            s_own = jnp.where(valid_own, dot(keys_own, q_head), MASKED)
            s_other = jnp.where(valid_other, dot(keys_other, q_head), MASKED)
            top = jnp.maximum(jnp.max(s_own, 0, keepdims=True), jnp.max(s_other, 0, keepdims=True))
            p_own = jnp.exp(s_own - top)
            p_other = jnp.exp(s_other - top)
            total = jnp.sum(p_own, 0, keepdims=True) + jnp.sum(p_other, 0, keepdims=True)
            head = pl.ds(pl.multiple_of(k * PAIR + h * HEAD, HEAD), HEAD)
            o = dot(vt[head, 0:rows], p_own.astype(BF16)) + dot(vt[head, rows : 2 * rows], p_other.astype(BF16))
            ot[head, :] = (o * (1.0 / total)).astype(BF16)
            lse[pl.ds(2 * k + h, 1), :] = top + jnp.log(total)
        return carry

    lax.fori_loop(0, HEADS // 2, pair, 0, unroll=3)
    acts[:, ATT : ATT + D] = ot[...].T
    copies[0].wait()
    h1, i1 = norm_parts(x[...].astype(F32) + (dot(acts[:, ATT : ATT + D], wo[...]) + row(bias_proj, layer, 0)))
    hat1[...] = h1
    inv1[...] = jnp.broadcast_to(i1, inv1.shape)
    normed = h1 * row(gains, layer, 0) + row(shifts, layer, 0)
    acts[:, NORMED : NORMED + D] = normed.astype(BF16)
    acc[...] = normed + row(bias_proj, layer, 1)
    copies[1].wait()
    copies[2].wait()
    for k in range(FF // FF_STEP):
        cols = slice(k * FF_STEP, (k + 1) * FF_STEP)
        before = dot(acts[:, NORMED : NORMED + D], wu[:, cols]) + bias_up[pl.ds(layer, 1), cols].astype(F32)
        value, steep = gelu_parts(before)
        value = value.astype(BF16)
        acts[:, cols] = value
        slope[:, cols] = steep.astype(BF16)
        acc[...] += dot(value, wd[cols, :])
    if chips:
        low_t[...] = acts[:, LOW : LOW + D].T
        normed_t[...] = acts[:, NORMED : NORMED + D].T
        core_halves(scal[CORE], chips, acts, (normed_t, ot, low_t), *halves)
    h2, i2 = norm_parts(acc[...])
    stream = h2 * row(gains, layer, 1) + row(shifts, layer, 1)
    hat2[...] = h2
    inv2[...] = jnp.broadcast_to(i2, inv2.shape)
    if not last:
        out[...] = stream
        low[...] = stream.astype(BF16)
        copies[3].wait()
        project(layer + 1, low, w, bias_qv, q_next, kv_next)
        return
    part(scal[LOW_Z], stream.astype(BF16), out0, out1)


def second_back(layer, grad, hat, inverse, gains, mixed, grad_two, small):
    two, gain_two, shift_two = norm_back(grad, hat, inverse, row(gains, layer, 1))
    grad_two[...] = two
    mixed[...] = two.astype(BF16)
    small[0:1] = jnp.sum(mixed[...].astype(F32), 0, keepdims=True)
    small[1:2] = gain_two
    small[2:3] = shift_two


def load_down(layer, w_down, wd, sems):
    step = wd.shape[1]
    return load([(w_down.at[layer, pl.ds(k * step, step)], wd.at[k]) for k in range(wd.shape[0])], sems)


def up_back(copies, mixed, slope, grad_before, bias_up_grad, wd):
    step = wd.shape[1]
    for k, out in enumerate(grad_before):
        copies[k].wait()
        cols = slice(k * step, (k + 1) * step)
        value = (dot_back(mixed[...], wd[k]) * slope[:, cols].astype(F32)).astype(BF16)
        out[...] = value
        bias_up_grad[:, cols] = jnp.sum(value.astype(F32), 0, keepdims=True)


def turn_kernel(layer, scal, meta, cot0, cot1, hat2, inv2, gains, slope, w_down, *refs):
    grad_before, (bias_up_grad, mixed, grad_two, small, wd, grad, sems) = refs[:-7], refs[-7:]
    copies = load_down(layer, w_down, wd, sems)
    join(scal[LOW_Z], cot0, cot1, grad)
    rows = grad.shape[0]
    spot = lax.broadcasted_iota(jnp.int32, (rows, D), 0) + scal[CORE] * rows
    scaled = grad[...] * jnp.where(spot.astype(F32) < meta[0:1], meta[1:2], 0.0)
    second_back(layer, scaled, hat2[...], inv2[:, 0:1], gains, mixed, grad_two, small)
    up_back(copies, mixed, slope, grad_before, bias_up_grad, wd)


def attention_back_kernel(layer, blocks, *refs):
    grad_before, refs = refs[:blocks], refs[blocks:]
    (scal, meta, grad_two, hat1, inv1, q, kv_own, kv_other, lse, att_t, w_up, w_out, gains) = refs[:13]
    (grad_one, branch, grad_q, dkv_own, small) = refs[13:18]
    sends, (wu, wo, datt, qt, dot_t, kt, dqt, dkv_other, sems) = refs[18:-9], refs[-9:]
    rows = q.shape[0]
    copies = load([(w_up.at[layer], wu), (w_out.at[layer], wo)], sems)
    qt[...] = q[...].T
    kt[:, 0:rows] = kv_own[0:rows, :D].T
    kt[:, rows : 2 * rows] = kv_other[0:rows, :D].T
    copies[0].wait()
    grad_normed = grad_two[...]
    for k, before in enumerate(grad_before):
        width = before.shape[1]
        grad_normed += dot_back(before[...], wu[:, k * width : (k + 1) * width])
    one, gain_one, shift_one = norm_back(grad_normed, hat1[...], inv1[:, 0:1], row(gains, layer, 0))
    grad_one[...] = one
    branch[...] = one.astype(BF16)
    small[0:1] = jnp.sum(branch[...].astype(F32), 0, keepdims=True)
    small[1:2] = gain_one
    small[2:3] = shift_one
    copies[1].wait()
    datt[...] = dot_back(branch[...], wo[...]).astype(BF16)
    dot_t[...] = datt[...].T
    valid_own, valid_other = key_masks(scal, meta[0:1, 0:rows], rows)

    def pair(k, carry):
        lanes = pl.ds(pl.multiple_of(k * PAIR, PAIR), PAIR)
        v_lanes = pl.ds(pl.multiple_of(D + k * PAIR, PAIR), PAIR)
        keys_own, keys_other = kv_own[0:rows, lanes], kv_other[0:rows, lanes]
        vals_own, vals_other = kv_own[0:rows, v_lanes], kv_other[0:rows, v_lanes]
        sums = None
        for h in range(2):
            qt_head = head_lanes(qt[lanes, :], h, 0)
            dt_head = head_lanes(dot_t[lanes, :], h, 0)
            q_head = head_lanes(q[:, lanes], h, 1)
            d_head = head_lanes(datt[:, lanes], h, 1)
            log_total = lse[pl.ds(2 * k + h, 1), :]
            head = pl.ds(pl.multiple_of(k * PAIR + h * HEAD, HEAD), HEAD)
            delta = jnp.sum(dot_t[head, :].astype(F32) * att_t[head, :].astype(F32), 0, keepdims=True)
            dq = None
            parts = []
            for at, keys, vals, valid in ((0, keys_own, vals_own, valid_own), (rows, keys_other, vals_other, valid_other)):
                p = jnp.exp(jnp.where(valid, dot(keys, qt_head), MASKED) - log_total)
                ds = (p * (dot(vals, dt_head) - delta)).astype(BF16)
                more = dot(kt[head, at : at + rows], ds)
                dq = more if dq is None else dq + more
                parts += [dot(ds, q_head), dot(p.astype(BF16), d_head)]
            dqt[head, :] = (dq * SCALE).astype(BF16)
            parts = (parts[0], parts[2], parts[1], parts[3])
            sums = parts if sums is None else tuple(a + b for a, b in zip(sums, parts))
        dkv_own[:, lanes] = sums[0]
        dkv_other[:, lanes] = sums[1].astype(BF16)
        dkv_own[:, v_lanes] = sums[2]
        dkv_other[:, v_lanes] = sums[3].astype(BF16)
        return carry

    lax.fori_loop(0, HEADS // 2, pair, 0, unroll=2)
    grad_q[...] = dqt[...].T
    for k, send in enumerate(sends):
        width = send.shape[1]
        send[...] = dkv_other[:, k * width : (k + 1) * width]


def input_back_kernel(layer, seq_width, *refs):
    got, refs = refs[:SENDS], refs[SENDS:]
    (scal, grad_q, dkv_own, grad_one, branch, w_qkv) = refs[:6]
    refs = refs[6:]
    if layer > 0:
        hat2, inv2, gains, slope, w_down = refs[:5]
        refs = refs[5:]
    right, refs = refs[0], refs[1:]
    if layer > 0:
        grad_before, refs = refs[:seq_width], refs[seq_width:]
        small_in, mixed, grad_two, small, bias_up_grad, w, packed, wd, sems, down_sems = refs
    else:
        small_in, out0, out1, w, packed, sems = refs
    (copy,) = load([(w_qkv.at[layer], w)], sems)
    if layer > 0:
        down_copies = load_down(layer - 1, w_down, wd, down_sems)
    packed[:, :D] = grad_q[...]
    for k, part_got in enumerate(got):
        width = part_got.shape[1]
        cols = slice(k * width, (k + 1) * width)
        packed[:, D + k * width : D + (k + 1) * width] = (dkv_own[:, cols] + part_got[...].astype(F32)).astype(BF16)
    small_in[0:1] = jnp.sum(packed[:, :D].astype(F32), 0, keepdims=True)
    small_in[1:2] = jnp.sum(packed[:, 2 * D :].astype(F32), 0, keepdims=True)
    wide, thin = 3 * D // seq_width, D // seq_width
    for z in range(seq_width):
        at = z * (wide + thin)
        right[:, at : at + wide] = packed[:, z * wide : (z + 1) * wide]
        right[:, at + wide : at + wide + thin] = branch[:, z * thin : (z + 1) * thin]
    copy.wait()
    grad = grad_one[...] + dot_back(packed[...], w[...])
    if layer > 0:
        second_back(layer - 1, grad, hat2[...], inv2[:, 0:1], gains, mixed, grad_two, small)
        up_back(down_copies, mixed, slope, grad_before, bias_up_grad, wd)
    else:
        part(scal[LOW_Z], grad.astype(BF16), out0, out1)


def spread_bit(i, bit, value):
    return ((i >> bit) << (bit + 1)) | (value << bit) | (i & ((1 << bit) - 1))


def chip_order(first, scal, chips):
    if first == "z0":
        return list(range(chips))
    bit = DIMS[first][1]
    mine = (scal[CHIP] >> bit) & 1
    return [spread_bit(i, bit, v) for v in (1 - mine, mine) for i in range(chips // 2)]


def pick_rows(source, order, block, out):
    for i, chip in enumerate(order):
        at = pl.multiple_of(chip * block, block)
        out[i * block : (i + 1) * block, :] = source[pl.ds(at, block), :]


def put(first, scal, chips, z, parts, block, send, keep):
    def store(dst, at, rows):
        for value, lanes in parts:
            dst[at[0], at[1], :, lanes] = value[rows]

    spots = [slice(i * block, (i + 1) * block) for i in range(chips)]
    if first != "z0":
        half = chips // 2
        for i in range(chips):
            store(send if i < half else keep, (i % half, z), spots[i])
        return

    @pl.when(scal[LOW_Z] == z % 2)
    def _():
        for i in range(chips):
            store(keep, (i, z // 2), spots[i])

    @pl.when(scal[LOW_Z] != z % 2)
    def _():
        for i in range(chips):
            store(send, (i, z // 2), spots[i])


def down_kernel(plan, scal, cols, cols_other, mixed, mixed_other, send, keep, turned):
    first, chips, seq_width, block = plan
    rows = mixed.shape[0]
    turned[:, 0:rows] = mixed[...].T
    turned[:, rows : 2 * rows] = mixed_other[...].T
    width = FF // (2 * chips)
    half = chips // 2
    for i, chip in enumerate(chip_order(first, scal, chips)):
        lanes = pl.ds(pl.multiple_of(chip * width, width), width)
        out = dot(turned[:, 0:rows], cols[:, lanes]) + dot(turned[:, rows:], cols_other[:, lanes])
        out = out.astype(BF16)
        dst = send if i < half else keep
        for z in range(seq_width):
            for h in range(2):
                at = (2 * z + h) * block
                dst[i % half, z, :, h * width : (h + 1) * width] = out[at : at + block]


def up_kernel(plan, scal, lhs, lhs_other, *refs):
    first, chips, seq_width, block = plan
    right, right_other, refs = refs[:seq_width], refs[seq_width : 2 * seq_width], refs[2 * seq_width :]
    send, keep, own, other = refs
    order = chip_order(first, scal, chips)
    pick_rows(lhs.at[0], order, block, own)
    pick_rows(lhs_other.at[0], order, block, other)
    for z in range(seq_width):
        out = dot(own[...], right[z][...]) + dot(other[...], right_other[z][...])
        put(first, scal, chips, z, [(out.astype(BF16), slice(None))], block, send, keep)


def oq_kernel(plan, scal, lhs, lhs_other, right, right_other, *refs):
    firsts, chips, seq_width, block = plan
    outs, (low_own, low_other, att_own, att_other) = refs[: 2 * len(firsts)], refs[2 * len(firsts) :]
    wide, width = 3 * D // seq_width, FF // seq_width
    count = seq_width // len(firsts)
    for k, first in enumerate(firsts):
        order = chip_order(first, scal, chips)
        for at, source, own in ((2, lhs, low_own), (2, lhs_other, low_other), (1, lhs, att_own), (1, lhs_other, att_other)):
            pick_rows(source.at[at], order, block, own.at[k])
        for z in range(count):
            at = (k * count + z) * width
            q_cols, o_cols = slice(at, at + wide), slice(at + wide, at + width)
            q_part = dot(low_own[k], right[:, q_cols]) + dot(low_other[k], right_other[:, q_cols])
            o_part = dot(att_own[k], right[:, o_cols]) + dot(att_other[k], right_other[:, o_cols])
            parts = [(q_part.astype(BF16), slice(0, wide)), (o_part.astype(BF16), slice(wide, None))]
            put(first, scal, chips, z, parts, block, outs[2 * k], outs[2 * k + 1])


def tail_sum(table, got):
    if got.dtype == F32:
        return table[...] + got[...]
    count = table.shape[0]
    rows = got.shape[0]
    return table[...].astype(BF16).astype(F32) + got[rows - TAIL : rows, :][0:count].astype(F32)


def add_kernel(groups, splits, block, scal, *refs):
    keeps, gots = refs[0 : 2 * groups : 2], refs[1 : 2 * groups : 2]
    refs = refs[2 * groups :]
    if len(refs) > 2:
        table, table_got, send, keep, table_out = refs
        table_out[...] = tail_sum(table, table_got)
        send[send.shape[0] - TAIL :, :] = jnp.zeros((TAIL, send.shape[1]), BF16)
        send[send.shape[0] - TAIL : send.shape[0] - TAIL + table.shape[0], :] = table_out[...].astype(BF16)
    else:
        send, keep = refs
    at = 0
    for got, kept, (bit, entry, shift) in zip(gots, keeps, splits):
        count = kept.shape[0] // block
        mine = (scal[entry] >> shift) & 1
        for i in range(count // 2):
            for dst, v in ((send, 1 - mine), (keep, mine)):
                src = pl.ds(pl.multiple_of(spread_bit(i, bit, v) * block, block), block)
                dst[at * block : (at + 1) * block] = (kept[src].astype(F32) + got[src].astype(F32)).astype(BF16)
            at += 1


def pack_kernel(*refs):
    out = refs[-1]
    for layer in range(LAYERS):
        first, one, two, up = refs[4 * layer : 4 * layer + 4]
        at = 12 * layer
        out[at : at + 2] = first[0:2]
        for k in range(3):
            out[at + 2 + 2 * k : at + 3 + 2 * k] = one[k : k + 1]
            out[at + 3 + 2 * k : at + 4 + 2 * k] = two[k : k + 1]
        for k in range(FF // D):
            out[at + 8 + k : at + 9 + k] = up[:, k * D : (k + 1) * D]


def finish_kernel(scal, one, two, out):
    out[...] = (one[...].astype(F32) + two[...].astype(F32)).astype(out.dtype)


def last_kernel(plan, *refs):
    seq_width, block, places, tail = plan
    table, grad_qkv, grad_out, grad_up, grad_down, bias_qv, bias_proj, bias_up, gains, shifts = refs[-10:]
    total = tail_sum(table, refs[tail])
    for layer in range(LAYERS):
        at = 12 * layer
        for k, out in enumerate((bias_qv, bias_proj, gains, shifts)):
            out[layer] = total[at + 2 * k : at + 2 * k + 2]
        for k in range(FF // D):
            bias_up[layer : layer + 1, k * D : (k + 1) * D] = total[at + 8 + k : at + 9 + k]
    wide = 3 * D // seq_width
    for layer in range(LAYERS):
        sums = []
        for flow, at in places[layer]:
            rows = slice(at * block, (at + 1) * block)
            sums.append(sum(refs[k][rows].astype(F32) for k in flow))
        down, up, oq = sums
        width = down.shape[1] // 2
        grad_down[layer, 0:block] = down[:, :width]
        grad_down[layer, block : 2 * block] = down[:, width:]
        grad_up[layer] = up
        grad_qkv[layer] = oq[:, :wide]
        grad_out[layer] = oq[:, wide:]


class Bundles:
    def __init__(self, place, chain, rows):
        self.place, self.chain, self.rows = place, chain, rows
        self.block = D // place.dp_width
        self.fast = place.chips == 4 and place.seq_width == 4 and self.block % 16 == 0
        self.cols = FF // place.seq_width

    def shape(self, *lead):
        return lead + (self.block, self.cols), BF16

    def run(self, *members, vmem=14, after=()):
        operands, outputs, scratch = [], [], []
        for _, own, out, temp in members:
            operands += [a if isinstance(a, tuple) else (a, "v") for a in own]
            outputs += out
            scratch += [pltpu.VMEM(shape, BF16) for shape in temp]

        def body(scal, *refs):
            ins, outs, temps = refs[: len(operands)], refs[len(operands) :][: len(outputs)], refs[len(operands) :]
            temps = temps[len(outputs) :]
            for member, own, out, temp in members:
                member(scal, *ins[: len(own)], *outs[: len(out)], *temps[: len(temp)])
                ins, outs, temps = ins[len(own) :], outs[len(out) :], temps[len(temp) :]

        results = self.chain.call(body, [(self.place.vector, "s")] + operands, outputs, scratch, vmem, after)
        parts = []
        for _, _, out, _ in members:
            parts.append(results[: len(out)])
            results = results[len(out) :]
        return parts if len(members) > 1 else parts[0]

    def first(self, first, count):
        chips, seqs = self.place.chips, count
        if first == "z0":
            return self.shape(chips, seqs // 2), ["y", "x", "z1"][: 2 + (seqs > 2)]
        left = ["x" if first == "y" else "y"] + ["z1", "z0"][-1 if seqs == 2 else 0 :]
        return self.shape(chips // 2, seqs), left

    def down(self, first, halves, mixed, mixed_other):
        plan = (first, self.place.chips, self.place.seq_width, self.block)
        out, left = self.first(first, self.place.seq_width)
        operands = [*halves[1], mixed, mixed_other]
        member = functools.partial(down_kernel, plan), operands, [out] * 2, [(D, 2 * self.rows)]
        return member, [(first, left)]

    def up(self, first, halves, right, right_other):
        plan = (first, self.place.chips, self.place.seq_width, self.block)
        out, left = self.first(first, self.place.seq_width)
        operands = [(v, "far") for v in halves[0]] + [*right, *right_other]
        scratch = [(D // 2, self.rows)] * 2
        return (functools.partial(up_kernel, plan), operands, [out] * 2, scratch), [(first, left)]

    def oq(self, firsts, halves, right, right_other):
        plan = (firsts, self.place.chips, self.place.seq_width, self.block)
        kinds = [self.first(first, self.place.seq_width // len(firsts)) for first in firsts]
        outs = [out for out, _ in kinds for _ in range(2)]
        operands = [(v, "far") for v in (*halves[0], right, right_other)]
        scratch = [(len(firsts), D // 2, self.rows)] * 4
        member = functools.partial(oq_kernel, plan), operands, outs, scratch
        return member, [(first, left) for first, (_, left) in zip(firsts, kinds)]

    def make(self, *members, far=False):
        where = ("far",) if far else ()
        calls = [(body, ins, [out + where for out in outs], temps) for (body, ins, outs, temps), _ in members]
        results = self.run(*calls)
        flows = []
        for (_, kinds), out in zip(members, results if len(members) > 1 else [results]):
            for k, (first, left) in enumerate(kinds):
                flows.append(Flow(self.place, out[2 * k], out[2 * k + 1], first, left, *where))
        return flows

    def finish(self, flow):
        return "finish", flow

    def add(self, *steps, after=()):
        members = []
        for flows, dim, *more in steps:
            if flows == "finish":
                members.append((finish_kernel, [dim.keep, dim.got], [(dim.keep.shape, BF16)], []))
                continue
            operands = [(v, flow.place) for flow in flows for v in (flow.keep, flow.got)]
            splits = [(len(flow.left) - 1 - flow.left.index(dim), *DIMS[dim]) for flow in flows]
            rows = sum(flow.keep.shape[0] for flow in flows) // 2
            send, outs = rows, []
            if more and isinstance(more[-1], tuple):
                operands += more[-1]
                send, outs = rows + TAIL, [(more[-1][0].shape, F32)]
            outs = [((send, self.cols), BF16), ((rows, self.cols), BF16)] + outs
            members.append((functools.partial(add_kernel, len(flows), splits, self.block), operands, outs, []))
        results = self.run(*members, vmem=12, after=after)
        made = []
        for (flows, dim, *more), out in zip(steps, results if len(members) > 1 else [results]):
            if flows == "finish":
                made.append(out[0])
                continue
            left = [name for name in more if isinstance(name, str)] + [name for name in flows[0].left if name != dim]
            made.append(Flow(self.place, out[0], out[1], dim, left))
            made += out[2:]
        return made if len(made) > 1 else made[0]


class Flow:
    def __init__(self, place, send, keep, dim, left, where="v"):
        flat = lambda value: value.reshape(-1, value.shape[-1])
        self.keep, self.left, self.place = flat(keep), left, where
        self.got = place.swap(flat(send), dim)


def local(
    tokens, cotangent, lengths, repeats, w_qkv, w_out, w_up, w_down, bias_qv, bias_proj, bias_up, gains, shifts
):
    place = Place()
    chain = Chain()
    rows = 2 * tokens.shape[1]
    bundles = Bundles(place, chain, rows)
    scal = (place.vector, "s")
    dma = pltpu.SemaphoreType.DMA
    wide, tall = (rows, D), (rows, FF)
    part_shape = ((rows // 2, D), BF16)
    weight = {"qkv": (w_qkv, "h"), "out": (w_out, "h"), "up": (w_up, "h"), "down": (w_down, "h")}
    tables = {"qv": (bias_qv, "v"), "proj": (bias_proj, "v"), "up": (bias_up, "v")}
    tables.update(gains=(gains, "v"), shifts=(shifts, "v"))
    swap = place.swap_core
    fast = bundles.fast

    got = place.to_chip(tokens)
    cot = place.to_chip(cotangent)
    low, q, kv = chain.call(
        first_kernel,
        [scal, (lengths, "s"), (repeats, "s"), (got[0], "v"), (got[1], "v"), weight["qkv"], tables["qv"]],
        [(wide, BF16), (wide, BF16), ((rows + 16, 2 * D), BF16)],
        [pltpu.VMEM((D, 3 * D), BF16), dma((1,))],
        16,
    )
    stream, kept = low, []
    for layer in range(LAYERS):
        last = layer == LAYERS - 1
        kv_other = swap(kv)
        operands = [scal, (stream, "v"), (q, "v"), (kv, "v"), (kv_other, "v")]
        operands += [weight["out"], weight["up"], weight["down"]]
        operands += [tables["proj"], tables["up"], tables["gains"], tables["shifts"]]
        far = () if last else ("far",)
        outputs = [((16, rows), F32), (wide, F32, *far), ((rows, 128), F32), (tall, BF16, *far), ((D, rows), BF16, *far)]
        if fast:
            halves = ((3, D // 2, rows), BF16), ((rows, FF // 2), BF16)
            outputs += [halves[0] + ("far",), halves[0], halves[1] + far, halves[1]]
        else:
            outputs += [((rows, ACTS), BF16)]
        if last:
            operands += [(meta, "v")]
            outputs += [(wide, F32), ((rows, 128), F32), part_shape, part_shape]
        else:
            operands += [weight["qkv"], tables["qv"]]
            outputs += [(wide, F32, "far"), ((rows, 128), F32), (wide, F32), (wide, BF16), (wide, BF16)]
            outputs += [((rows, 2 * D), BF16), ((8, D), F32)]
        scratch = [pltpu.VMEM((D, D), BF16), pltpu.VMEM((D, FF), BF16), pltpu.VMEM((FF, D), BF16)]
        scratch += [pltpu.VMEM((D, 3 * D), BF16), pltpu.VMEM((D, rows), BF16), pltpu.VMEM((D, 2 * rows), BF16)]
        scratch += [pltpu.VMEM(wide, F32), dma((4,))]
        if fast:
            scratch += [pltpu.VMEM((rows, ACTS), BF16), pltpu.VMEM((D, rows), BF16), pltpu.VMEM((D, rows), BF16)]
        body = functools.partial(layer_kernel, layer, last, place.chips if fast else 0)
        results = chain.call(body, operands, outputs, scratch, 32)
        lse, hat1, inv1, slope, att_t = results[:5]
        values = dict(q=q, kv=kv, kv_other=kv_other, lse=lse, hat1=hat1, inv1=inv1, slope=slope, att_t=att_t)
        if fast:
            rows_keep, rows_send, cols_keep, cols_send = results[5:9]
            cols = cols_keep, swap(cols_send)
            values["halves"] = (rows_keep, swap(rows_send)), cols if last else [(v, "far") for v in cols]
        else:
            values["acts"], values["acts_other"] = results[5], swap(results[5])
        results = results[9 if fast else 6 :]
        if last:
            values["hat2"], values["inv2"], out0, out1 = results
        else:
            values["hat2"], values["inv2"], stream, low, q, kv, meta = results
        kept.append(values)

    seqs = place.seq_width
    block_shape = ((rows, FF // seqs), BF16)
    swap_all = lambda values: [swap(v) for v in values]

    def turn(layer):
        k = kept[layer]
        operands = [scal, (meta, "v"), (cot[0], "v"), (cot[1], "v"), (k["hat2"], "v"), (k["inv2"], "v")]
        operands += [tables["gains"], (k["slope"], "v"), weight["down"]]
        outputs = [block_shape] * seqs + [((1, FF), F32), (wide, BF16), (wide, F32), ((8, D), F32)]
        scratch = [pltpu.VMEM((seqs, FF // seqs, D), BF16), pltpu.VMEM(wide, F32), dma((seqs,))]
        results = chain.call(functools.partial(turn_kernel, layer), operands, outputs, scratch, 16)
        return results[:seqs], results[seqs:]

    def attention_back(layer, grad_before, grad_two):
        k = kept[layer]
        scratch = [pltpu.VMEM((D, FF), BF16), pltpu.VMEM((D, D), BF16), pltpu.VMEM(wide, BF16)]
        scratch += [pltpu.VMEM((D, rows), BF16), pltpu.VMEM((D, rows), BF16), pltpu.VMEM((D, 2 * rows), BF16)]
        scratch += [pltpu.VMEM((D, rows), BF16), pltpu.VMEM((rows, 2 * D), BF16), dma((2,))]
        operands = [(v, "v") for v in grad_before] + [scal, (meta, "v"), (grad_two, "v")]
        far = "v" if layer == LAYERS - 1 else "far"
        operands += [(k["hat1"], far), (k["inv1"], "v")]
        operands += [(k[name], far) for name in ("q", "kv", "kv_other")] + [(k["lse"], "v"), (k["att_t"], far)]
        operands += [weight["up"], weight["out"], tables["gains"]]
        outputs = [(wide, F32), (wide, BF16), (wide, BF16), ((rows, 2 * D), F32), ((8, D), F32)]
        outputs += [((rows, 2 * D // SENDS), BF16)] * SENDS
        body = functools.partial(attention_back_kernel, layer, seqs)
        return chain.call(body, operands, outputs, scratch, 20)

    def input_back(layer, grad_one, branch, grad_q, dkv, small, *sends, after=()):
        operands = [(swap(v), "v") for v in sends]
        operands += [scal, (grad_q, "v"), (dkv, "v"), (grad_one, "v"), (branch, "v"), weight["qkv"]]
        outputs = [((rows, 4 * D), BF16, "far")]
        scratch = [pltpu.VMEM((D, 3 * D), BF16), pltpu.VMEM((rows, 3 * D), BF16)]
        if layer > 0:
            before = kept[layer - 1]
            operands += [(before["hat2"], "far"), (before["inv2"], "v"), tables["gains"]]
            operands += [(before["slope"], "far"), weight["down"]]
            outputs += [block_shape] * seqs + [((8, D), F32), (wide, BF16), (wide, F32), ((8, D), F32), ((1, FF), F32)]
            scratch += [pltpu.VMEM((seqs, FF // seqs, D), BF16), dma((1,)), dma((seqs,))]
        else:
            outputs += [((8, D), F32), part_shape, part_shape]
            scratch += [dma((1,))]
        body = functools.partial(input_back_kernel, layer, seqs)
        return chain.call(body, operands, outputs, scratch, 20, after)

    z_wide, z_thin = 3 * D // place.seq_width, D // place.seq_width
    plain = [None] * LAYERS

    def plain_sums(layer, mixed, mixed_other, grad_before, before_other, right, right_other):
        k = kept[layer]
        pick = lambda name, at, width: k[name][:, at : at + width]
        split = lambda v: v.reshape(rows, place.seq_width, z_wide + z_thin)
        results = []
        for at, parts in ((LOW, slice(0, z_wide)), (ATT, slice(z_wide, None))):
            rhs = [split(v)[:, :, parts].reshape(rows, -1) for v in (right, right_other)]
            results.append(place.scatter_plain(pick("acts", at, D), pick("acts_other", at, D), *rhs))
        results.append(
            place.scatter_plain(
                pick("acts", NORMED, D),
                pick("acts_other", NORMED, D),
                jnp.concatenate(grad_before, 1),
                jnp.concatenate(before_other, 1),
            )
        )
        results.append(
            place.scatter_plain(pick("acts", ACTIVE, FF), pick("acts_other", ACTIVE, FF), mixed, mixed_other)
        )
        return results

    k1, k0 = kept[1], kept[0]
    halves1, halves0 = (k["halves"] if fast else None for k in (k1, k0))
    before1, (small_up1, mixed1, grad_two, small_two) = turn(1)
    mixed1_other = swap(mixed1)
    before1_other = swap_all(before1)
    if fast:
        d1, u1 = bundles.make(
            bundles.down("x", halves1, mixed1, mixed1_other),
            bundles.up("y", halves1, before1, before1_other),
        )
    back = attention_back(1, before1, grad_two)
    small_one1 = back[4]
    hidden = place.from_chip(out0, out1)
    chain.early[HIDDEN_AT] = [hidden]
    right1, *results = input_back(1, *back)
    before0, (small_in1, mixed0, grad_two, small_two0, small_up0) = results[:seqs], results[seqs:]
    mixed0_other = swap(mixed0)
    before0_other = swap_all(before0)
    right1_other = swap(right1)
    if fast:
        d1, u1 = bundles.add(([d1], "y"), ([u1], "x"))
        d0, u0 = bundles.make(
            bundles.down("x", halves0, mixed0, mixed0_other),
            bundles.up("y", halves0, before0, before0_other),
        )
    else:
        plain[1] = plain_sums(1, mixed1, mixed1_other, before1, before1_other, right1, right1_other)
    back = attention_back(0, before0, grad_two)
    small_one0 = back[4]
    if fast:
        du1 = bundles.add(([d1, u1], "z0", "g"))
        oq1a, oq1b = bundles.make(bundles.oq(("x", "y"), halves1, right1, right1_other))
    right0, small_in0, last0, last1 = input_back(0, *back)
    right0_other = swap(right0)
    grad_tokens = place.from_chip(last0, last1)
    chain.early.setdefault(GRAD_AT, []).append(grad_tokens)
    smalls = []
    for group in ((small_in0, small_one0, small_two0, small_up0), (small_in1, small_one1, small_two, small_up1)):
        smalls += [(v, "v") for v in group]
    (table,) = chain.call(pack_kernel, smalls, [((LAYERS * 12, D), F32)], [])
    if fast:
        du1 = bundles.add(([du1], "z1"))
        d0, u0, table = bundles.add(([d0], "y"), ([u0], "x", (table, swap(table))))
        u0_got = u0.got
        oq0a, oq0b = bundles.make(bundles.oq(("x", "y"), halves0, right0, right0_other))
        oq1a, oq1b = bundles.add(([oq1a], "y"), ([oq1b], "x"))
        du0, du1 = bundles.add(([d0, u0], "z0", "g"), bundles.finish(du1))
        oq0a, table, oq0b = bundles.add(([oq0a], "y", (table, u0_got)), ([oq0b], "x"))
        oq1 = bundles.add(([oq1a, oq1b], "z0", "z1"))
        du0 = bundles.add(([du0], "z1"))
        oq0, table, oq1 = bundles.add(([oq0a, oq0b], "z0", "z1", (table, oq0a.got)), ([oq1], "z1"))
        oq0, table = bundles.add(([oq0], "z1", (table, oq0.got)))
        places = (((1, 2), 0), ((1, 2), 1), ((3, 4), 0)), (((0,), 0), ((0,), 1), ((5, 6), 0))
        pairs = [(v, "v") for v in (du1, du0.keep, du0.got, oq0.keep, oq0.got, oq1.keep, oq1.got, table)]
        block = bundles.block
        shapes = [(block, z_wide), (block, z_thin), (block, bundles.cols), (z_thin, FF // place.dp_width)]
        pair = ((LAYERS, 2, D), F32)
        *stacked, bias_qv, bias_proj, bias_up, gains, shifts = chain.call(
            functools.partial(last_kernel, (place.seq_width, block, places, 4)),
            pairs,
            [((LAYERS,) + shape, F32) for shape in shapes] + [pair, pair, ((LAYERS, FF), F32), pair, pair],
            [],
        )
        stacked[3] = stacked[3].transpose(0, 2, 1)
    else:
        plain[0] = plain_sums(0, mixed0, mixed0_other, before0, before0_other, right0, right0_other)
        total = place.all_sum(table).reshape(LAYERS, 12, D)
        bias_qv, bias_proj, gains, shifts = (total[:, 2 * k : 2 * k + 2] for k in range(4))
        bias_up = total[:, 8:].reshape(LAYERS, FF)
        stacked = [jnp.stack([plain[layer][k] for layer in range(LAYERS)]) for k in range(4)]
    return (hidden, grad_tokens, *stacked, bias_qv, bias_proj, bias_up, gains, shifts)


def solution(mesh):
    rows = P("dp", "seq", None)
    blocks = P(None, "dp", "seq")
    return jax.shard_map(
        local,
        mesh=mesh,
        in_specs=(rows, rows, P("dp"), P("dp")) + (P(),) * 9,
        out_specs=(rows, rows) + (blocks,) * 4 + (P(),) * 5,
        check_vma=False,
    )
```
